256 devices in a mesh: gx: 8 (over z), gy: 4 (over x_hi, core), gz: 8 (over x_lo, y).
Axes of the slice: x: 4 (x_hi: 2, x_lo: 2; x = x_hi * 2 + x_lo), y: 4, z: 8, core: 2. Of those that a mesh axis runs over, the one named last changes fastest.
Arguments:
- fine_state: float32 [27, 64, 64, 1024], P(None, 'gx', 'gy', 'gz'), may hold values from 0.6 to 1.4
- coarse_state: float32 [27, 64, 64, 1024], P(None, 'gx', 'gy', 'gz'), may hold values from 0.6 to 1.4
- fine_rates: float32 [27], replicated, may hold values from 0.7 to 1.8
- coarse_rates: float32 [27], replicated, may hold values from 0.7 to 1.8
- solid_flags: int32 [64, 64, 1024], P('gx', 'gy', 'gz'), may hold values 0 or 1
- down_source: int32 [8, 4, 8, 64, 2], P('gx', 'gy', 'gz'), may hold values from -1 to 127, as said below
- down_target: int32 [8, 4, 8, 64, 2], P('gx', 'gy', 'gz'), may hold values from -1 to 127, as said below
- up_source: int32 [8, 4, 8, 64, 2], P('gx', 'gy', 'gz'), may hold values from -1 to 127, as said below
- up_target: int32 [8, 4, 8, 64, 2], P('gx', 'gy', 'gz'), may hold values from -1 to 127, as said below
Outputs:
- fine_next: float32 [27, 64, 64, 1024], P(None, 'gx', 'gy', 'gz')
- coarse_next: float32 [27, 64, 64, 1024], P(None, 'gx', 'gy', 'gz')
The draws below stay inside these ranges and needn't reach their ends.
Inputs may be any that keep to these rules, and one draw needn't show every extreme that they name: `down_source`: entry [x, y, z, r, j] is slot j of the coarse tiles that device (x, y, z) sends to the r-th device of its gx+gz group (gx index times the size of gz plus gz index, same gy); -1 marks an empty slot. Live slots of one pair come first; a device fills all 2 slots to itself. `down_target`: entry [x, y, z, r, j]: the fine tile of device (x, y, z) that receives slot j of what the r-th device of its gx+gz group sends it, -1 exactly where that slot is empty in down_source; the live entries of one device are distinct. `up_source`: as down_source, with fine tiles of the sending device. `up_target`: as down_target, with coarse tiles of the receiving device; live entries of one device distinct.
All inputs are finite; a program needn't handle non-finite values. No bound on the sum of `solid_flags` on one device may be relied on, other than what follows from the above.
Results may differ from the reference program's by a relative error of at most 0.0001.
Values sent between devices are 32-bit elements; how exact they have to be, the bound alone decides.
No kernel may reach another device: no remote copies, remote signals or barrier semaphores. Data moves between devices by JAX's collectives and lax.ppermute only.
A program may use at most 128 MiB of HBM per device.

```python
import jax
import jax.numpy as jnp
import numpy as np
from jax import lax

CX = 8
CY = 16
KX = 8
KY = 16
CAP = 2
NX = 64
NY = 64
NZ = 1024
MX = 64
MY = 64
N_GX = 8
N_GY = 4
N_GZ = 8


def routing(key, source_tiles, target_tiles):
    peer_count = N_GX * N_GZ
    count_key, tile_key, order_key = jax.random.split(key, 3)
    axis_x = jnp.arange(N_GX, dtype=jnp.int32).reshape(-1, 1, 1, 1)
    axis_y = jnp.arange(N_GY, dtype=jnp.int32).reshape(1, -1, 1, 1)
    axis_z = jnp.arange(N_GZ, dtype=jnp.int32).reshape(1, 1, -1, 1)
    peer_index = jnp.arange(peer_count, dtype=jnp.int32).reshape(1, 1, 1, -1)
    counts = jax.random.randint(count_key, (N_GX, N_GY, N_GZ, peer_count), 0, CAP + 1)
    counts = jnp.where(axis_x * N_GZ + axis_z == peer_index, CAP, counts)
    slot_index = jnp.arange(CAP, dtype=jnp.int32).reshape(1, 1, 1, 1, -1)
    filled = slot_index < counts[..., None]
    tile_ids = jax.random.randint(tile_key, filled.shape, 0, source_tiles)
    source = jnp.where(filled, tile_ids, -1)
    receiver_x = axis_x[..., None]
    receiver_y = axis_y[..., None]
    receiver_z = axis_z[..., None]
    sender = peer_index[..., None]
    received = filled[sender // N_GZ, receiver_y, sender % N_GZ, receiver_x * N_GZ + receiver_z, slot_index]

    def shuffled(subkey):
        return jax.random.permutation(subkey, target_tiles)
    orders = jax.vmap(shuffled)(jax.random.split(order_key, N_GX * N_GY * N_GZ))
    chosen = orders[:, :peer_count * CAP].reshape(N_GX, N_GY, N_GZ, peer_count, CAP).astype(jnp.int32)
    target = jnp.where(received, chosen, -1)
    return (source.astype(jnp.int32), target)


def draw_down_source(key, part):
    return routing(jax.random.fold_in(key, 11), KX * KY, CX * CY)[0]


def draw_down_target(key, part):
    return routing(jax.random.fold_in(key, 11), KX * KY, CX * CY)[1]


def draw_up_source(key, part):
    return routing(jax.random.fold_in(key, 12), CX * CY, KX * KY)[0]


def draw_up_target(key, part):
    return routing(jax.random.fold_in(key, 12), CX * CY, KX * KY)[1]


def set_ends(drawn, rng, smallest, top_value):
    longest = drawn.shape.index(max(drawn.shape))
    spots = []
    for shift in (0, 1):
        where = [jax.random.randint(jax.random.fold_in(rng, axis), (), 0, length) for axis, length in enumerate(drawn.shape)]
        where[longest] = (where[longest] + shift) % drawn.shape[longest]
        spots.append(tuple(where))
    return drawn.at[spots[0]].set(smallest).at[spots[1]].set(top_value)


def steps_of(stream_key, dims, shards, least, high):
    level = 1.0
    for position, blocks in shards:
        steps = jax.random.uniform(jax.random.fold_in(jax.random.fold_in(stream_key, 6), position), (blocks,), jnp.float32, least / len(shards), high / len(shards))
        level = level * jnp.repeat(jnp.exp(steps), dims[position] // blocks).reshape((-1,) + (1,) * (len(dims) - 1 - position))
    return level


def setup_inputs(seed: int = 0) -> dict:
    key_list = jax.random.split(jax.random.key(seed), 10)
    return {
        "fine_state": jnp.clip(0.6 + 0.79999995 * jax.random.uniform(key_list[0], (27, NX, NY, NZ), jnp.float32) ** steps_of(key_list[0], (27, NX, NY, NZ), ((1, 8), (2, 4), (3, 8)), -0.2, 0.2), 0.6, 1.4),
        "coarse_state": jnp.clip(0.6 + 0.79999995 * jax.random.uniform(key_list[1], (27, MX, MY, NZ), jnp.float32) ** steps_of(key_list[1], (27, MX, MY, NZ), ((1, 8), (2, 4), (3, 8)), -0.2, 0.2), 0.6, 1.4),
        "fine_rates": jnp.clip(jax.random.uniform(key_list[2], (27,), jnp.float32, 0.7, 1.8), 0.7, 1.8),
        "coarse_rates": jnp.clip(jax.random.uniform(key_list[3], (27,), jnp.float32, 0.7, 1.8), 0.7, 1.8),
        "solid_flags": set_ends((jax.random.randint(key_list[4], (NX, NY, NZ), 0, 8) < 1).astype(jnp.int32), jax.random.fold_in(key_list[4], 1), 0, 1),
        "down_source": draw_down_source(jax.random.fold_in(key_list[9], 71), 0),
        "down_target": draw_down_target(jax.random.fold_in(key_list[9], 71), 0),
        "up_source": draw_up_source(jax.random.fold_in(key_list[9], 71), 0),
        "up_target": draw_up_target(jax.random.fold_in(key_list[9], 71), 0),
    }


LEVEL_VALUES = np.array([-1.0, 0.0, 1.0])
VELOCITY = np.stack(np.meshgrid(LEVEL_VALUES, LEVEL_VALUES, LEVEL_VALUES, indexing="ij"), -1).reshape(27, 3)
SQUARED = np.sum(VELOCITY * VELOCITY, axis=1).astype(np.int64)
WEIGHTS = np.array([8.0 / 27.0, 2.0 / 27.0, 1.0 / 54.0, 1.0 / 216.0])[SQUARED]
VANDER = np.array([[1.0, 1.0, 1.0], [-1.0, 0.0, 1.0], [1.0, 0.0, 1.0]])
VANDER_INVERSE = np.array([[0.0, -0.5, 0.5], [1.0, 0.0, -1.0], [0.0, 0.5, 0.5]])
MOMENTS = np.kron(np.kron(VANDER, VANDER), VANDER)
INVERSE = np.kron(np.kron(VANDER_INVERSE, VANDER_INVERSE), VANDER_INVERSE)
SHIFTS = [[step_x, step_y, step_z] for step_x in (-1, 0, 1) for step_y in (-1, 0, 1) for step_z in (-1, 0, 1)]


def relax(populations, relax_rates):
    highest = lax.Precision.HIGHEST
    weights = jnp.asarray(WEIGHTS, jnp.float32)
    velocity = jnp.asarray(VELOCITY, jnp.float32)
    moments = jnp.asarray(MOMENTS, jnp.float32)
    inverse = jnp.asarray(INVERSE, jnp.float32)
    density = jnp.einsum("i,ixyz->xyz", weights, populations, precision=highest)
    momentum = jnp.einsum("ik,ixyz->kxyz", velocity * weights[:, None], populations, precision=highest)
    projected = jnp.einsum("ik,kxyz->ixyz", velocity, momentum, precision=highest)
    speed_square = jnp.sum(momentum * momentum, axis=0)
    equilibrium = density[None] + 3.0 * projected + 4.5 * projected * projected - 1.5 * speed_square[None]
    deviation = weights[:, None, None, None] * (equilibrium - populations)
    moment_values = jnp.einsum("ji,ixyz->jxyz", moments, deviation, precision=highest)
    returned = jnp.einsum("ij,jxyz->ixyz", inverse, relax_rates[:, None, None, None] * moment_values, precision=highest)
    return populations + returned / weights[:, None, None, None]


def stream(lattice):
    return jnp.stack([jnp.roll(lattice[direction], SHIFTS[direction], axis=(0, 1, 2)) for direction in range(27)])


def to_tiles(lattice, size_x, size_y):
    length = lattice.shape[3] // N_GZ
    blocks = lattice.reshape(27, N_GX, size_x, N_GY, size_y, N_GZ, length)
    blocks = blocks.transpose(0, 1, 3, 5, 2, 4, 6)
    return blocks.reshape(27, N_GX * N_GY * N_GZ * size_x * size_y, length)


def from_tiles(tile_table, size_x, size_y):
    length = tile_table.shape[2]
    blocks = tile_table.reshape(27, N_GX, N_GY, N_GZ, size_x, size_y, length)
    blocks = blocks.transpose(0, 1, 4, 2, 5, 3, 6)
    return blocks.reshape(27, N_GX * size_x, N_GY * size_y, N_GZ * length)


def route(source_table, target_table, source_tiles, target_tiles):
    axis_x = jnp.arange(N_GX, dtype=jnp.int32).reshape(-1, 1, 1, 1, 1)
    axis_y = jnp.arange(N_GY, dtype=jnp.int32).reshape(1, -1, 1, 1, 1)
    axis_z = jnp.arange(N_GZ, dtype=jnp.int32).reshape(1, 1, -1, 1, 1)
    sender = jnp.arange(N_GX * N_GZ, dtype=jnp.int32).reshape(1, 1, 1, -1, 1)
    slot_index = jnp.arange(CAP, dtype=jnp.int32).reshape(1, 1, 1, 1, -1)
    sender_x = sender // N_GZ
    sender_z = sender % N_GZ
    receiver_peer = axis_x * N_GZ + axis_z
    source_tile = source_table[sender_x, axis_y, sender_z, receiver_peer, slot_index]
    source_device = (sender_x * N_GY + axis_y) * N_GZ + sender_z
    target_device = (axis_x * N_GY + axis_y) * N_GZ + axis_z
    source_rows = source_device * source_tiles + jnp.maximum(source_tile, 0)
    total = N_GX * N_GY * N_GZ * target_tiles
    target_rows = jnp.where(target_table < 0, total, target_device * target_tiles + target_table)
    target_rows = jnp.broadcast_to(target_rows, source_rows.shape)
    return source_rows.reshape(-1).astype(jnp.int32), target_rows.reshape(-1).astype(jnp.int32)


def install(tile_table, offset, values, targets):
    section = tile_table[offset:offset + 9].at[:, targets, :].set(values, mode="drop")
    return tile_table.at[offset:offset + 9].set(section)


def reference(fine_state, coarse_state, fine_rates, coarse_rates, solid_flags, down_source, down_target, up_source, up_target):
    down_from, down_to = route(down_source, down_target, KX * KY, CX * CY)
    up_from, up_to = route(up_source, up_target, CX * CY, KX * KY)
    coarse_new = stream(relax(coarse_state, coarse_rates))
    interface_old = to_tiles(coarse_state, KX, KY)[18:27][:, down_from, :]
    new_tiles = to_tiles(coarse_new, KX, KY)[18:27][:, down_from, :]
    interface_mean = 0.5 * (interface_old + new_tiles)
    lattice = fine_state
    for interface in (interface_old, interface_mean):
        tile_table = install(to_tiles(lattice, CX, CY), 18, interface, down_to)
        lattice = from_tiles(tile_table, CX, CY)
        collided = jnp.where(solid_flags[None] == 1, lattice[::-1], relax(lattice, fine_rates))
        lattice = stream(collided)
    fine_tiles = to_tiles(lattice, CX, CY)[0:9][:, up_from, :]
    coarse_table = install(to_tiles(coarse_new, KX, KY), 0, fine_tiles, up_to)
    return lattice, from_tiles(coarse_table, KX, KY)
```

```python
import jax
import jax.numpy as jnp
from jax import lax
from jax.experimental import pallas as pl
from jax.experimental.pallas import tpu as pltpu
from jax.sharding import PartitionSpec as P

SLABS = 8
ROWS = 16
LANES = 128
TILES = SLABS * ROWS
CHUNK = 18
PEERS = 64
VMEM_BYTES = 24 * 1024 * 1024


def load8(ref, i, u):
    return ref[pl.ds(pl.multiple_of(i * TILES + u * 8, 8), 8), :]


def forward(values):
    for step in (9, 3, 1):
        out = list(values)
        for i in range(27):
            if (i // step) % 3 == 0:
                low, mid, high = values[i], values[i + step], values[i + 2 * step]
                even = high + low
                out[i] = even + 4.0 * mid
                out[i + step] = high - low
                out[i + 2 * step] = even
        values = out
    return values


def backward(values):
    for step in (9, 3, 1):
        out = list(values)
        for i in range(27):
            if (i // step) % 3 == 0:
                zero, one, two = values[i], values[i + step], values[i + 2 * step]
                out[i] = two - one
                out[i + step] = zero - two
                out[i + 2 * step] = two + one
        values = out
    return values


def equilibrium(moments):
    density = moments[0]
    momentum = (moments[9], moments[3], moments[1])
    squares = [part * part * (1.0 / 72.0) for part in momentum]
    scale = (1.0, 1.0 / 3.0, 1.0 / 9.0, 1.0 / 27.0)
    result = []
    for k in range(27):
        powers = (k // 9, (k // 3) % 3, k % 3)
        ones = [axis for axis in range(3) if powers[axis] == 1]
        twos = [axis for axis in range(3) if powers[axis] == 2]
        if len(ones) == 0:
            value = density
            for axis in twos:
                value = value + squares[axis]
        elif len(ones) == 1:
            value = momentum[ones[0]]
        elif len(ones) == 2:
            value = momentum[ones[0]] * momentum[ones[1]] * (1.0 / 216.0)
        else:
            value = jnp.zeros_like(density)
        if twos:
            value = value * scale[len(twos)]
        result.append(value)
    return result


def relax(values, rates_ref):
    moments = forward(values)
    target = equilibrium(moments)
    change = backward([(rates_ref[k] * 0.125) * (target[k] - moments[k]) for k in range(27)])
    result = []
    for i in range(27):
        rests = sum(1 for part in (i // 9, (i // 3) % 3, i % 3) if part == 1)
        moved = change[i] if rests == 0 else change[i] * (0.5**rests)
        result.append(values[i] + moved)
    return result


def lane_index(rows):
    return lax.broadcasted_iota(jnp.int32, (rows, LANES), 1)


def turn(value, amount):
    amount = amount % LANES if isinstance(amount, int) else amount
    if isinstance(amount, int) and amount == 0:
        return value
    return pltpu.roll(value, amount, 1)


def collide(source, flags_ref, rates_ref, out_ref, zp_ref, zm_ref, yp_ref, ym_ref, xp_ref, xm_ref):
    lanes = lane_index(8)

    def step(u, carry):
        values = [load8(source, i, u) for i in range(27)]
        result = relax(values, rates_ref)
        if flags_ref is not None:
            solid = flags_ref[pl.ds(pl.multiple_of(u * 8, 8), 8), :] == 1
            result = [jnp.where(solid, values[26 - i], result[i]) for i in range(27)]
        for i in range(27):
            out_ref[pl.ds(pl.multiple_of(i * TILES + u * 8, 8), 8), :] = result[i]
        slab = u // 2
        half = u % 2
        here = jnp.logical_and(lanes >= slab * 16, lanes < slab * 16 + 16)
        for ref, c, edge in ((zp_ref, 2, LANES - 1), (zm_ref, 0, 0)):
            packed = None
            for j in range(9):
                column = turn(result[3 * j + c], j - edge)
                packed = column if packed is None else jnp.where(lanes == j, column, packed)
            packed = turn(packed, slab * 16)
            rows = pl.ds(pl.multiple_of(half * 8, 8), 8)
            ref[rows, :] = jnp.where(here, packed, ref[rows, :])
        return carry

    zp_ref[...] = jnp.zeros_like(zp_ref)
    zm_ref[...] = jnp.zeros_like(zm_ref)
    lax.fori_loop(0, 2 * SLABS, step, 0)
    for ref, b, q in ((yp_ref, 2, ROWS - 1), (ym_ref, 0, 0)):
        for a in range(3):
            for c in range(3):
                i = 9 * a + 3 * b + c
                rows = out_ref[pl.ds(i * TILES + q, 8, stride=ROWS), :]
                ref[pl.ds((3 * a + c) * 8, 8), :] = rows
                j = 3 * a + b
                if c == 2:
                    zp_ref[16:24, :] = jnp.where(lanes == j, turn(rows, j + 1), zp_ref[16:24, :])
                if c == 0:
                    zm_ref[16:24, :] = jnp.where(lanes == j, turn(rows, j), zm_ref[16:24, :])
    for j in range(9):
        xp_ref[pl.ds(j * ROWS, ROWS), :] = out_ref[pl.ds((18 + j) * TILES + 7 * ROWS, ROWS), :]
        xm_ref[pl.ds(j * ROWS, ROWS), :] = out_ref[pl.ds(j * TILES, ROWS), :]


def pack(source, first, table_ref, out_ref, mix):
    def step(r, carry):
        for j in range(2):
            tile = jnp.maximum(table_ref[j, r], 0)
            most = source[pl.ds(first * TILES + tile, 8, stride=TILES), :]
            last = source[pl.ds((first + 8) * TILES + tile, 1), :]
            rows = pl.ds(r * CHUNK + j, 8, stride=2)
            row = pl.ds(r * CHUNK + 16 + j, 1)
            if mix is not None:
                most = 0.5 * (mix[rows, :] + most)
                last = 0.5 * (mix[row, :] + last)
            out_ref[rows, :] = most
            out_ref[row, :] = last
        return carry

    lax.fori_loop(0, PEERS, step, 0, unroll=4)


def install(target, first, table_ref, received_ref):
    def step(r, carry):
        for j in range(2):
            tile = table_ref[j, r]

            @pl.when(tile >= 0)
            def _():
                most = received_ref[pl.ds(r * CHUNK + j, 8, stride=2), :]
                last = received_ref[pl.ds(r * CHUNK + 16 + j, 1), :]
                target[pl.ds(first * TILES + tile, 8, stride=TILES), :] = most
                target[pl.ds((first + 8) * TILES + tile, 1), :] = last

        return carry

    lax.fori_loop(0, PEERS, step, 0, unroll=4)


def move_z(value, c, low_ghost, high_ghost, lanes):
    if c == 2:
        return jnp.where(lanes == 0, low_ghost, turn(value, 1))
    if c == 0:
        return jnp.where(lanes == LANES - 1, high_ghost, turn(value, LANES - 1))
    return value


def move_y(value, b, ghost, rows):
    if b == 2:
        return jnp.where(rows == 0, ghost, pltpu.roll(value, 1, 0))
    if b == 0:
        return jnp.where(rows == ROWS - 1, ghost, pltpu.roll(value, ROWS - 1, 0))
    return value


def face_y_kernel(yp_ref, ym_ref, zp_ref, zm_ref, op_ref, om_ref):
    lanes = lane_index(8)
    zp, zm = zp_ref[16:24, :], zm_ref[16:24, :]
    for ref, out, b in ((yp_ref, op_ref, 2), (ym_ref, om_ref, 0)):
        for a in range(3):
            j = 3 * a + b
            for c in range(3):
                place = pl.ds((3 * a + c) * 8, 8)
                low = turn(zp, -j) if c == 2 else None
                high = turn(zm, LANES - 1 - j) if c == 0 else None
                out[place, :] = move_z(ref[place, :], c, low, high, lanes)


def face_x_kernel(xp_ref, xm_ref, zp_ref, zm_ref, yp_ref, ym_ref, op_ref, om_ref):
    lanes = lane_index(ROWS)
    rows = lax.broadcasted_iota(jnp.int32, (ROWS, LANES), 0)
    zp, zm = zp_ref[0:16, :], zm_ref[0:16, :]
    for ref, out, a, p in ((xp_ref, op_ref, 2, SLABS - 1), (xm_ref, om_ref, 0, 0)):
        for b in range(3):
            j = 3 * a + b
            for c in range(3):
                place = pl.ds((3 * b + c) * ROWS, ROWS)
                low = turn(zp, -(16 * p + j)) if c == 2 else None
                high = turn(zm, LANES - 1 - 16 * p - j) if c == 0 else None
                value = move_z(ref[place, :], c, low, high, lanes)
                spot = pl.ds((3 * a + c) * 8 + p, 1)
                ghost = yp_ref[spot, :] if b == 2 else ym_ref[spot, :]
                out[place, :] = move_y(value, b, ghost, rows)


def stream(source, ghosts, out_ref):
    zp_ref, zm_ref, yp_ref, ym_ref, xp_ref, xm_ref = ghosts
    lanes = lane_index(ROWS)
    rows = lax.broadcasted_iota(jnp.int32, (ROWS, LANES), 0)

    def step(p, carry):
        for a in range(3):
            origin = p if a == 1 else (jnp.maximum(p - 1, 0) if a == 2 else jnp.minimum(p + 1, SLABS - 1))
            back = lax.rem(LANES - 16 * origin, LANES)
            zp = turn(zp_ref[0:16, :], back)
            zm = turn(zm_ref[0:16, :], back)
            for b in range(3):
                j = 3 * a + b
                for c in range(3):
                    i = 9 * a + 3 * b + c
                    value = source[pl.ds(pl.multiple_of(i * TILES + origin * ROWS, ROWS), ROWS), :]
                    low = turn(zp, -j) if c == 2 else None
                    high = turn(zm, LANES - 1 - j) if c == 0 else None
                    value = move_z(value, c, low, high, lanes)
                    spot = pl.ds((3 * a + c) * 8 + origin, 1)
                    ghost = yp_ref[spot, :] if b == 2 else ym_ref[spot, :]
                    value = move_y(value, b, ghost, rows)
                    place = pl.ds((3 * b + c) * ROWS, ROWS)
                    if a == 2:
                        value = jnp.where(p == 0, xp_ref[place, :], value)
                    if a == 0:
                        value = jnp.where(p == SLABS - 1, xm_ref[place, :], value)
                    out_ref[pl.ds(pl.multiple_of(i * TILES + p * ROWS, ROWS), ROWS), :] = value
        return carry

    lax.fori_loop(0, SLABS, step, 0)


def pack_kernel(state_ref, table_ref, out_ref):
    pack(state_ref, 18, table_ref, out_ref, None)


def coarse_kernel(state_ref, rates_ref, *outs):
    collide(state_ref, None, rates_ref, *outs)


def fine_first_kernel(state_ref, flags_ref, rates_ref, received_ref, table_ref, *refs):
    outs, lattice = refs[:7], refs[7]
    lattice[...] = state_ref[...]
    install(lattice, 18, table_ref, received_ref)
    collide(lattice, flags_ref, rates_ref, *outs)


def fine_second_kernel(state_ref, flags_ref, rates_ref, received_ref, table_ref, *refs):
    ghosts, outs, lattice = refs[:6], refs[6:13], refs[13]
    stream(state_ref, ghosts, lattice)
    install(lattice, 18, table_ref, received_ref)
    collide(lattice, flags_ref, rates_ref, *outs)


def coarse_stream_kernel(state_ref, old_ref, table_ref, *refs):
    ghosts, out_ref, sent_ref = refs[:6], refs[6], refs[7]
    stream(state_ref, ghosts, out_ref)
    pack(out_ref, 18, table_ref, sent_ref, old_ref)


def fine_stream_kernel(state_ref, table_ref, *refs):
    ghosts, out_ref, sent_ref = refs[:6], refs[6], refs[7]
    stream(state_ref, ghosts, out_ref)
    pack(out_ref, 0, table_ref, sent_ref, None)


def coarse_install_kernel(state_ref, received_ref, table_ref, out_ref):
    out_ref[...] = state_ref[...]
    install(out_ref, 0, table_ref, received_ref)


STATE = (27 * TILES, LANES)
MESSAGE = (PEERS * CHUNK, LANES)
Z_FACE = (24, LANES)
Y_FACE = (9 * 8, LANES)
X_FACE = (9 * ROWS, LANES)
COLLIDED = (STATE, Z_FACE, Z_FACE, Y_FACE, Y_FACE, X_FACE, X_FACE)


def run(kernel, name, spaces, shapes, *operands, scratch=(), microseconds=1.0):
    spots = {"s": pltpu.SMEM, "v": pltpu.VMEM}
    return pl.pallas_call(
        kernel,
        name=name,
        out_shape=tuple(jax.ShapeDtypeStruct(shape, jnp.float32) for shape in shapes),
        in_specs=[pl.BlockSpec(memory_space=spots[space]) for space in spaces],
        out_specs=tuple(pl.BlockSpec(memory_space=pltpu.VMEM) for _ in shapes),
        scratch_shapes=[pltpu.VMEM(shape, jnp.float32) for shape in scratch],
        compiler_params=pltpu.CompilerParams(vmem_limit_bytes=VMEM_BYTES),
        cost_estimate=pl.CostEstimate(
            flops=0, bytes_accessed=int(microseconds * 3.0e6), transcendentals=0
        ),
    )(*operands)


def swap(plus, minus, axis):
    count = lax.axis_size(axis)
    up = [(i, (i + 1) % count) for i in range(count)]
    down = [(i, (i - 1) % count) for i in range(count)]
    return lax.ppermute(plus, axis, up), lax.ppermute(minus, axis, down)


def halo(parts):
    zp, zm, yp, ym, xp, xm = parts
    zp, zm = swap(zp, zm, "gz")
    yp, ym = run(face_y_kernel, "face_y", "vvvv", (Y_FACE, Y_FACE), yp, ym, zp, zm)
    yp, ym = swap(yp, ym, "gy")
    xp, xm = run(face_x_kernel, "face_x", "vvvvvv", (X_FACE, X_FACE), xp, xm, zp, zm, yp, ym)
    xp, xm = swap(xp, xm, "gx")
    return zp, zm, yp, ym, xp, xm


def routed(message):
    chunks = message.reshape(PEERS, 9, 2, LANES)
    received = lax.all_to_all(chunks, ("gx", "gz"), split_axis=0, concat_axis=0, tiled=True)
    return received.reshape(MESSAGE)


def body(fine, coarse, fine_rates, coarse_rates, flags, down_source, down_target, up_source, up_target):
    fine = fine.reshape(STATE)
    coarse = coarse.reshape(STATE)
    flags = flags.reshape(TILES, LANES)
    down_source, down_target, up_source, up_target = (
        table.reshape(-1, 2).T for table in (down_source, down_target, up_source, up_target)
    )
    (sent_old,) = run(pack_kernel, "pack_old", "vs", (MESSAGE,), coarse, down_source)
    old = routed(sent_old)
    collided, *faces = run(coarse_kernel, "coarse_collide", "vs", COLLIDED, coarse, coarse_rates)
    ghosts = halo(faces)
    coarse_new, sent_mean = run(
        coarse_stream_kernel, "coarse_stream", "vvsvvvvvv", (STATE, MESSAGE),
        collided, sent_old, down_source, *ghosts,
    )
    mean = routed(sent_mean)
    collided, *faces = run(
        fine_first_kernel, "fine_first", "vvsvs", COLLIDED,
        fine, flags, fine_rates, old, down_target, scratch=(STATE,),
    )
    ghosts = halo(faces)
    collided, *faces = run(
        fine_second_kernel, "fine_second", "vvsvsvvvvvv", COLLIDED,
        collided, flags, fine_rates, mean, down_target, *ghosts, scratch=(STATE,),
    )
    ghosts = halo(faces)
    fine_next, sent_up = run(
        fine_stream_kernel, "fine_stream", "vsvvvvvv", (STATE, MESSAGE), collided, up_source, *ghosts
    )
    up = routed(sent_up)
    (coarse_next,) = run(
        coarse_install_kernel, "coarse_install", "vvs", (STATE,), coarse_new, up, up_target
    )
    block = (27, SLABS, ROWS, LANES)
    return fine_next.reshape(block), coarse_next.reshape(block)


def solution(mesh):
    placed = (
        P(None, "gx", "gy", "gz"),
        P(None, "gx", "gy", "gz"),
        P(),
        P(),
        P("gx", "gy", "gz"),
        P("gx", "gy", "gz", None, None),
        P("gx", "gy", "gz", None, None),
        P("gx", "gy", "gz", None, None),
        P("gx", "gy", "gz", None, None),
    )
    return jax.shard_map(
        body,
        mesh=mesh,
        in_specs=placed,
        out_specs=(P(None, "gx", "gy", "gz"), P(None, "gx", "gy", "gz")),
        check_vma=False,
    )
```

```python
import jax
import jax.numpy as jnp
from jax import lax
from jax.experimental import pallas as pl
from jax.experimental.pallas import tpu as pltpu
from jax.sharding import PartitionSpec as P

SLABS = 8
ROWS = 16
LANES = 128
TILES = SLABS * ROWS
CHUNK = 18
PEERS = 64
VMEM_BYTES = 10 * 1024 * 1024
WIDE = 136


def load8(ref, i, u):
    return ref[pl.ds(pl.multiple_of(i * TILES + u * 8, 8), 8), :]


def forward(values):
    for step in (9, 3, 1):
        out = list(values)
        for i in range(27):
            if (i // step) % 3 == 0:
                low, mid, high = values[i], values[i + step], values[i + 2 * step]
                even = high + low
                out[i] = even + 4.0 * mid
                out[i + step] = high - low
                out[i + 2 * step] = even
        values = out
    return values


def backward(values):
    for step in (9, 3, 1):
        out = list(values)
        for i in range(27):
            if (i // step) % 3 == 0:
                zero, one, two = values[i], values[i + step], values[i + 2 * step]
                out[i] = two - one
                out[i + step] = zero - two
                out[i + 2 * step] = two + one
        values = out
    return values


def equilibrium(moments):
    density = moments[0]
    momentum = (moments[9], moments[3], moments[1])
    squares = [part * part * (1.0 / 72.0) for part in momentum]
    scale = (1.0, 1.0 / 3.0, 1.0 / 9.0, 1.0 / 27.0)
    result = []
    for k in range(27):
        powers = (k // 9, (k // 3) % 3, k % 3)
        ones = [axis for axis in range(3) if powers[axis] == 1]
        twos = [axis for axis in range(3) if powers[axis] == 2]
        if len(ones) == 0:
            value = density
            for axis in twos:
                value = value + squares[axis]
        elif len(ones) == 1:
            value = momentum[ones[0]]
        elif len(ones) == 2:
            value = momentum[ones[0]] * momentum[ones[1]] * (1.0 / 216.0)
        else:
            value = jnp.zeros_like(density)
        if twos:
            value = value * scale[len(twos)]
        result.append(value)
    return result


def relax(values, rates_ref):
    moments = forward(values)
    target = equilibrium(moments)
    change = backward([(rates_ref[k] * 0.125) * (target[k] - moments[k]) for k in range(27)])
    result = []
    for i in range(27):
        rests = sum(1 for part in (i // 9, (i // 3) % 3, i % 3) if part == 1)
        moved = change[i] if rests == 0 else change[i] * (0.5**rests)
        result.append(values[i] + moved)
    return result


def lane_index(rows):
    return lax.broadcasted_iota(jnp.int32, (rows, LANES), 1)


def turn(value, amount):
    amount = amount % LANES if isinstance(amount, int) else amount
    if isinstance(amount, int) and amount == 0:
        return value
    return pltpu.roll(value, amount, 1)


def collide(load, flags_ref, rates_ref, out_ref, zp_ref, zm_ref, yp_ref, ym_ref, xp_ref, xm_ref, ready=None):
    def step(u, carry):
        if ready is not None:
            ready(u)
        values = [load(i, u) for i in range(27)]
        result = relax(values, rates_ref)
        if flags_ref is not None:
            solid = flags_ref[pl.ds(pl.multiple_of(u * 8, 8), 8), :] == 1
            result = [jnp.where(solid, values[26 - i], result[i]) for i in range(27)]
        for i in range(27):
            out_ref[pl.ds(pl.multiple_of(i * TILES + u * 8, 8), 8), :] = result[i]
        return carry

    lax.fori_loop(0, 2 * SLABS, step, 0, unroll=2)
    lanes = lane_index(8)
    for ref, c, edge in ((zp_ref, 2, LANES - 1), (zm_ref, 0, 0)):
        for half in range(2):
            packed = None
            for p in range(SLABS):
                for j in range(9):
                    start = (3 * j + c) * TILES + p * ROWS + half * 8
                    column = turn(out_ref[start : start + 8, :], 16 * p + j - edge)
                    packed = column if packed is None else jnp.where(lanes == 16 * p + j, column, packed)
            ref[half * 8 : half * 8 + 8, :] = packed
    ends = [jnp.zeros((8, LANES), jnp.float32), None, jnp.zeros((8, LANES), jnp.float32)]
    for ref, b, q in ((yp_ref, 2, ROWS - 1), (ym_ref, 0, 0)):
        for a in range(3):
            for c in range(3):
                i = 9 * a + 3 * b + c
                rows = out_ref[pl.ds(i * TILES + q, 8, stride=ROWS), :]
                ref[pl.ds((3 * a + c) * 8, 8), :] = rows
                j = 3 * a + b
                if c != 1:
                    edge = LANES - 1 if c == 2 else 0
                    ends[c] = jnp.where(lanes == j, turn(rows, j - edge), ends[c])
    zp_ref[16:24, :] = ends[2]
    zm_ref[16:24, :] = ends[0]
    for j in range(9):
        xp_ref[pl.ds(j * ROWS, ROWS), :] = out_ref[pl.ds((18 + j) * TILES + 7 * ROWS, ROWS), :]
        xm_ref[pl.ds(j * ROWS, ROWS), :] = out_ref[pl.ds(j * TILES, ROWS), :]


def fill(tiles, state_ref, first, ghost_ref=None, slab=None):
    for k in range(9):
        tiles[pl.ds(k * WIDE, TILES), :] = state_ref[pl.ds((first + k) * TILES, TILES), :]
        if ghost_ref is not None:
            tiles[pl.ds(k * WIDE + slab * ROWS, ROWS), :] = ghost_ref[pl.ds(k * ROWS, ROWS), :]


def pack(tiles, table_ref, out_ref, mix):
    def step(r, carry):
        for j in range(2):
            tile = jnp.maximum(table_ref[j, r], 0)
            most = tiles[pl.ds(tile, 8, stride=WIDE), :]
            last = tiles[pl.ds(8 * WIDE + tile, 1), :]
            rows = pl.ds(r * CHUNK + j, 8, stride=2)
            row = pl.ds(r * CHUNK + 16 + j, 1)
            if mix is not None:
                most = 0.5 * (mix[rows, :] + most)
                last = 0.5 * (mix[row, :] + last)
            out_ref[rows, :] = most
            out_ref[row, :] = last
        return carry

    lax.fori_loop(0, PEERS, step, 0, unroll=4)


def install(tiles, table_ref, received_ref):
    def step(r, carry):
        moved = []
        for j in range(2):
            tile = table_ref[j, r]
            tile = jnp.where(tile < 0, TILES, tile)
            most = received_ref[pl.ds(r * CHUNK + j, 8, stride=2), :]
            last = received_ref[pl.ds(r * CHUNK + 16 + j, 1), :]
            moved.append((tile, most, last))
        for tile, most, last in moved:
            tiles[pl.ds(tile, 8, stride=WIDE), :] = most
            tiles[pl.ds(8 * WIDE + tile, 1), :] = last
        return carry

    lax.fori_loop(0, PEERS, step, 0, unroll=4)


def move_z(value, c, low_ghost, high_ghost, lanes):
    if c == 2:
        return jnp.where(lanes == 0, low_ghost, turn(value, 1))
    if c == 0:
        return jnp.where(lanes == LANES - 1, high_ghost, turn(value, LANES - 1))
    return value


def move_y(value, b, ghost, rows):
    if b == 2:
        return jnp.where(rows == 0, ghost, pltpu.roll(value, 1, 0))
    if b == 0:
        return jnp.where(rows == ROWS - 1, ghost, pltpu.roll(value, ROWS - 1, 0))
    return value


def face_y_kernel(yp_ref, ym_ref, zp_ref, zm_ref, op_ref, om_ref):
    lanes = lane_index(8)
    zp, zm = zp_ref[16:24, :], zm_ref[16:24, :]
    for ref, out, b in ((yp_ref, op_ref, 2), (ym_ref, om_ref, 0)):
        for a in range(3):
            j = 3 * a + b
            for c in range(3):
                place = pl.ds((3 * a + c) * 8, 8)
                low = turn(zp, -j) if c == 2 else None
                high = turn(zm, LANES - 1 - j) if c == 0 else None
                out[place, :] = move_z(ref[place, :], c, low, high, lanes)


def face_x_kernel(xp_ref, xm_ref, zp_ref, zm_ref, yp_ref, ym_ref, op_ref, om_ref):
    lanes = lane_index(ROWS)
    rows = lax.broadcasted_iota(jnp.int32, (ROWS, LANES), 0)
    zp, zm = zp_ref[0:16, :], zm_ref[0:16, :]
    for ref, out, a, p in ((xp_ref, op_ref, 2, SLABS - 1), (xm_ref, om_ref, 0, 0)):
        for b in range(3):
            j = 3 * a + b
            for c in range(3):
                place = pl.ds((3 * b + c) * ROWS, ROWS)
                low = turn(zp, -(16 * p + j)) if c == 2 else None
                high = turn(zm, LANES - 1 - 16 * p - j) if c == 0 else None
                value = move_z(ref[place, :], c, low, high, lanes)
                spot = pl.ds((3 * a + c) * 8 + p, 1)
                ghost = yp_ref[spot, :] if b == 2 else ym_ref[spot, :]
                out[place, :] = move_y(value, b, ghost, rows)


def stream_kernel(source, zp_ref, zm_ref, yp_ref, ym_ref, out_ref):
    lanes = lane_index(ROWS)
    rows = lax.broadcasted_iota(jnp.int32, (ROWS, LANES), 0)

    def step(p, carry):
        for a in range(3):
            origin = p if a == 1 else (jnp.maximum(p - 1, 0) if a == 2 else jnp.minimum(p + 1, SLABS - 1))
            back = lax.rem(LANES - 16 * origin, LANES)
            zp = turn(zp_ref[0:16, :], back)
            zm = turn(zm_ref[0:16, :], back)
            for b in range(3):
                j = 3 * a + b
                for c in range(3):
                    i = 9 * a + 3 * b + c
                    value = source[pl.ds(pl.multiple_of(i * TILES + origin * ROWS, ROWS), ROWS), :]
                    low = turn(zp, -j) if c == 2 else None
                    high = turn(zm, LANES - 1 - j) if c == 0 else None
                    value = move_z(value, c, low, high, lanes)
                    spot = pl.ds((3 * a + c) * 8 + origin, 1)
                    ghost = yp_ref[spot, :] if b == 2 else ym_ref[spot, :]
                    value = move_y(value, b, ghost, rows)
                    out_ref[pl.ds(pl.multiple_of(i * TILES + p * ROWS, ROWS), ROWS), :] = value
        return carry

    lax.fori_loop(0, SLABS, step, 0)


def fetch(source, target, semaphore):
    copy = pltpu.make_async_copy(source, target, semaphore)
    copy.start()
    return copy


def coarse_kernel(state_hbm, rates_hbm, table_hbm, *refs):
    outs, sent_ref = refs[:7], refs[7]
    state, rates, table, tiles, chunks, semaphores = refs[8:]
    first = fetch(rates_hbm, rates, semaphores.at[0])

    def chunk(k):
        rows = pl.ds(pl.multiple_of(k * 32, 32), 32)
        return pltpu.make_async_copy(state_hbm.at[:, rows, :], state.at[:, rows, :], chunks.at[k])

    for k in range(4):
        chunk(k).start()
    second = fetch(table_hbm, table, semaphores.at[1])
    first.wait()

    def ready(u):
        @pl.when(lax.rem(u, 4) == 0)
        def _():
            chunk(u // 4).wait()

    def load(i, u):
        return state[i, pl.ds(pl.multiple_of(u * 8, 8), 8), :]

    collide(load, None, rates, *outs, ready=ready)
    for k in range(9):
        tiles[pl.ds(k * WIDE, TILES), :] = state[18 + k]
    second.wait()
    pack(tiles, table, sent_ref, None)


def tile8(tiles, k, u):
    return tiles[pl.ds(pl.multiple_of(k * WIDE + u * 8, 8), 8), :]


def fine_first_kernel(state_hbm, flags_hbm, rates_hbm, table_hbm, received_ref, *refs):
    outs = refs[:7]
    state, flags, rates, table, tiles, chunks, semaphores = refs[7:]
    pieces = [
        fetch(
            state_hbm.at[pl.ds((18 + k) * TILES, TILES)], tiles.at[pl.ds(k * WIDE, TILES)], chunks.at[k]
        )
        for k in range(9)
    ]
    second = fetch(table_hbm, table, semaphores.at[0])
    others = [
        fetch(state_hbm.at[pl.ds(0, 18 * TILES)], state, semaphores.at[1]),
        fetch(flags_hbm, flags, semaphores.at[2]),
        fetch(rates_hbm, rates, semaphores.at[3]),
    ]
    for piece in pieces:
        piece.wait()
    second.wait()
    install(tiles, table, received_ref)
    for other in others:
        other.wait()

    def load(i, u):
        return tile8(tiles, i - 18, u) if i >= 18 else load8(state, i, u)

    collide(load, flags, rates, *outs)


def fine_second_kernel(state_ref, xp_ref, xm_ref, received_ref, flags_hbm, rates_hbm, table_hbm, *refs):
    outs = refs[:7]
    flags, rates, table, tiles, semaphores = refs[7:]
    first = fetch(table_hbm, table, semaphores.at[0])
    others = [fetch(flags_hbm, flags, semaphores.at[1]), fetch(rates_hbm, rates, semaphores.at[2])]
    fill(tiles, state_ref, 18, xp_ref, 0)
    first.wait()
    install(tiles, table, received_ref)
    for other in others:
        other.wait()

    def load(i, u):
        if i >= 18:
            return tile8(tiles, i - 18, u)
        value = load8(state_ref, i, u)
        if i < 9:
            ghost = xm_ref[pl.ds(pl.multiple_of(i * ROWS + lax.rem(u, 2) * 8, 8), 8), :]
            value = jnp.where(u >= 2 * SLABS - 2, ghost, value)
        return value

    collide(load, flags, rates, *outs)


def finish(state_ref, xp_ref, xm_ref, whole, out_hbm, semaphore):
    whole[...] = state_ref[...]
    for k in range(9):
        whole[pl.ds((18 + k) * TILES, ROWS), :] = xp_ref[pl.ds(k * ROWS, ROWS), :]
        whole[pl.ds(k * TILES + TILES - ROWS, ROWS), :] = xm_ref[pl.ds(k * ROWS, ROWS), :]
    return fetch(whole, out_hbm, semaphore)


def mean_kernel(state_ref, xp_ref, xm_ref, old_ref, table_hbm, sent_ref, kept_ref, out_hbm, *scratch):
    whole, table, tiles, semaphores = scratch
    first = fetch(table_hbm, table, semaphores.at[0])
    copy = finish(state_ref, xp_ref, xm_ref, whole, out_hbm, semaphores.at[1])
    fill(kept_ref, state_ref, 0, xm_ref, SLABS - 1)
    fill(tiles, state_ref, 18, xp_ref, 0)
    first.wait()
    pack(tiles, table, sent_ref, old_ref)
    copy.wait()


def up_kernel(state_ref, xp_ref, xm_ref, table_hbm, sent_ref, out_hbm, *scratch):
    whole, table, tiles, semaphores = scratch
    first = fetch(table_hbm, table, semaphores.at[0])
    copy = finish(state_ref, xp_ref, xm_ref, whole, out_hbm, semaphores.at[1])
    fill(tiles, state_ref, 0, xm_ref, SLABS - 1)
    first.wait()
    pack(tiles, table, sent_ref, None)
    copy.wait()


def coarse_install_kernel(whole_hbm, kept_ref, received_ref, table_hbm, out_hbm, *scratch):
    table, tiles, semaphores, chunks = scratch
    first = fetch(table_hbm, table, semaphores.at[0])
    for k in range(9):
        tiles[pl.ds(k * WIDE, TILES), :] = kept_ref[pl.ds(k * WIDE, TILES), :]
    first.wait()
    install(tiles, table, received_ref)
    copies = [
        fetch(tiles.at[pl.ds(k * WIDE, TILES)], out_hbm.at[pl.ds(k * TILES, TILES)], chunks.at[k])
        for k in range(9)
    ]
    for copy in copies:
        copy.wait()


STATE = (27 * TILES, LANES)
MESSAGE = (PEERS * CHUNK, LANES)
Z_FACE = (24, LANES)
Y_FACE = (9 * 8, LANES)
X_FACE = (9 * ROWS, LANES)
WIDE_TILES = (9 * WIDE, LANES)
COLLIDED = (STATE, Z_FACE, Z_FACE, Y_FACE, Y_FACE, X_FACE, X_FACE)


def floats(*shape):
    return pltpu.VMEM(shape, jnp.float32)


def copies(count):
    return pltpu.SemaphoreType.DMA((count,))


FLAGS = pltpu.VMEM((TILES, LANES), jnp.int32)
RATES = pltpu.SMEM((27,), jnp.float32)
TABLE = pltpu.SMEM((2, PEERS), jnp.int32)


def run(kernel, name, spaces, shapes, *operands, scratch=(), alias=False, microseconds=1.0):
    spots = {"v": pltpu.VMEM, "h": pltpu.HBM}
    given, made = spaces.split(":")
    operands = [
        pltpu.with_memory_space_constraint(operand, pltpu.HBM) if space == "h" else operand
        for operand, space in zip(operands, given)
    ]
    return pl.pallas_call(
        kernel,
        name=name,
        out_shape=tuple(jax.ShapeDtypeStruct(shape, jnp.float32) for shape in shapes),
        in_specs=[pl.BlockSpec(memory_space=spots[space]) for space in given],
        out_specs=tuple(pl.BlockSpec(memory_space=spots[space]) for space in made),
        scratch_shapes=list(scratch),
        input_output_aliases={0: 0} if alias else {},
        compiler_params=pltpu.CompilerParams(vmem_limit_bytes=VMEM_BYTES),
        cost_estimate=pl.CostEstimate(
            flops=0, bytes_accessed=int(microseconds * 3.0e6), transcendentals=0
        ),
    )(*operands)


def swap(plus, minus, axis):
    count = lax.axis_size(axis)
    up = [(i, (i + 1) % count) for i in range(count)]
    down = [(i, (i - 1) % count) for i in range(count)]
    return lax.ppermute(plus, axis, up), lax.ppermute(minus, axis, down)


def halo(collided, zp, zm, yp, ym, xp, xm):
    zp, zm = swap(zp, zm, "gz")
    yp, ym = run(face_y_kernel, "face_y", "vvvv:vv", (Y_FACE, Y_FACE), yp, ym, zp, zm)
    yp, ym = swap(yp, ym, "gy")
    xp, xm = run(face_x_kernel, "face_x", "vvvvvv:vv", (X_FACE, X_FACE), xp, xm, zp, zm, yp, ym)
    xp, xm = swap(xp, xm, "gx")
    (moved,) = run(
        stream_kernel, "stream", "vvvvv:v", (STATE,), collided, zp, zm, yp, ym, microseconds=2.0
    )
    return moved, xp, xm


def routed(message):
    chunks = message.reshape(PEERS, 9, 2, LANES)
    received = lax.all_to_all(chunks, ("gx", "gz"), split_axis=0, concat_axis=0, tiled=True)
    return received.reshape(MESSAGE)


def body(fine, coarse, fine_rates, coarse_rates, flags, down_source, down_target, up_source, up_target):
    fine = fine.reshape(STATE)
    coarse = coarse.reshape(27, TILES, LANES)
    flags = flags.reshape(TILES, LANES)
    down_source, down_target, up_source, up_target = (
        table.reshape(-1, 2).T for table in (down_source, down_target, up_source, up_target)
    )
    *parts, sent_old = run(
        coarse_kernel, "coarse_collide", "hhh:vvvvvvvv", COLLIDED + (MESSAGE,),
        coarse, coarse_rates, down_source,
        scratch=(floats(27, TILES, LANES), RATES, TABLE, floats(*WIDE_TILES), copies(4), copies(2)),
        microseconds=4.0,
    )
    old = routed(sent_old)
    moved, xp, xm = halo(*parts)
    sent_mean, kept, coarse_new = run(
        mean_kernel, "pack_mean", "vvvvh:vvh", (MESSAGE, WIDE_TILES, STATE),
        moved, xp, xm, sent_old, down_source,
        scratch=(floats(*STATE), TABLE, floats(*WIDE_TILES), copies(2)),
        microseconds=2.0,
    )
    mean = routed(sent_mean)
    parts = run(
        fine_first_kernel, "fine_first", "hhhhv:vvvvvvv", COLLIDED,
        fine, flags, fine_rates, down_target, old,
        scratch=(
            floats(18 * TILES, LANES), FLAGS, RATES, TABLE, floats(*WIDE_TILES), copies(9), copies(4)
        ),
        microseconds=4.0,
    )
    moved, xp, xm = halo(*parts)
    parts = run(
        fine_second_kernel, "fine_second", "vvvvhhh:vvvvvvv", COLLIDED,
        moved, xp, xm, mean, flags, fine_rates, down_target,
        scratch=(FLAGS, RATES, TABLE, floats(*WIDE_TILES), copies(3)),
        microseconds=4.0,
    )
    moved, xp, xm = halo(*parts)
    sent_up, fine_next = run(
        up_kernel, "pack_up", "vvvh:vh", (MESSAGE, STATE), moved, xp, xm, up_source,
        scratch=(floats(*STATE), TABLE, floats(*WIDE_TILES), copies(2)),
        microseconds=2.0,
    )
    up = routed(sent_up)
    (coarse_next,) = run(
        coarse_install_kernel, "coarse_install", "hvvh:h", (STATE,), coarse_new, kept, up, up_target,
        scratch=(TABLE, floats(*WIDE_TILES), copies(1), copies(9)),
        alias=True,
        microseconds=2.0,
    )
    block = (27, SLABS, ROWS, LANES)
    return fine_next.reshape(block), coarse_next.reshape(block)


def solution(mesh):
    placed = (
        P(None, "gx", "gy", "gz"),
        P(None, "gx", "gy", "gz"),
        P(),
        P(),
        P("gx", "gy", "gz"),
        P("gx", "gy", "gz", None, None),
        P("gx", "gy", "gz", None, None),
        P("gx", "gy", "gz", None, None),
        P("gx", "gy", "gz", None, None),
    )
    return jax.shard_map(
        body,
        mesh=mesh,
        in_specs=placed,
        out_specs=(P(None, "gx", "gy", "gz"), P(None, "gx", "gy", "gz")),
        check_vma=False,
    )
```

```python
import jax
import jax.numpy as jnp
from jax import lax
from jax.experimental import pallas as pl
from jax.experimental.pallas import tpu as pltpu
from jax.sharding import PartitionSpec as P

SLABS = 8
ROWS = 16
LANES = 128
TILES = SLABS * ROWS
CHUNK = 18
PEERS = 64
VMEM_BYTES = 10 * 1024 * 1024
WIDE = 136


def load8(ref, i, u):
    return ref[pl.ds(pl.multiple_of(i * TILES + u * 8, 8), 8), :]


def fetch(source, target, semaphore):
    copy = pltpu.make_async_copy(source, target, semaphore)
    copy.start()
    return copy


def wait(copies):
    for copy in copies:
        copy.wait()


def forward(values):
    for step in (9, 3, 1):
        out = list(values)
        for i in range(27):
            if (i // step) % 3 == 0:
                low, mid, high = values[i], values[i + step], values[i + 2 * step]
                even = high + low
                out[i] = even + 4.0 * mid
                out[i + step] = high - low
                out[i + 2 * step] = even
        values = out
    return values


def backward(values):
    for step in (9, 3, 1):
        out = list(values)
        for i in range(27):
            if (i // step) % 3 == 0:
                zero, one, two = values[i], values[i + step], values[i + 2 * step]
                out[i] = two - one
                out[i + step] = zero - two
                out[i + 2 * step] = two + one
        values = out
    return values


def equilibrium(moments):
    density = moments[0]
    momentum = (moments[9], moments[3], moments[1])
    squares = [part * part * (1.0 / 72.0) for part in momentum]
    scale = (1.0, 1.0 / 3.0, 1.0 / 9.0, 1.0 / 27.0)
    result = []
    for k in range(27):
        powers = (k // 9, (k // 3) % 3, k % 3)
        ones = [axis for axis in range(3) if powers[axis] == 1]
        twos = [axis for axis in range(3) if powers[axis] == 2]
        if len(ones) == 0:
            value = density
            for axis in twos:
                value = value + squares[axis]
        elif len(ones) == 1:
            value = momentum[ones[0]]
        elif len(ones) == 2:
            value = momentum[ones[0]] * momentum[ones[1]] * (1.0 / 216.0)
        else:
            value = jnp.zeros_like(density)
        if twos:
            value = value * scale[len(twos)]
        result.append(value)
    return result


def relax(values, rates_ref):
    moments = forward(values)
    target = equilibrium(moments)
    change = backward([(rates_ref[k] * 0.125) * (target[k] - moments[k]) for k in range(27)])
    result = []
    for i in range(27):
        rests = sum(1 for part in (i // 9, (i // 3) % 3, i % 3) if part == 1)
        moved = change[i] if rests == 0 else change[i] * (0.5**rests)
        result.append(values[i] + moved)
    return result


def lane_index(rows):
    return lax.broadcasted_iota(jnp.int32, (rows, LANES), 1)


def turn(value, amount):
    amount = amount % LANES if isinstance(amount, int) else amount
    if isinstance(amount, int) and amount == 0:
        return value
    return pltpu.roll(value, amount, 1)


def collide(load, flags_ref, rates_ref, out_ref, zp_ref, zm_ref, yp_ref, ym_ref, xp_ref, xm_ref, ready=None):
    def step(u, carry):
        if ready is not None:
            ready(u)
        values = [load(i, u) for i in range(27)]
        result = relax(values, rates_ref)
        if flags_ref is not None:
            solid = flags_ref[pl.ds(pl.multiple_of(u * 8, 8), 8), :] == 1
            result = [jnp.where(solid, values[26 - i], result[i]) for i in range(27)]
        for i in range(27):
            out_ref[pl.ds(pl.multiple_of(i * TILES + u * 8, 8), 8), :] = result[i]
        return carry

    lax.fori_loop(0, 2 * SLABS, step, 0, unroll=2)
    lanes = lane_index(8)
    for ref, c, edge in ((zp_ref, 2, LANES - 1), (zm_ref, 0, 0)):
        for half in range(2):
            packed = None
            for p in range(SLABS):
                for j in range(9):
                    start = (3 * j + c) * TILES + p * ROWS + half * 8
                    column = turn(out_ref[start : start + 8, :], 16 * p + j - edge)
                    packed = column if packed is None else jnp.where(lanes == 16 * p + j, column, packed)
            ref[half * 8 : half * 8 + 8, :] = packed
    ends = [jnp.zeros((8, LANES), jnp.float32), None, jnp.zeros((8, LANES), jnp.float32)]
    for ref, b, q in ((yp_ref, 2, ROWS - 1), (ym_ref, 0, 0)):
        for a in range(3):
            for c in range(3):
                i = 9 * a + 3 * b + c
                rows = out_ref[pl.ds(i * TILES + q, 8, stride=ROWS), :]
                ref[pl.ds((3 * a + c) * 8, 8), :] = rows
                j = 3 * a + b
                if c != 1:
                    edge = LANES - 1 if c == 2 else 0
                    ends[c] = jnp.where(lanes == j, turn(rows, j - edge), ends[c])
    zp_ref[16:24, :] = ends[2]
    zm_ref[16:24, :] = ends[0]
    for j in range(9):
        xp_ref[pl.ds(j * ROWS, ROWS), :] = out_ref[pl.ds((18 + j) * TILES + 7 * ROWS, ROWS), :]
        xm_ref[pl.ds(j * ROWS, ROWS), :] = out_ref[pl.ds(j * TILES, ROWS), :]


def fill(tiles, state_ref, first, ghost_ref=None, slab=None):
    for k in range(9):
        tiles[pl.ds(k * WIDE, TILES), :] = state_ref[pl.ds((first + k) * TILES, TILES), :]
        if ghost_ref is not None:
            tiles[pl.ds(k * WIDE + slab * ROWS, ROWS), :] = ghost_ref[pl.ds(k * ROWS, ROWS), :]


def pack(tiles, table_ref, sent, out_hbm, semaphores):
    def step(r, carry):
        for j in range(2):
            tile = jnp.maximum(table_ref[j, r], 0)
            most = tiles[pl.ds(tile, 8, stride=WIDE), :]
            last = tiles[pl.ds(8 * WIDE + tile, 1), :]
            sent[pl.ds(r * CHUNK + j, 8, stride=2), :] = most
            sent[pl.ds(r * CHUNK + 16 + j, 1), :] = last
        return carry

    bounds = [PEERS * k // 4 for k in range(5)]
    copies = []
    for k in range(4):
        lax.fori_loop(bounds[k], bounds[k + 1], step, 0, unroll=4)
        rows = pl.ds(bounds[k] * CHUNK, (bounds[k + 1] - bounds[k]) * CHUNK)
        copies.append(fetch(sent.at[rows], out_hbm.at[rows], semaphores.at[k]))
    return copies


def install(tiles, table_ref, received_ref):
    def step(r, carry):
        moved = []
        for j in range(2):
            tile = table_ref[j, r]
            tile = jnp.where(tile < 0, TILES, tile)
            most = received_ref[pl.ds(r * CHUNK + j, 8, stride=2), :]
            last = received_ref[pl.ds(r * CHUNK + 16 + j, 1), :]
            moved.append((tile, most, last))
        for tile, most, last in moved:
            tiles[pl.ds(tile, 8, stride=WIDE), :] = most
            tiles[pl.ds(8 * WIDE + tile, 1), :] = last
        return carry

    lax.fori_loop(0, PEERS, step, 0, unroll=4)


def move_z(value, c, low_ghost, high_ghost, lanes):
    if c == 2:
        return jnp.where(lanes == 0, low_ghost, turn(value, 1))
    if c == 0:
        return jnp.where(lanes == LANES - 1, high_ghost, turn(value, LANES - 1))
    return value


def move_y(value, b, ghost, rows):
    if b == 2:
        return jnp.where(rows == 0, ghost, pltpu.roll(value, 1, 0))
    if b == 0:
        return jnp.where(rows == ROWS - 1, ghost, pltpu.roll(value, ROWS - 1, 0))
    return value


def face_y_kernel(yp_ref, ym_ref, zp_ref, zm_ref, op_ref, om_ref):
    lanes = lane_index(8)
    zp, zm = zp_ref[16:24, :], zm_ref[16:24, :]
    for ref, out, b in ((yp_ref, op_ref, 2), (ym_ref, om_ref, 0)):
        for a in range(3):
            j = 3 * a + b
            for c in range(3):
                place = pl.ds((3 * a + c) * 8, 8)
                low = turn(zp, -j) if c == 2 else None
                high = turn(zm, LANES - 1 - j) if c == 0 else None
                out[place, :] = move_z(ref[place, :], c, low, high, lanes)


def face_x_kernel(xp_ref, xm_ref, zp_ref, zm_ref, yp_ref, ym_ref, *refs):
    op_ref, om_ref = refs[-2:]
    for extra_ref in refs[:-2]:
        om_ref[pl.ds(9 * ROWS, 9 * ROWS), :] = extra_ref[...]
    lanes = lane_index(ROWS)
    rows = lax.broadcasted_iota(jnp.int32, (ROWS, LANES), 0)
    zp, zm = zp_ref[0:16, :], zm_ref[0:16, :]
    for ref, out, a, p in ((xp_ref, op_ref, 2, SLABS - 1), (xm_ref, om_ref, 0, 0)):
        for b in range(3):
            j = 3 * a + b
            for c in range(3):
                place = pl.ds((3 * b + c) * ROWS, ROWS)
                low = turn(zp, -(16 * p + j)) if c == 2 else None
                high = turn(zm, LANES - 1 - 16 * p - j) if c == 0 else None
                value = move_z(ref[place, :], c, low, high, lanes)
                spot = pl.ds((3 * a + c) * 8 + p, 1)
                ghost = yp_ref[spot, :] if b == 2 else ym_ref[spot, :]
                out[place, :] = move_y(value, b, ghost, rows)


def stream_kernel(source, zp_ref, zm_ref, yp_ref, ym_ref, out_ref):
    lanes = lane_index(ROWS)
    rows = lax.broadcasted_iota(jnp.int32, (ROWS, LANES), 0)

    def step(p, carry):
        for a in range(3):
            origin = p if a == 1 else (jnp.maximum(p - 1, 0) if a == 2 else jnp.minimum(p + 1, SLABS - 1))
            back = lax.rem(LANES - 16 * origin, LANES)
            zp = turn(zp_ref[0:16, :], back)
            zm = turn(zm_ref[0:16, :], back)
            for b in range(3):
                j = 3 * a + b
                for c in range(3):
                    i = 9 * a + 3 * b + c
                    value = source[pl.ds(pl.multiple_of(i * TILES + origin * ROWS, ROWS), ROWS), :]
                    low = turn(zp, -j) if c == 2 else None
                    high = turn(zm, LANES - 1 - j) if c == 0 else None
                    value = move_z(value, c, low, high, lanes)
                    spot = pl.ds((3 * a + c) * 8 + origin, 1)
                    ghost = yp_ref[spot, :] if b == 2 else ym_ref[spot, :]
                    value = move_y(value, b, ghost, rows)
                    out_ref[pl.ds(pl.multiple_of(i * TILES + p * ROWS, ROWS), ROWS), :] = value
        return carry

    lax.fori_loop(0, SLABS, step, 0)


def coarse_kernel(state_hbm, rates_hbm, table_hbm, *refs):
    outs, sent_hbm = refs[:7], refs[7]
    state, rates, table, tiles, sent, chunks, semaphores, sends = refs[8:]
    first = fetch(rates_hbm, rates, semaphores.at[0])

    def chunk(k):
        rows = pl.ds(pl.multiple_of(k * 32, 32), 32)
        return pltpu.make_async_copy(state_hbm.at[:, rows, :], state.at[:, rows, :], chunks.at[k])

    for k in range(4):
        chunk(k).start()
    second = fetch(table_hbm, table, semaphores.at[1])
    first.wait()

    def ready(u):
        @pl.when(lax.rem(u, 4) == 0)
        def _():
            chunk(u // 4).wait()

    def load(i, u):
        return state[i, pl.ds(pl.multiple_of(u * 8, 8), 8), :]

    collide(load, None, rates, *outs, ready=ready)
    for k in range(9):
        tiles[pl.ds(k * WIDE, TILES), :] = state[18 + k]
    second.wait()
    wait(pack(tiles, table, sent, sent_hbm, sends))


def tile8(tiles, k, u):
    return tiles[pl.ds(pl.multiple_of(k * WIDE + u * 8, 8), 8), :]


def fine_first_kernel(state_hbm, flags_hbm, rates_hbm, table_hbm, received_ref, *refs):
    outs = refs[:7]
    state, flags, rates, table, tiles, chunks, semaphores = refs[7:]
    pieces = [
        fetch(
            state_hbm.at[pl.ds((18 + k) * TILES, TILES)], tiles.at[pl.ds(k * WIDE, TILES)], chunks.at[k]
        )
        for k in range(9)
    ]
    second = fetch(table_hbm, table, semaphores.at[0])
    others = [
        fetch(state_hbm.at[pl.ds(0, 18 * TILES)], state, semaphores.at[1]),
        fetch(flags_hbm, flags, semaphores.at[2]),
        fetch(rates_hbm, rates, semaphores.at[3]),
    ]
    for piece in pieces:
        piece.wait()
    second.wait()
    install(tiles, table, received_ref)
    for other in others:
        other.wait()

    def load(i, u):
        return tile8(tiles, i - 18, u) if i >= 18 else load8(state, i, u)

    collide(load, flags, rates, *outs)


def fine_second_kernel(state_ref, xp_ref, xm_ref, received_ref, flags_hbm, rates_hbm, table_hbm, *refs):
    outs = refs[:7]
    flags, rates, table, tiles, semaphores = refs[7:]
    first = fetch(table_hbm, table, semaphores.at[0])
    others = [fetch(flags_hbm, flags, semaphores.at[1]), fetch(rates_hbm, rates, semaphores.at[2])]
    fill(tiles, state_ref, 18, xp_ref, 0)
    first.wait()
    install(tiles, table, received_ref)
    for other in others:
        other.wait()

    def load(i, u):
        if i >= 18:
            return tile8(tiles, i - 18, u)
        value = load8(state_ref, i, u)
        if i < 9:
            ghost = xm_ref[pl.ds(pl.multiple_of(i * ROWS + lax.rem(u, 2) * 8, 8), 8), :]
            value = jnp.where(u >= 2 * SLABS - 2, ghost, value)
        return value

    collide(load, flags, rates, *outs)


def plain(rows, state_ref, first, ghost_ref=None, slab=None):
    rows[...] = state_ref[pl.ds(first * TILES, 9 * TILES), :]
    if ghost_ref is not None:
        for k in range(9):
            rows[pl.ds(k * TILES + slab * ROWS, ROWS), :] = ghost_ref[pl.ds(k * ROWS, ROWS), :]


def mean_kernel(state_ref, xp_ref, old_hbm, table_hbm, sent_hbm, kept_ref, out_hbm, *scratch):
    old, fresh, table, tiles, sent, semaphores, sends = scratch
    middle = pl.ds(9 * TILES, 9 * TILES)
    upper = pl.ds(18 * TILES, 9 * TILES)
    first = fetch(old_hbm.at[upper], old, semaphores.at[0])
    second = fetch(table_hbm, table, semaphores.at[1])
    stores = [fetch(state_ref.at[middle], out_hbm.at[middle], semaphores.at[2])]
    plain(fresh, state_ref, 18, xp_ref, 0)
    stores.append(fetch(fresh, out_hbm.at[upper], semaphores.at[3]))
    plain(kept_ref, state_ref, 0)
    first.wait()
    for k in range(9):
        rows = pl.ds(k * TILES, TILES)
        tiles[pl.ds(k * WIDE, TILES), :] = 0.5 * (old[rows, :] + fresh[rows, :])
    second.wait()
    stores += pack(tiles, table, sent, sent_hbm, sends)
    wait(stores)


def up_kernel(state_ref, xp_ref, xm_ref, table_hbm, sent_hbm, out_hbm, *scratch):
    low, high, table, tiles, sent, semaphores, sends = scratch
    lower = pl.ds(0, 9 * TILES)
    middle = pl.ds(9 * TILES, 9 * TILES)
    upper = pl.ds(18 * TILES, 9 * TILES)
    first = fetch(table_hbm, table, semaphores.at[0])
    stores = [fetch(state_ref.at[middle], out_hbm.at[middle], semaphores.at[1])]
    plain(low, state_ref, 0, xm_ref, SLABS - 1)
    stores.append(fetch(low, out_hbm.at[lower], semaphores.at[2]))
    for k in range(9):
        tiles[pl.ds(k * WIDE, TILES), :] = low[pl.ds(k * TILES, TILES), :]
    first.wait()
    sends = pack(tiles, table, sent, sent_hbm, sends)
    plain(high, state_ref, 18, xp_ref, 0)
    stores.append(fetch(high, out_hbm.at[upper], semaphores.at[3]))
    wait(sends + stores)


def coarse_install_kernel(whole_hbm, kept_ref, xm_ref, received_ref, table_hbm, out_hbm, *scratch):
    table, tiles, semaphores, stores = scratch
    first = fetch(table_hbm, table, semaphores.at[0])
    for k in range(9):
        tiles[pl.ds(k * WIDE, TILES), :] = kept_ref[pl.ds(k * TILES, TILES), :]
        ghost = xm_ref[pl.ds((9 + k) * ROWS, ROWS), :]
        tiles[pl.ds(k * WIDE + TILES - ROWS, ROWS), :] = ghost
    first.wait()
    install(tiles, table, received_ref)
    wait(
        [
            fetch(tiles.at[pl.ds(k * WIDE, TILES)], out_hbm.at[pl.ds(k * TILES, TILES)], stores.at[k])
            for k in range(9)
        ]
    )


STATE = (27 * TILES, LANES)
MESSAGE = (PEERS * CHUNK, LANES)
Z_FACE = (24, LANES)
Y_FACE = (9 * 8, LANES)
X_FACE = (9 * ROWS, LANES)
WIDE_TILES = (9 * WIDE, LANES)
NINE = (9 * TILES, LANES)
COLLIDED = (STATE, Z_FACE, Z_FACE, Y_FACE, Y_FACE, X_FACE, X_FACE)


def floats(*shape):
    return pltpu.VMEM(shape, jnp.float32)


def copies(count):
    return pltpu.SemaphoreType.DMA((count,))


FLAGS = pltpu.VMEM((TILES, LANES), jnp.int32)
RATES = pltpu.SMEM((27,), jnp.float32)
TABLE = pltpu.SMEM((2, PEERS), jnp.int32)


def run(kernel, name, spaces, shapes, *operands, scratch=(), alias=False, microseconds=1.0):
    spots = {"v": pltpu.VMEM, "h": pltpu.HBM}
    given, made = spaces.split(":")
    operands = [
        pltpu.with_memory_space_constraint(operand, pltpu.HBM) if space == "h" else operand
        for operand, space in zip(operands, given)
    ]
    return pl.pallas_call(
        kernel,
        name=name,
        out_shape=tuple(jax.ShapeDtypeStruct(shape, jnp.float32) for shape in shapes),
        in_specs=[pl.BlockSpec(memory_space=spots[space]) for space in given],
        out_specs=tuple(pl.BlockSpec(memory_space=spots[space]) for space in made),
        scratch_shapes=list(scratch),
        input_output_aliases={0: 0} if alias else {},
        compiler_params=pltpu.CompilerParams(vmem_limit_bytes=VMEM_BYTES),
        cost_estimate=pl.CostEstimate(
            flops=0, bytes_accessed=int(microseconds * 3.0e6), transcendentals=0
        ),
    )(*operands)


def swap(axis, plus, minus=None):
    count = lax.axis_size(axis)
    up = [(i, (i + 1) % count) for i in range(count)]
    down = [(i, (i - 1) % count) for i in range(count)]
    plus = lax.ppermute(plus, axis, up)
    return plus if minus is None else (plus, lax.ppermute(minus, axis, down))


def halo(collided, zp, zm, yp, ym, xp, xm):
    zp, zm = swap("gz", zp, zm)
    yp, ym = run(face_y_kernel, "face_y", "vvvv:vv", (Y_FACE, Y_FACE), yp, ym, zp, zm)
    yp, ym = swap("gy", yp, ym)
    return (xp, xm, zp, zm, yp, ym), (collided, zp, zm, yp, ym)


def stream(operands):
    return run(stream_kernel, "stream", "vvvvv:v", (STATE,), *operands, microseconds=2.0)[0]


def routed(message):
    chunks = message.reshape(PEERS, 9, 2, LANES)
    received = lax.all_to_all(chunks, ("gx", "gz"), split_axis=0, concat_axis=0, tiled=True)
    return received.reshape(MESSAGE)


def body(fine, coarse, fine_rates, coarse_rates, flags, down_source, down_target, up_source, up_target):
    fine = fine.reshape(STATE)
    coarse = coarse.reshape(STATE)
    flags = flags.reshape(TILES, LANES)
    down_source, down_target, up_source, up_target = (
        table.reshape(-1, 2).T for table in (down_source, down_target, up_source, up_target)
    )
    *parts, sent_old = run(
        coarse_kernel, "coarse_collide", "hhh:vvvvvvvh", COLLIDED + (MESSAGE,),
        coarse.reshape(27, TILES, LANES), coarse_rates, down_source,
        scratch=(
            floats(27, TILES, LANES), RATES, TABLE, floats(*WIDE_TILES), floats(*MESSAGE),
            copies(4), copies(2), copies(4),
        ),
        microseconds=4.0,
    )
    old = routed(sent_old)
    faces, whole = halo(*parts)
    xp, coarse_xm = run(face_x_kernel, "face_x", "vvvvvv:vv", (X_FACE, X_FACE), *faces)
    xp = swap("gx", xp)
    sent_mean, kept, coarse_new = run(
        mean_kernel, "pack_mean", "vvhh:hvh", (MESSAGE, NINE, STATE),
        stream(whole), xp, coarse, down_source,
        scratch=(
            floats(*NINE), floats(*NINE), TABLE, floats(*WIDE_TILES), floats(*MESSAGE), copies(4), copies(4)
        ),
        microseconds=2.0,
    )
    mean = routed(sent_mean)
    parts = run(
        fine_first_kernel, "fine_first", "hhhhv:vvvvvvv", COLLIDED,
        fine, flags, fine_rates, down_target, old,
        scratch=(
            floats(18 * TILES, LANES), FLAGS, RATES, TABLE, floats(*WIDE_TILES), copies(9), copies(4)
        ),
        microseconds=4.0,
    )
    faces, whole = halo(*parts)
    xp, xm = run(
        face_x_kernel, "face_x", "vvvvvvv:vv", (X_FACE, (2 * X_FACE[0], LANES)), *faces, coarse_xm
    )
    xp, both_xm = swap("gx", xp, xm)
    parts = run(
        fine_second_kernel, "fine_second", "vvvvhhh:vvvvvvv", COLLIDED,
        stream(whole), xp, both_xm, mean, flags, fine_rates, down_target,
        scratch=(FLAGS, RATES, TABLE, floats(*WIDE_TILES), copies(3)),
        microseconds=4.0,
    )
    faces, whole = halo(*parts)
    xp, xm = run(face_x_kernel, "face_x", "vvvvvv:vv", (X_FACE, X_FACE), *faces)
    xp, xm = swap("gx", xp, xm)
    sent_up, fine_next = run(
        up_kernel, "pack_up", "vvvh:hh", (MESSAGE, STATE), stream(whole), xp, xm, up_source,
        scratch=(
            floats(*NINE), floats(*NINE), TABLE, floats(*WIDE_TILES), floats(*MESSAGE), copies(4), copies(4)
        ),
        microseconds=2.0,
    )
    up = routed(sent_up)
    (coarse_next,) = run(
        coarse_install_kernel, "coarse_install", "hvvvh:h", (STATE,),
        coarse_new, kept, both_xm, up, up_target,
        scratch=(TABLE, floats(*WIDE_TILES), copies(1), copies(9)),
        alias=True,
        microseconds=2.0,
    )
    block = (27, SLABS, ROWS, LANES)
    return fine_next.reshape(block), coarse_next.reshape(block)


def solution(mesh):
    placed = (
        P(None, "gx", "gy", "gz"),
        P(None, "gx", "gy", "gz"),
        P(),
        P(),
        P("gx", "gy", "gz"),
        P("gx", "gy", "gz", None, None),
        P("gx", "gy", "gz", None, None),
        P("gx", "gy", "gz", None, None),
        P("gx", "gy", "gz", None, None),
    )
    return jax.shard_map(
        body,
        mesh=mesh,
        in_specs=placed,
        out_specs=(P(None, "gx", "gy", "gz"), P(None, "gx", "gy", "gz")),
        check_vma=False,
    )
```

```python
import jax
import jax.numpy as jnp
from jax import lax
from jax.experimental import pallas as pl
from jax.experimental.pallas import tpu as pltpu
from jax.sharding import PartitionSpec as P

SLABS = 8
ROWS = 16
LANES = 128
TILES = SLABS * ROWS
CHUNK = 18
PEERS = 64
OLD_COST = 2.0
VMEM_BYTES = 10 * 1024 * 1024
WIDE = 136


def load8(ref, i, u):
    return ref[pl.ds(pl.multiple_of(i * TILES + u * 8, 8), 8), :]


def fetch(source, target, semaphore):
    copy = pltpu.make_async_copy(source, target, semaphore)
    copy.start()
    return copy


def wait(copies):
    for copy in copies:
        copy.wait()


def forward(values):
    for step in (9, 3, 1):
        out = list(values)
        for i in range(27):
            if (i // step) % 3 == 0:
                low, mid, high = values[i], values[i + step], values[i + 2 * step]
                even = high + low
                out[i] = even + 4.0 * mid
                out[i + step] = high - low
                out[i + 2 * step] = even
        values = out
    return values


def backward(values):
    for step in (9, 3, 1):
        out = list(values)
        for i in range(27):
            if (i // step) % 3 == 0:
                zero, one, two = values[i], values[i + step], values[i + 2 * step]
                out[i] = two - one
                out[i + step] = zero - two
                out[i + 2 * step] = two + one
        values = out
    return values


def equilibrium(moments):
    density = moments[0]
    momentum = (moments[9], moments[3], moments[1])
    squares = [part * part * (1.0 / 72.0) for part in momentum]
    scale = (1.0, 1.0 / 3.0, 1.0 / 9.0, 1.0 / 27.0)
    result = []
    for k in range(27):
        powers = (k // 9, (k // 3) % 3, k % 3)
        ones = [axis for axis in range(3) if powers[axis] == 1]
        twos = [axis for axis in range(3) if powers[axis] == 2]
        if len(ones) == 0:
            value = density
            for axis in twos:
                value = value + squares[axis]
        elif len(ones) == 1:
            value = momentum[ones[0]]
        elif len(ones) == 2:
            value = momentum[ones[0]] * momentum[ones[1]] * (1.0 / 216.0)
        else:
            value = jnp.zeros_like(density)
        if twos:
            value = value * scale[len(twos)]
        result.append(value)
    return result


def relax(values, rates_ref):
    moments = forward(values)
    target = equilibrium(moments)
    change = backward([(rates_ref[k] * 0.125) * (target[k] - moments[k]) for k in range(27)])
    result = []
    for i in range(27):
        rests = sum(1 for part in (i // 9, (i // 3) % 3, i % 3) if part == 1)
        moved = change[i] if rests == 0 else change[i] * (0.5**rests)
        result.append(values[i] + moved)
    return result


def lane_index(rows):
    return lax.broadcasted_iota(jnp.int32, (rows, LANES), 1)


def turn(value, amount):
    amount = amount % LANES if isinstance(amount, int) else amount
    if isinstance(amount, int) and amount == 0:
        return value
    return pltpu.roll(value, amount, 1)


def collide(load, flags_ref, rates_ref, out_ref, zp_ref, zm_ref, yp_ref, ym_ref, xp_ref, xm_ref, ready=None):
    def step(u, carry):
        if ready is not None:
            ready(u)
        values = [load(i, u) for i in range(27)]
        result = relax(values, rates_ref)
        if flags_ref is not None:
            solid = flags_ref[pl.ds(pl.multiple_of(u * 8, 8), 8), :] == 1
            result = [jnp.where(solid, values[26 - i], result[i]) for i in range(27)]
        for i in range(27):
            out_ref[pl.ds(pl.multiple_of(i * TILES + u * 8, 8), 8), :] = result[i]
        return carry

    lax.fori_loop(0, 2 * SLABS, step, 0, unroll=2)
    lanes = lane_index(8)
    for ref, c, edge in ((zp_ref, 2, LANES - 1), (zm_ref, 0, 0)):
        for half in range(2):
            packed = None
            for p in range(SLABS):
                for j in range(9):
                    start = (3 * j + c) * TILES + p * ROWS + half * 8
                    column = turn(out_ref[start : start + 8, :], 16 * p + j - edge)
                    packed = column if packed is None else jnp.where(lanes == 16 * p + j, column, packed)
            ref[half * 8 : half * 8 + 8, :] = packed
    ends = [jnp.zeros((8, LANES), jnp.float32), None, jnp.zeros((8, LANES), jnp.float32)]
    for ref, b, q in ((yp_ref, 2, ROWS - 1), (ym_ref, 0, 0)):
        for a in range(3):
            for c in range(3):
                i = 9 * a + 3 * b + c
                rows = out_ref[pl.ds(i * TILES + q, 8, stride=ROWS), :]
                ref[pl.ds((3 * a + c) * 8, 8), :] = rows
                j = 3 * a + b
                if c != 1:
                    edge = LANES - 1 if c == 2 else 0
                    ends[c] = jnp.where(lanes == j, turn(rows, j - edge), ends[c])
    zp_ref[16:24, :] = ends[2]
    zm_ref[16:24, :] = ends[0]
    for j in range(9):
        xp_ref[pl.ds(j * ROWS, ROWS), :] = out_ref[pl.ds((18 + j) * TILES + 7 * ROWS, ROWS), :]
        xm_ref[pl.ds(j * ROWS, ROWS), :] = out_ref[pl.ds(j * TILES, ROWS), :]


def fill(tiles, state_ref, first, ghost_ref=None, slab=None):
    for k in range(9):
        tiles[pl.ds(k * WIDE, TILES), :] = state_ref[pl.ds((first + k) * TILES, TILES), :]
        if ghost_ref is not None:
            tiles[pl.ds(k * WIDE + slab * ROWS, ROWS), :] = ghost_ref[pl.ds(k * ROWS, ROWS), :]


def pack(tiles, table_ref, sent):
    def step(r, carry):
        for j in range(2):
            tile = jnp.maximum(table_ref[j, r], 0)
            most = tiles[pl.ds(tile, 8, stride=WIDE), :]
            last = tiles[pl.ds(8 * WIDE + tile, 1), :]
            sent[pl.ds(r * CHUNK + j, 8, stride=2), :] = most
            sent[pl.ds(r * CHUNK + 16 + j, 1), :] = last
        return carry

    lax.fori_loop(0, PEERS, step, 0, unroll=4)


def install(tiles, table_ref, received_ref):
    def step(r, carry):
        moved = []
        for j in range(2):
            tile = table_ref[j, r]
            tile = jnp.where(tile < 0, TILES, tile)
            most = received_ref[pl.ds(r * CHUNK + j, 8, stride=2), :]
            last = received_ref[pl.ds(r * CHUNK + 16 + j, 1), :]
            moved.append((tile, most, last))
        for tile, most, last in moved:
            tiles[pl.ds(tile, 8, stride=WIDE), :] = most
            tiles[pl.ds(8 * WIDE + tile, 1), :] = last
        return carry

    lax.fori_loop(0, PEERS, step, 0, unroll=4)


def move_z(value, c, low_ghost, high_ghost, lanes):
    if c == 2:
        return jnp.where(lanes == 0, low_ghost, turn(value, 1))
    if c == 0:
        return jnp.where(lanes == LANES - 1, high_ghost, turn(value, LANES - 1))
    return value


def move_y(value, b, ghost, rows):
    if b == 2:
        return jnp.where(rows == 0, ghost, pltpu.roll(value, 1, 0))
    if b == 0:
        return jnp.where(rows == ROWS - 1, ghost, pltpu.roll(value, ROWS - 1, 0))
    return value


def face_y_kernel(yp_ref, ym_ref, zp_ref, zm_ref, op_ref, om_ref):
    lanes = lane_index(8)
    zp, zm = zp_ref[16:24, :], zm_ref[16:24, :]
    for ref, out, b in ((yp_ref, op_ref, 2), (ym_ref, om_ref, 0)):
        for a in range(3):
            j = 3 * a + b
            for c in range(3):
                place = pl.ds((3 * a + c) * 8, 8)
                low = turn(zp, -j) if c == 2 else None
                high = turn(zm, LANES - 1 - j) if c == 0 else None
                out[place, :] = move_z(ref[place, :], c, low, high, lanes)


def face_x_kernel(xp_ref, xm_ref, zp_ref, zm_ref, yp_ref, ym_ref, op_ref, om_ref):
    lanes = lane_index(ROWS)
    rows = lax.broadcasted_iota(jnp.int32, (ROWS, LANES), 0)
    zp, zm = zp_ref[0:16, :], zm_ref[0:16, :]
    for ref, out, a, p in ((xp_ref, op_ref, 2, SLABS - 1), (xm_ref, om_ref, 0, 0)):
        for b in range(3):
            j = 3 * a + b
            for c in range(3):
                place = pl.ds((3 * b + c) * ROWS, ROWS)
                low = turn(zp, -(16 * p + j)) if c == 2 else None
                high = turn(zm, LANES - 1 - 16 * p - j) if c == 0 else None
                value = move_z(ref[place, :], c, low, high, lanes)
                spot = pl.ds((3 * a + c) * 8 + p, 1)
                ghost = yp_ref[spot, :] if b == 2 else ym_ref[spot, :]
                out[place, :] = move_y(value, b, ghost, rows)


def stream_kernel(source, zp_ref, zm_ref, yp_ref, ym_ref, out_ref):
    lanes = lane_index(ROWS)
    rows = lax.broadcasted_iota(jnp.int32, (ROWS, LANES), 0)

    def step(p, carry):
        for a in range(3):
            origin = p if a == 1 else (jnp.maximum(p - 1, 0) if a == 2 else jnp.minimum(p + 1, SLABS - 1))
            back = lax.rem(LANES - 16 * origin, LANES)
            zp = turn(zp_ref[0:16, :], back)
            zm = turn(zm_ref[0:16, :], back)
            for b in range(3):
                j = 3 * a + b
                for c in range(3):
                    i = 9 * a + 3 * b + c
                    value = source[pl.ds(pl.multiple_of(i * TILES + origin * ROWS, ROWS), ROWS), :]
                    low = turn(zp, -j) if c == 2 else None
                    high = turn(zm, LANES - 1 - j) if c == 0 else None
                    value = move_z(value, c, low, high, lanes)
                    spot = pl.ds((3 * a + c) * 8 + origin, 1)
                    ghost = yp_ref[spot, :] if b == 2 else ym_ref[spot, :]
                    value = move_y(value, b, ghost, rows)
                    out_ref[pl.ds(pl.multiple_of(i * TILES + p * ROWS, ROWS), ROWS), :] = value
        return carry

    lax.fori_loop(0, SLABS, step, 0)


def coarse_kernel(state_hbm, rates_hbm, *refs):
    outs = refs[:7]
    state, rates, chunks, semaphores = refs[7:]
    first = fetch(rates_hbm, rates, semaphores.at[0])

    def chunk(k):
        rows = pl.ds(pl.multiple_of(k * 32, 32), 32)
        return pltpu.make_async_copy(state_hbm.at[:, rows, :], state.at[:, rows, :], chunks.at[k])

    for k in range(4):
        chunk(k).start()
    first.wait()

    def ready(u):
        @pl.when(lax.rem(u, 4) == 0)
        def _():
            chunk(u // 4).wait()

    def load(i, u):
        return state[i, pl.ds(pl.multiple_of(u * 8, 8), 8), :]

    collide(load, None, rates, *outs, ready=ready)


def old_kernel(state_hbm, table_hbm, sent_ref, old_ref, table, tiles, semaphores):
    first = fetch(state_hbm.at[pl.ds(18 * TILES, 9 * TILES)], old_ref, semaphores.at[0])
    second = fetch(table_hbm, table, semaphores.at[1])
    first.wait()
    for k in range(9):
        tiles[pl.ds(k * WIDE, TILES), :] = old_ref[pl.ds(k * TILES, TILES), :]
    second.wait()
    pack(tiles, table, sent_ref)


def tile8(tiles, k, u):
    return tiles[pl.ds(pl.multiple_of(k * WIDE + u * 8, 8), 8), :]


def fine_first_kernel(state_hbm, flags_hbm, rates_hbm, table_hbm, received_ref, *refs):
    outs = refs[:7]
    state, flags, rates, table, tiles, chunks, semaphores = refs[7:]
    pieces = [
        fetch(
            state_hbm.at[pl.ds((18 + k) * TILES, TILES)], tiles.at[pl.ds(k * WIDE, TILES)], chunks.at[k]
        )
        for k in range(9)
    ]
    second = fetch(table_hbm, table, semaphores.at[0])
    others = [
        fetch(state_hbm.at[pl.ds(0, 18 * TILES)], state, semaphores.at[1]),
        fetch(flags_hbm, flags, semaphores.at[2]),
        fetch(rates_hbm, rates, semaphores.at[3]),
    ]
    for piece in pieces:
        piece.wait()
    second.wait()
    install(tiles, table, received_ref)
    for other in others:
        other.wait()

    def load(i, u):
        return tile8(tiles, i - 18, u) if i >= 18 else load8(state, i, u)

    collide(load, flags, rates, *outs)


def fine_second_kernel(state_ref, xp_ref, xm_ref, received_ref, flags_hbm, rates_hbm, table_hbm, *refs):
    outs = refs[:7]
    flags, rates, table, tiles, semaphores = refs[7:]
    first = fetch(table_hbm, table, semaphores.at[0])
    others = [fetch(flags_hbm, flags, semaphores.at[1]), fetch(rates_hbm, rates, semaphores.at[2])]
    fill(tiles, state_ref, 18, xp_ref, 0)
    first.wait()
    install(tiles, table, received_ref)
    for other in others:
        other.wait()

    def load(i, u):
        if i >= 18:
            return tile8(tiles, i - 18, u)
        value = load8(state_ref, i, u)
        if i < 9:
            ghost = xm_ref[pl.ds(pl.multiple_of(i * ROWS + lax.rem(u, 2) * 8, 8), 8), :]
            value = jnp.where(u >= 2 * SLABS - 2, ghost, value)
        return value

    collide(load, flags, rates, *outs)


def finish(state_ref, xp_ref, xm_ref, whole, out_hbm, semaphore):
    whole[...] = state_ref[...]
    for k in range(9):
        whole[pl.ds((18 + k) * TILES, ROWS), :] = xp_ref[pl.ds(k * ROWS, ROWS), :]
        whole[pl.ds(k * TILES + TILES - ROWS, ROWS), :] = xm_ref[pl.ds(k * ROWS, ROWS), :]
    return fetch(whole, out_hbm, semaphore)


def mean_kernel(state_ref, xp_ref, xm_ref, old_ref, table_hbm, sent_ref, kept_ref, out_hbm, *scratch):
    whole, table, tiles, semaphores = scratch
    first = fetch(table_hbm, table, semaphores.at[0])
    copy = finish(state_ref, xp_ref, xm_ref, whole, out_hbm, semaphores.at[1])
    kept_ref[...] = whole[pl.ds(0, 9 * TILES), :]
    for k in range(9):
        new = whole[pl.ds((18 + k) * TILES, TILES), :]
        tiles[pl.ds(k * WIDE, TILES), :] = 0.5 * (old_ref[pl.ds(k * TILES, TILES), :] + new)
    first.wait()
    pack(tiles, table, sent_ref)
    copy.wait()


def up_kernel(state_ref, xp_ref, xm_ref, table_hbm, sent_ref, out_hbm, *scratch):
    whole, table, tiles, semaphores = scratch
    first = fetch(table_hbm, table, semaphores.at[0])
    copy = finish(state_ref, xp_ref, xm_ref, whole, out_hbm, semaphores.at[1])
    fill(tiles, state_ref, 0, xm_ref, SLABS - 1)
    first.wait()
    pack(tiles, table, sent_ref)
    copy.wait()


def coarse_install_kernel(whole_hbm, kept_ref, received_ref, table_hbm, out_hbm, *scratch):
    table, tiles, semaphores, stores = scratch
    first = fetch(table_hbm, table, semaphores.at[0])
    for k in range(9):
        tiles[pl.ds(k * WIDE, TILES), :] = kept_ref[pl.ds(k * TILES, TILES), :]
    first.wait()
    install(tiles, table, received_ref)
    wait(
        [
            fetch(tiles.at[pl.ds(k * WIDE, TILES)], out_hbm.at[pl.ds(k * TILES, TILES)], stores.at[k])
            for k in range(9)
        ]
    )


STATE = (27 * TILES, LANES)
MESSAGE = (PEERS * CHUNK, LANES)
Z_FACE = (24, LANES)
Y_FACE = (9 * 8, LANES)
X_FACE = (9 * ROWS, LANES)
WIDE_TILES = (9 * WIDE, LANES)
NINE = (9 * TILES, LANES)
COLLIDED = (STATE, Z_FACE, Z_FACE, Y_FACE, Y_FACE, X_FACE, X_FACE)


def floats(*shape):
    return pltpu.VMEM(shape, jnp.float32)


def copies(count):
    return pltpu.SemaphoreType.DMA((count,))


FLAGS = pltpu.VMEM((TILES, LANES), jnp.int32)
RATES = pltpu.SMEM((27,), jnp.float32)
TABLE = pltpu.SMEM((2, PEERS), jnp.int32)


def run(kernel, name, spaces, shapes, *operands, scratch=(), alias=False, microseconds=1.0):
    spots = {"v": pltpu.VMEM, "h": pltpu.HBM}
    given, made = spaces.split(":")
    operands = [
        pltpu.with_memory_space_constraint(operand, pltpu.HBM) if space == "h" else operand
        for operand, space in zip(operands, given)
    ]
    return pl.pallas_call(
        kernel,
        name=name,
        out_shape=tuple(jax.ShapeDtypeStruct(shape, jnp.float32) for shape in shapes),
        in_specs=[pl.BlockSpec(memory_space=spots[space]) for space in given],
        out_specs=tuple(pl.BlockSpec(memory_space=spots[space]) for space in made),
        scratch_shapes=list(scratch),
        input_output_aliases={0: 0} if alias else {},
        compiler_params=pltpu.CompilerParams(vmem_limit_bytes=VMEM_BYTES),
        cost_estimate=pl.CostEstimate(
            flops=0, bytes_accessed=int(microseconds * 3.0e6), transcendentals=0
        ),
    )(*operands)


def swap(axis, plus, minus):
    count = lax.axis_size(axis)
    up = [(i, (i + 1) % count) for i in range(count)]
    down = [(i, (i - 1) % count) for i in range(count)]
    return lax.ppermute(plus, axis, up), lax.ppermute(minus, axis, down)


def halo(collided, zp, zm, yp, ym, xp, xm):
    zp, zm = swap("gz", zp, zm)
    yp, ym = run(face_y_kernel, "face_y", "vvvv:vv", (Y_FACE, Y_FACE), yp, ym, zp, zm)
    yp, ym = swap("gy", yp, ym)
    xp, xm = run(face_x_kernel, "face_x", "vvvvvv:vv", (X_FACE, X_FACE), xp, xm, zp, zm, yp, ym)
    xp, xm = swap("gx", xp, xm)
    (moved,) = run(
        stream_kernel, "stream", "vvvvv:v", (STATE,), collided, zp, zm, yp, ym, microseconds=2.0
    )
    return moved, xp, xm


def routed(message):
    chunks = message.reshape(PEERS, 9, 2, LANES)
    received = lax.all_to_all(chunks, ("gx", "gz"), split_axis=0, concat_axis=0, tiled=True)
    return received.reshape(MESSAGE)


def body(fine, coarse, fine_rates, coarse_rates, flags, down_source, down_target, up_source, up_target):
    fine = fine.reshape(STATE)
    coarse = coarse.reshape(STATE)
    flags = flags.reshape(TILES, LANES)
    down_source, down_target, up_source, up_target = (
        table.reshape(-1, 2).T for table in (down_source, down_target, up_source, up_target)
    )
    parts = run(
        coarse_kernel, "coarse_collide", "hh:vvvvvvv", COLLIDED,
        coarse.reshape(27, TILES, LANES), coarse_rates,
        scratch=(floats(27, TILES, LANES), RATES, copies(4), copies(1)),
        microseconds=3.0,
    )
    coarse, parts = lax.optimization_barrier((coarse, parts))
    sent_old, old = run(
        old_kernel, "pack_old", "hh:vv", (MESSAGE, NINE), coarse, down_source,
        scratch=(TABLE, floats(*WIDE_TILES), copies(2)),
        microseconds=OLD_COST,
    )
    received = routed(sent_old)
    moved, xp, xm = halo(*parts)
    sent_mean, kept, coarse_new = run(
        mean_kernel, "pack_mean", "vvvvh:vvh", (MESSAGE, NINE, STATE),
        moved, xp, xm, old, down_source,
        scratch=(floats(*STATE), TABLE, floats(*WIDE_TILES), copies(2)),
        microseconds=2.0,
    )
    mean = routed(sent_mean)
    parts = run(
        fine_first_kernel, "fine_first", "hhhhv:vvvvvvv", COLLIDED,
        fine, flags, fine_rates, down_target, received,
        scratch=(
            floats(18 * TILES, LANES), FLAGS, RATES, TABLE, floats(*WIDE_TILES), copies(9), copies(4)
        ),
        microseconds=4.0,
    )
    moved, xp, xm = halo(*parts)
    parts = run(
        fine_second_kernel, "fine_second", "vvvvhhh:vvvvvvv", COLLIDED,
        moved, xp, xm, mean, flags, fine_rates, down_target,
        scratch=(FLAGS, RATES, TABLE, floats(*WIDE_TILES), copies(3)),
        microseconds=4.0,
    )
    moved, xp, xm = halo(*parts)
    sent_up, fine_next = run(
        up_kernel, "pack_up", "vvvh:vh", (MESSAGE, STATE), moved, xp, xm, up_source,
        scratch=(floats(*STATE), TABLE, floats(*WIDE_TILES), copies(2)),
        microseconds=2.0,
    )
    up = routed(sent_up)
    (coarse_next,) = run(
        coarse_install_kernel, "coarse_install", "hvvh:h", (STATE,), coarse_new, kept, up, up_target,
        scratch=(TABLE, floats(*WIDE_TILES), copies(1), copies(9)),
        alias=True,
        microseconds=2.0,
    )
    block = (27, SLABS, ROWS, LANES)
    return fine_next.reshape(block), coarse_next.reshape(block)


def solution(mesh):
    placed = (
        P(None, "gx", "gy", "gz"),
        P(None, "gx", "gy", "gz"),
        P(),
        P(),
        P("gx", "gy", "gz"),
        P("gx", "gy", "gz", None, None),
        P("gx", "gy", "gz", None, None),
        P("gx", "gy", "gz", None, None),
        P("gx", "gy", "gz", None, None),
    )
    return jax.shard_map(
        body,
        mesh=mesh,
        in_specs=placed,
        out_specs=(P(None, "gx", "gy", "gz"), P(None, "gx", "gy", "gz")),
        check_vma=False,
    )
```

```python
import jax
import jax.numpy as jnp
from jax import lax
from jax.experimental import pallas as pl
from jax.experimental.pallas import tpu as pltpu
from jax.sharding import PartitionSpec as P

SLABS = 8
ROWS = 16
LANES = 128
TILES = SLABS * ROWS
CHUNK = 18
PEERS = 64
VMEM_BYTES = 10 * 1024 * 1024
WIDE = 136


def load8(ref, i, u):
    return ref[pl.ds(pl.multiple_of(i * TILES + u * 8, 8), 8), :]


def fetch(source, target, semaphore):
    copy = pltpu.make_async_copy(source, target, semaphore)
    copy.start()
    return copy


def wait(copies):
    for copy in copies:
        copy.wait()


def forward(values):
    for step in (9, 3, 1):
        out = list(values)
        for i in range(27):
            if (i // step) % 3 == 0:
                low, mid, high = values[i], values[i + step], values[i + 2 * step]
                even = high + low
                out[i] = even + 4.0 * mid
                out[i + step] = high - low
                out[i + 2 * step] = even
        values = out
    return values


def backward(values):
    for step in (9, 3, 1):
        out = list(values)
        for i in range(27):
            if (i // step) % 3 == 0:
                zero, one, two = values[i], values[i + step], values[i + 2 * step]
                out[i] = two - one
                out[i + step] = zero - two
                out[i + 2 * step] = two + one
        values = out
    return values


def equilibrium(moments):
    density = moments[0]
    momentum = (moments[9], moments[3], moments[1])
    squares = [part * part * (1.0 / 72.0) for part in momentum]
    scale = (1.0, 1.0 / 3.0, 1.0 / 9.0, 1.0 / 27.0)
    result = []
    for k in range(27):
        powers = (k // 9, (k // 3) % 3, k % 3)
        ones = [axis for axis in range(3) if powers[axis] == 1]
        twos = [axis for axis in range(3) if powers[axis] == 2]
        if len(ones) == 0:
            value = density
            for axis in twos:
                value = value + squares[axis]
        elif len(ones) == 1:
            value = momentum[ones[0]]
        elif len(ones) == 2:
            value = momentum[ones[0]] * momentum[ones[1]] * (1.0 / 216.0)
        else:
            value = jnp.zeros_like(density)
        if twos:
            value = value * scale[len(twos)]
        result.append(value)
    return result


def relax(values, rates_ref):
    moments = forward(values)
    target = equilibrium(moments)
    change = backward([(rates_ref[k] * 0.125) * (target[k] - moments[k]) for k in range(27)])
    result = []
    for i in range(27):
        rests = sum(1 for part in (i // 9, (i // 3) % 3, i % 3) if part == 1)
        moved = change[i] if rests == 0 else change[i] * (0.5**rests)
        result.append(values[i] + moved)
    return result


def lane_index(rows):
    return lax.broadcasted_iota(jnp.int32, (rows, LANES), 1)


def turn(value, amount):
    amount = amount % LANES if isinstance(amount, int) else amount
    if isinstance(amount, int) and amount == 0:
        return value
    return pltpu.roll(value, amount, 1)


def collide_at(load, flags_ref, rates_ref, store, u):
    values = [load(i, u) for i in range(27)]
    result = relax(values, rates_ref)
    if flags_ref is not None:
        solid = flags_ref[pl.ds(pl.multiple_of(u * 8, 8), 8), :] == 1
        result = [jnp.where(solid, values[26 - i], result[i]) for i in range(27)]
    for i in range(27):
        store(i, u, result[i])


def store8(ref):
    def store(i, u, value):
        ref[pl.ds(pl.multiple_of(i * TILES + u * 8, 8), 8), :] = value

    return store


def pack_z(out_ref, zp_ref, zm_ref, shifted):
    lanes = lane_index(8)
    for ref, c, edge in ((zp_ref, 2, LANES - 1), (zm_ref, 0, 0)):
        for half in range(2):
            packed = jnp.zeros((8, LANES), jnp.float32)
            for p in range(SLABS):
                for j in range(9):
                    source = p - (j // 3 - 1) if shifted else p
                    if 0 <= source < SLABS:
                        start = (3 * j + c) * TILES + source * ROWS + half * 8
                        column = turn(out_ref[start : start + 8, :], 16 * p + j - edge)
                        packed = jnp.where(lanes == 16 * p + j, column, packed)
            ref[half * 8 : half * 8 + 8, :] = packed


def pack_y(out_ref, zp_ref, zm_ref, yp_ref, ym_ref, shifted):
    lanes = lane_index(8)
    ends = [jnp.zeros((8, LANES), jnp.float32), None, jnp.zeros((8, LANES), jnp.float32)]
    for ref, b, q in ((yp_ref, 2, ROWS - 1), (ym_ref, 0, 0)):
        for a in range(3):
            for c in range(3):
                i = 9 * a + 3 * b + c
                rows = out_ref[pl.ds(i * TILES + q, 8, stride=ROWS), :]
                ref[pl.ds((3 * a + c) * 8, 8), :] = rows
                j = 3 * a + b
                if c != 1:
                    edge = LANES - 1 if c == 2 else 0
                    if shifted and a != 1:
                        rows = pltpu.roll(rows, 1 if a == 2 else 7, 0)
                    ends[c] = jnp.where(lanes == j, turn(rows, j - edge), ends[c])
    zp_ref[16:24, :] = ends[2]
    zm_ref[16:24, :] = ends[0]


def collide(load, flags_ref, rates_ref, out_ref, zp_ref, zm_ref, yp_ref, ym_ref, xp_ref, xm_ref):
    def step(u, carry):
        collide_at(load, flags_ref, rates_ref, store8(out_ref), u)
        return carry

    lax.fori_loop(0, 2 * SLABS, step, 0, unroll=2)
    pack_z(out_ref, zp_ref, zm_ref, False)
    pack_y(out_ref, zp_ref, zm_ref, yp_ref, ym_ref, False)
    for j in range(9):
        xp_ref[pl.ds(j * ROWS, ROWS), :] = out_ref[pl.ds((18 + j) * TILES + 7 * ROWS, ROWS), :]
        xm_ref[pl.ds(j * ROWS, ROWS), :] = out_ref[pl.ds(j * TILES, ROWS), :]


def collide_ends(load, flags_ref, rates_ref, ends_ref, xp_ref, xm_ref):
    def step(k, carry):
        def store(i, u, value):
            ends_ref[pl.ds(pl.multiple_of(i * 2 * ROWS + k * 8, 8), 8), :] = value

        collide_at(load, flags_ref, rates_ref, store, k + (2 * SLABS - 4) * (k // 2))
        return carry

    lax.fori_loop(0, 4, step, 0, unroll=2)
    for j in range(9):
        xp_ref[pl.ds(j * ROWS, ROWS), :] = ends_ref[pl.ds((18 + j) * 2 * ROWS + ROWS, ROWS), :]
        xm_ref[pl.ds(j * ROWS, ROWS), :] = ends_ref[pl.ds(j * 2 * ROWS, ROWS), :]


def collide_rest(load, flags_ref, rates_ref, ends_ref, out_ref, zp_ref, zm_ref, yp_ref, ym_ref):
    def step(u, carry):
        collide_at(load, flags_ref, rates_ref, store8(out_ref), u)
        return carry

    lax.fori_loop(2, 2 * SLABS - 2, step, 0, unroll=2)
    for i in range(27):
        out_ref[pl.ds(i * TILES, ROWS), :] = ends_ref[pl.ds(i * 2 * ROWS, ROWS), :]
        out_ref[pl.ds((i + 1) * TILES - ROWS, ROWS), :] = ends_ref[pl.ds(i * 2 * ROWS + ROWS, ROWS), :]
    pack_z(out_ref, zp_ref, zm_ref, True)
    pack_y(out_ref, zp_ref, zm_ref, yp_ref, ym_ref, True)


def face_z_kernel(zp_ref, zm_ref, xp_ref, xm_ref, op_ref, om_ref):
    lanes = lane_index(8)
    subs = lax.broadcasted_iota(jnp.int32, (8, LANES), 0)
    for ref, out, c, edge in ((zp_ref, op_ref, 2, LANES - 1), (zm_ref, om_ref, 0, 0)):
        parts = [ref[0:8, :], ref[8:16, :], ref[16:24, :]]
        for ghost, a, p in ((xp_ref, 2, 0), (xm_ref, 0, SLABS - 1)):
            for b in range(3):
                j = 3 * a + b
                first = (3 * b + c) * ROWS
                for half in range(2):
                    column = turn(ghost[first + half * 8 : first + half * 8 + 8, :], 16 * p + j - edge)
                    parts[half] = jnp.where(lanes == 16 * p + j, column, parts[half])
                if b != 1:
                    q = ROWS - 1 if b == 2 else 0
                    row = jnp.broadcast_to(ghost[first + q : first + q + 1, :], (8, LANES))
                    here = jnp.logical_and(lanes == j, subs == p)
                    parts[2] = jnp.where(here, turn(row, j - edge), parts[2])
        for k in range(3):
            out[k * 8 : k * 8 + 8, :] = parts[k]


def face_y_last_kernel(yp_ref, ym_ref, xp_ref, xm_ref, zp_ref, zm_ref, op_ref, om_ref):
    lanes = lane_index(8)
    subs = lax.broadcasted_iota(jnp.int32, (8, LANES), 0)
    zp, zm = zp_ref[16:24, :], zm_ref[16:24, :]
    for ref, out, b, q in ((yp_ref, op_ref, 2, ROWS - 1), (ym_ref, om_ref, 0, 0)):
        for a in range(3):
            j = 3 * a + b
            for c in range(3):
                place = pl.ds((3 * a + c) * 8, 8)
                value = ref[place, :]
                if a != 1:
                    ghost = xp_ref if a == 2 else xm_ref
                    spot = (3 * b + c) * ROWS + q
                    row = jnp.broadcast_to(ghost[spot : spot + 1, :], (8, LANES))
                    value = pltpu.roll(value, 1 if a == 2 else 7, 0)
                    value = jnp.where(subs == (0 if a == 2 else SLABS - 1), row, value)
                low = turn(zp, -j) if c == 2 else None
                high = turn(zm, LANES - 1 - j) if c == 0 else None
                out[place, :] = move_z(value, c, low, high, lanes)


def stream_first_kernel(source, xp_ref, xm_ref, zp_ref, zm_ref, out_ref):
    lanes = lane_index(ROWS)

    def step(p, carry):
        back = lax.rem(LANES - 16 * p, LANES)
        zp = turn(zp_ref[0:16, :], back)
        zm = turn(zm_ref[0:16, :], back)
        for a in range(3):
            origin = p if a == 1 else (jnp.maximum(p - 1, 0) if a == 2 else jnp.minimum(p + 1, SLABS - 1))
            for b in range(3):
                j = 3 * a + b
                for c in range(3):
                    i = 9 * a + 3 * b + c
                    value = source[pl.ds(pl.multiple_of(i * TILES + origin * ROWS, ROWS), ROWS), :]
                    place = pl.ds((3 * b + c) * ROWS, ROWS)
                    if a == 2:
                        value = jnp.where(p == 0, xp_ref[place, :], value)
                    if a == 0:
                        value = jnp.where(p == SLABS - 1, xm_ref[place, :], value)
                    low = turn(zp, -j) if c == 2 else None
                    high = turn(zm, LANES - 1 - j) if c == 0 else None
                    value = move_z(value, c, low, high, lanes)
                    if b != 1:
                        value = pltpu.roll(value, 1 if b == 2 else ROWS - 1, 0)
                    out_ref[pl.ds(pl.multiple_of(i * TILES + p * ROWS, ROWS), ROWS), :] = value
        return carry

    lax.fori_loop(0, SLABS, step, 0)


def fill(tiles, state_ref, first, ghost_ref=None, slab=None):
    for k in range(9):
        tiles[pl.ds(k * WIDE, TILES), :] = state_ref[pl.ds((first + k) * TILES, TILES), :]
        if ghost_ref is not None:
            tiles[pl.ds(k * WIDE + slab * ROWS, ROWS), :] = ghost_ref[pl.ds(k * ROWS, ROWS), :]


def pack(tiles, table_ref, sent):
    def step(r, carry):
        for j in range(2):
            tile = jnp.maximum(table_ref[j, r], 0)
            most = tiles[pl.ds(tile, 8, stride=WIDE), :]
            last = tiles[pl.ds(8 * WIDE + tile, 1), :]
            sent[pl.ds(r * CHUNK + j, 8, stride=2), :] = most
            sent[pl.ds(r * CHUNK + 16 + j, 1), :] = last
        return carry

    lax.fori_loop(0, PEERS, step, 0, unroll=4)


def install(tiles, table_ref, received_ref):
    def step(r, carry):
        moved = []
        for j in range(2):
            tile = table_ref[j, r]
            tile = jnp.where(tile < 0, TILES, tile)
            most = received_ref[pl.ds(r * CHUNK + j, 8, stride=2), :]
            last = received_ref[pl.ds(r * CHUNK + 16 + j, 1), :]
            moved.append((tile, most, last))
        for tile, most, last in moved:
            tiles[pl.ds(tile, 8, stride=WIDE), :] = most
            tiles[pl.ds(8 * WIDE + tile, 1), :] = last
        return carry

    lax.fori_loop(0, PEERS, step, 0, unroll=4)


def move_z(value, c, low_ghost, high_ghost, lanes):
    if c == 2:
        return jnp.where(lanes == 0, low_ghost, turn(value, 1))
    if c == 0:
        return jnp.where(lanes == LANES - 1, high_ghost, turn(value, LANES - 1))
    return value


def move_y(value, b, ghost, rows):
    if b == 2:
        return jnp.where(rows == 0, ghost, pltpu.roll(value, 1, 0))
    if b == 0:
        return jnp.where(rows == ROWS - 1, ghost, pltpu.roll(value, ROWS - 1, 0))
    return value


def face_y_kernel(yp_ref, ym_ref, zp_ref, zm_ref, op_ref, om_ref):
    lanes = lane_index(8)
    zp, zm = zp_ref[16:24, :], zm_ref[16:24, :]
    for ref, out, b in ((yp_ref, op_ref, 2), (ym_ref, om_ref, 0)):
        for a in range(3):
            j = 3 * a + b
            for c in range(3):
                place = pl.ds((3 * a + c) * 8, 8)
                low = turn(zp, -j) if c == 2 else None
                high = turn(zm, LANES - 1 - j) if c == 0 else None
                out[place, :] = move_z(ref[place, :], c, low, high, lanes)


def face_x_kernel(xp_ref, xm_ref, zp_ref, zm_ref, yp_ref, ym_ref, op_ref, om_ref):
    lanes = lane_index(ROWS)
    rows = lax.broadcasted_iota(jnp.int32, (ROWS, LANES), 0)
    zp, zm = zp_ref[0:16, :], zm_ref[0:16, :]
    for ref, out, a, p in ((xp_ref, op_ref, 2, SLABS - 1), (xm_ref, om_ref, 0, 0)):
        for b in range(3):
            j = 3 * a + b
            for c in range(3):
                place = pl.ds((3 * b + c) * ROWS, ROWS)
                low = turn(zp, -(16 * p + j)) if c == 2 else None
                high = turn(zm, LANES - 1 - 16 * p - j) if c == 0 else None
                value = move_z(ref[place, :], c, low, high, lanes)
                spot = pl.ds((3 * a + c) * 8 + p, 1)
                ghost = yp_ref[spot, :] if b == 2 else ym_ref[spot, :]
                out[place, :] = move_y(value, b, ghost, rows)


def stream_kernel(source, zp_ref, zm_ref, yp_ref, ym_ref, out_ref):
    lanes = lane_index(ROWS)
    rows = lax.broadcasted_iota(jnp.int32, (ROWS, LANES), 0)

    def step(p, carry):
        for a in range(3):
            origin = p if a == 1 else (jnp.maximum(p - 1, 0) if a == 2 else jnp.minimum(p + 1, SLABS - 1))
            back = lax.rem(LANES - 16 * origin, LANES)
            zp = turn(zp_ref[0:16, :], back)
            zm = turn(zm_ref[0:16, :], back)
            for b in range(3):
                j = 3 * a + b
                for c in range(3):
                    i = 9 * a + 3 * b + c
                    value = source[pl.ds(pl.multiple_of(i * TILES + origin * ROWS, ROWS), ROWS), :]
                    low = turn(zp, -j) if c == 2 else None
                    high = turn(zm, LANES - 1 - j) if c == 0 else None
                    value = move_z(value, c, low, high, lanes)
                    spot = pl.ds((3 * a + c) * 8 + origin, 1)
                    ghost = yp_ref[spot, :] if b == 2 else ym_ref[spot, :]
                    value = move_y(value, b, ghost, rows)
                    out_ref[pl.ds(pl.multiple_of(i * TILES + p * ROWS, ROWS), ROWS), :] = value
        return carry

    lax.fori_loop(0, SLABS, step, 0)


def coarse_ends_kernel(state_hbm, rates_hbm, *refs):
    outs = refs[:3]
    state, rates, semaphores = refs[3:]
    pieces = [
        fetch(state_hbm.at[:, pl.ds(0, ROWS), :], state.at[:, pl.ds(0, ROWS), :], semaphores.at[0]),
        fetch(
            state_hbm.at[:, pl.ds(TILES - ROWS, ROWS), :], state.at[:, pl.ds(ROWS, ROWS), :], semaphores.at[1]
        ),
        fetch(rates_hbm, rates, semaphores.at[2]),
    ]
    wait(pieces)

    def load(i, u):
        return state[i, pl.ds(pl.multiple_of(lax.rem(u, 4) * 8, 8), 8), :]

    collide_ends(load, None, rates, *outs)


def coarse_rest_kernel(state_hbm, rates_hbm, ends_ref, *refs):
    outs = refs[:5]
    state, rates, semaphores = refs[5:]
    middle = pl.ds(ROWS, TILES - 2 * ROWS)
    pieces = [
        fetch(state_hbm.at[:, middle, :], state, semaphores.at[0]),
        fetch(rates_hbm, rates, semaphores.at[1]),
    ]
    wait(pieces)

    def load(i, u):
        return state[i, pl.ds(pl.multiple_of((u - 2) * 8, 8), 8), :]

    collide_rest(load, None, rates, ends_ref, *outs)


def old_kernel(state_hbm, table_hbm, sent_ref, old_ref, table, tiles, semaphores):
    first = fetch(state_hbm.at[pl.ds(18 * TILES, 9 * TILES)], old_ref, semaphores.at[0])
    second = fetch(table_hbm, table, semaphores.at[1])
    first.wait()
    for k in range(9):
        tiles[pl.ds(k * WIDE, TILES), :] = old_ref[pl.ds(k * TILES, TILES), :]
    second.wait()
    pack(tiles, table, sent_ref)


def tile8(tiles, k, u):
    return tiles[pl.ds(pl.multiple_of(k * WIDE + u * 8, 8), 8), :]


def fine_first_kernel(state_hbm, flags_hbm, rates_hbm, table_hbm, received_ref, *refs):
    outs = refs[:7]
    state, flags, rates, table, tiles, chunks, semaphores = refs[7:]
    pieces = [
        fetch(
            state_hbm.at[pl.ds((18 + k) * TILES, TILES)], tiles.at[pl.ds(k * WIDE, TILES)], chunks.at[k]
        )
        for k in range(9)
    ]
    second = fetch(table_hbm, table, semaphores.at[0])
    others = [
        fetch(state_hbm.at[pl.ds(0, 18 * TILES)], state, semaphores.at[1]),
        fetch(flags_hbm, flags, semaphores.at[2]),
        fetch(rates_hbm, rates, semaphores.at[3]),
    ]
    for piece in pieces:
        piece.wait()
    second.wait()
    install(tiles, table, received_ref)
    for other in others:
        other.wait()

    def load(i, u):
        return tile8(tiles, i - 18, u) if i >= 18 else load8(state, i, u)

    collide(load, flags, rates, *outs)


def fine_ends_kernel(state_ref, xp_ref, xm_ref, received_ref, flags_hbm, rates_hbm, table_hbm, *refs):
    tiles, outs = refs[0], refs[1:4]
    flags, rates, table, semaphores = refs[4:]
    first = fetch(table_hbm, table, semaphores.at[0])
    others = [fetch(flags_hbm, flags, semaphores.at[1]), fetch(rates_hbm, rates, semaphores.at[2])]
    fill(tiles, state_ref, 18, xp_ref, 0)
    first.wait()
    install(tiles, table, received_ref)
    wait(others)

    def load(i, u):
        if i >= 18:
            return tile8(tiles, i - 18, u)
        value = load8(state_ref, i, u)
        if i < 9:
            ghost = xm_ref[pl.ds(pl.multiple_of(i * ROWS + lax.rem(u, 2) * 8, 8), 8), :]
            value = jnp.where(u >= 2 * SLABS - 2, ghost, value)
        return value

    collide_ends(load, flags, rates, *outs)


def fine_rest_kernel(state_ref, tiles_ref, flags_hbm, rates_hbm, ends_ref, *refs):
    outs = refs[:5]
    flags, rates, semaphores = refs[5:]
    wait([fetch(flags_hbm, flags, semaphores.at[0]), fetch(rates_hbm, rates, semaphores.at[1])])

    def load(i, u):
        return tile8(tiles_ref, i - 18, u) if i >= 18 else load8(state_ref, i, u)

    collide_rest(load, flags, rates, ends_ref, *outs)


def finish(state_ref, yp_ref, ym_ref, whole, out_hbm, semaphore):
    whole[...] = state_ref[...]
    for i in range(27):
        a, b, c = i // 9, (i // 3) % 3, i % 3
        if b != 1:
            ghost, q = (yp_ref, 0) if b == 2 else (ym_ref, ROWS - 1)
            whole[pl.ds(i * TILES + q, 8, stride=ROWS), :] = ghost[pl.ds((3 * a + c) * 8, 8), :]
    return fetch(whole, out_hbm, semaphore)


def mean_kernel(state_ref, yp_ref, ym_ref, old_ref, table_hbm, sent_ref, kept_ref, out_hbm, *scratch):
    whole, table, tiles, semaphores = scratch
    first = fetch(table_hbm, table, semaphores.at[0])
    copy = finish(state_ref, yp_ref, ym_ref, whole, out_hbm, semaphores.at[1])
    kept_ref[...] = whole[pl.ds(0, 9 * TILES), :]
    for k in range(9):
        new = whole[pl.ds((18 + k) * TILES, TILES), :]
        tiles[pl.ds(k * WIDE, TILES), :] = 0.5 * (old_ref[pl.ds(k * TILES, TILES), :] + new)
    first.wait()
    pack(tiles, table, sent_ref)
    copy.wait()


def up_kernel(state_ref, yp_ref, ym_ref, table_hbm, sent_ref, out_hbm, *scratch):
    whole, table, tiles, semaphores = scratch
    first = fetch(table_hbm, table, semaphores.at[0])
    copy = finish(state_ref, yp_ref, ym_ref, whole, out_hbm, semaphores.at[1])
    fill(tiles, whole, 0)
    first.wait()
    pack(tiles, table, sent_ref)
    copy.wait()


def coarse_install_kernel(whole_hbm, kept_ref, received_ref, table_hbm, out_hbm, *scratch):
    table, tiles, semaphores, stores = scratch
    first = fetch(table_hbm, table, semaphores.at[0])
    for k in range(9):
        tiles[pl.ds(k * WIDE, TILES), :] = kept_ref[pl.ds(k * TILES, TILES), :]
    first.wait()
    install(tiles, table, received_ref)
    wait(
        [
            fetch(tiles.at[pl.ds(k * WIDE, TILES)], out_hbm.at[pl.ds(k * TILES, TILES)], stores.at[k])
            for k in range(9)
        ]
    )


STATE = (27 * TILES, LANES)
MESSAGE = (PEERS * CHUNK, LANES)
Z_FACE = (24, LANES)
Y_FACE = (9 * 8, LANES)
X_FACE = (9 * ROWS, LANES)
WIDE_TILES = (9 * WIDE, LANES)
NINE = (9 * TILES, LANES)
ENDS = (27 * 2 * ROWS, LANES)
REST = (STATE, Z_FACE, Z_FACE, Y_FACE, Y_FACE)
COLLIDED = (STATE, Z_FACE, Z_FACE, Y_FACE, Y_FACE, X_FACE, X_FACE)


def floats(*shape):
    return pltpu.VMEM(shape, jnp.float32)


def copies(count):
    return pltpu.SemaphoreType.DMA((count,))


FLAGS = pltpu.VMEM((TILES, LANES), jnp.int32)
RATES = pltpu.SMEM((27,), jnp.float32)
TABLE = pltpu.SMEM((2, PEERS), jnp.int32)


def run(kernel, name, spaces, shapes, *operands, scratch=(), alias=False, microseconds=1.0):
    spots = {"v": pltpu.VMEM, "h": pltpu.HBM}
    given, made = spaces.split(":")
    operands = [
        pltpu.with_memory_space_constraint(operand, pltpu.HBM) if space == "h" else operand
        for operand, space in zip(operands, given)
    ]
    return pl.pallas_call(
        kernel,
        name=name,
        out_shape=tuple(jax.ShapeDtypeStruct(shape, jnp.float32) for shape in shapes),
        in_specs=[pl.BlockSpec(memory_space=spots[space]) for space in given],
        out_specs=tuple(pl.BlockSpec(memory_space=spots[space]) for space in made),
        scratch_shapes=list(scratch),
        input_output_aliases={0: 0} if alias else {},
        compiler_params=pltpu.CompilerParams(vmem_limit_bytes=VMEM_BYTES),
        cost_estimate=pl.CostEstimate(
            flops=0, bytes_accessed=int(microseconds * 3.0e6), transcendentals=0
        ),
    )(*operands)


def swap(axis, plus, minus):
    count = lax.axis_size(axis)
    up = [(i, (i + 1) % count) for i in range(count)]
    down = [(i, (i - 1) % count) for i in range(count)]
    return lax.ppermute(plus, axis, up), lax.ppermute(minus, axis, down)


def halo(collided, zp, zm, yp, ym, xp, xm):
    zp, zm = swap("gz", zp, zm)
    yp, ym = run(face_y_kernel, "face_y", "vvvv:vv", (Y_FACE, Y_FACE), yp, ym, zp, zm)
    yp, ym = swap("gy", yp, ym)
    xp, xm = run(face_x_kernel, "face_x", "vvvvvv:vv", (X_FACE, X_FACE), xp, xm, zp, zm, yp, ym)
    xp, xm = swap("gx", xp, xm)
    (moved,) = run(
        stream_kernel, "stream", "vvvvv:v", (STATE,), collided, zp, zm, yp, ym, microseconds=2.0
    )
    return moved, xp, xm


def halo_x_first(xp, xm, rest):
    xp, xm = swap("gx", xp, xm)
    collided, zp, zm, yp, ym = rest()
    zp, zm = run(face_z_kernel, "face_z", "vvvv:vv", (Z_FACE, Z_FACE), zp, zm, xp, xm)
    zp, zm = swap("gz", zp, zm)
    yp, ym = run(face_y_last_kernel, "face_y", "vvvvvv:vv", (Y_FACE, Y_FACE), yp, ym, xp, xm, zp, zm)
    return yp, ym, (collided, xp, xm, zp, zm)


def stream_first(operands):
    return run(stream_first_kernel, "stream", "vvvvv:v", (STATE,), *operands, microseconds=2.0)[0]


def routed(message):
    chunks = message.reshape(PEERS, 9, 2, LANES)
    received = lax.all_to_all(chunks, ("gx", "gz"), split_axis=0, concat_axis=0, tiled=True)
    return received.reshape(MESSAGE)


def body(fine, coarse, fine_rates, coarse_rates, flags, down_source, down_target, up_source, up_target):
    fine = fine.reshape(STATE)
    coarse = coarse.reshape(STATE)
    flags = flags.reshape(TILES, LANES)
    down_source, down_target, up_source, up_target = (
        table.reshape(-1, 2).T for table in (down_source, down_target, up_source, up_target)
    )
    cube = coarse.reshape(27, TILES, LANES)
    ends, xp, xm = run(
        coarse_ends_kernel, "coarse_ends", "hh:vvv", (ENDS, X_FACE, X_FACE), cube, coarse_rates,
        scratch=(floats(27, 2 * ROWS, LANES), RATES, copies(3)),
        microseconds=2.0,
    )

    def coarse_rest():
        return run(
            coarse_rest_kernel, "coarse_rest", "hhv:vvvvv", REST, cube, coarse_rates, ends,
            scratch=(floats(27, TILES - 2 * ROWS, LANES), RATES, copies(2)),
            microseconds=3.0,
        )

    yp, ym, whole = halo_x_first(xp, xm, coarse_rest)
    sent_old, old = run(
        old_kernel, "pack_old", "hh:vv", (MESSAGE, NINE), coarse, down_source,
        scratch=(TABLE, floats(*WIDE_TILES), copies(2)),
        microseconds=2.0,
    )
    sent_old, yp, ym = lax.optimization_barrier((sent_old, yp, ym))
    received = routed(sent_old)
    yp, ym = swap("gy", yp, ym)
    moved = stream_first(whole)
    sent_mean, kept, coarse_new = run(
        mean_kernel, "pack_mean", "vvvvh:vvh", (MESSAGE, NINE, STATE),
        moved, yp, ym, old, down_source,
        scratch=(floats(*STATE), TABLE, floats(*WIDE_TILES), copies(2)),
        microseconds=2.0,
    )
    mean = routed(sent_mean)
    parts = run(
        fine_first_kernel, "fine_first", "hhhhv:vvvvvvv", COLLIDED,
        fine, flags, fine_rates, down_target, received,
        scratch=(
            floats(18 * TILES, LANES), FLAGS, RATES, TABLE, floats(*WIDE_TILES), copies(9), copies(4)
        ),
        microseconds=4.0,
    )
    moved, xp, xm = halo(*parts)
    tiles, ends, face_xp, face_xm = run(
        fine_ends_kernel, "fine_ends", "vvvvhhh:vvvv", (WIDE_TILES, ENDS, X_FACE, X_FACE),
        moved, xp, xm, mean, flags, fine_rates, down_target,
        scratch=(FLAGS, RATES, TABLE, copies(3)),
        microseconds=3.0,
    )

    def fine_rest():
        return run(
            fine_rest_kernel, "fine_rest", "vvhhv:vvvvv", REST, moved, tiles, flags, fine_rates, ends,
            scratch=(FLAGS, RATES, copies(2)),
            microseconds=3.0,
        )

    yp, ym, whole = halo_x_first(face_xp, face_xm, fine_rest)
    yp, ym = swap("gy", yp, ym)
    sent_up, fine_next = run(
        up_kernel, "pack_up", "vvvh:vh", (MESSAGE, STATE), stream_first(whole), yp, ym, up_source,
        scratch=(floats(*STATE), TABLE, floats(*WIDE_TILES), copies(2)),
        microseconds=2.0,
    )
    up = routed(sent_up)
    (coarse_next,) = run(
        coarse_install_kernel, "coarse_install", "hvvh:h", (STATE,), coarse_new, kept, up, up_target,
        scratch=(TABLE, floats(*WIDE_TILES), copies(1), copies(9)),
        alias=True,
        microseconds=2.0,
    )
    block = (27, SLABS, ROWS, LANES)
    return fine_next.reshape(block), coarse_next.reshape(block)


def solution(mesh):
    placed = (
        P(None, "gx", "gy", "gz"),
        P(None, "gx", "gy", "gz"),
        P(),
        P(),
        P("gx", "gy", "gz"),
        P("gx", "gy", "gz", None, None),
        P("gx", "gy", "gz", None, None),
        P("gx", "gy", "gz", None, None),
        P("gx", "gy", "gz", None, None),
    )
    return jax.shard_map(
        body,
        mesh=mesh,
        in_specs=placed,
        out_specs=(P(None, "gx", "gy", "gz"), P(None, "gx", "gy", "gz")),
        check_vma=False,
    )
```

```python
import jax
import jax.numpy as jnp
from jax import lax
from jax.experimental import pallas as pl
from jax.experimental.pallas import tpu as pltpu
from jax.sharding import PartitionSpec as P

SLABS = 8
ROWS = 16
LANES = 128
TILES = SLABS * ROWS
CHUNK = 18
PEERS = 64
VMEM_BYTES = 10 * 1024 * 1024
WIDE = 136


def load8(ref, i, u):
    return ref[pl.ds(pl.multiple_of(i * TILES + u * 8, 8), 8), :]


def fetch(source, target, semaphore):
    copy = pltpu.make_async_copy(source, target, semaphore)
    copy.start()
    return copy


def wait(copies):
    for copy in copies:
        copy.wait()


def forward(values):
    for step in (9, 3, 1):
        out = list(values)
        for i in range(27):
            if (i // step) % 3 == 0:
                low, mid, high = values[i], values[i + step], values[i + 2 * step]
                even = high + low
                out[i] = even + 4.0 * mid
                out[i + step] = high - low
                out[i + 2 * step] = even
        values = out
    return values


def backward(values):
    for step in (9, 3, 1):
        out = list(values)
        for i in range(27):
            if (i // step) % 3 == 0:
                zero, one, two = values[i], values[i + step], values[i + 2 * step]
                out[i] = two - one
                out[i + step] = zero - two
                out[i + 2 * step] = two + one
        values = out
    return values


def equilibrium(moments):
    density = moments[0]
    momentum = (moments[9], moments[3], moments[1])
    squares = [part * part * (1.0 / 72.0) for part in momentum]
    scale = (1.0, 1.0 / 3.0, 1.0 / 9.0, 1.0 / 27.0)
    result = []
    for k in range(27):
        powers = (k // 9, (k // 3) % 3, k % 3)
        ones = [axis for axis in range(3) if powers[axis] == 1]
        twos = [axis for axis in range(3) if powers[axis] == 2]
        if len(ones) == 0:
            value = density
            for axis in twos:
                value = value + squares[axis]
        elif len(ones) == 1:
            value = momentum[ones[0]]
        elif len(ones) == 2:
            value = momentum[ones[0]] * momentum[ones[1]] * (1.0 / 216.0)
        else:
            value = jnp.zeros_like(density)
        if twos:
            value = value * scale[len(twos)]
        result.append(value)
    return result


def relax(values, rates_ref):
    moments = forward(values)
    target = equilibrium(moments)
    change = backward([(rates_ref[k] * 0.125) * (target[k] - moments[k]) for k in range(27)])
    result = []
    for i in range(27):
        rests = sum(1 for part in (i // 9, (i // 3) % 3, i % 3) if part == 1)
        moved = change[i] if rests == 0 else change[i] * (0.5**rests)
        result.append(values[i] + moved)
    return result


def lane_index(rows):
    return lax.broadcasted_iota(jnp.int32, (rows, LANES), 1)


def turn(value, amount):
    amount = amount % LANES if isinstance(amount, int) else amount
    if isinstance(amount, int) and amount == 0:
        return value
    return pltpu.roll(value, amount, 1)


def collide_at(load, flags_ref, rates_ref, store, u):
    values = [load(i, u) for i in range(27)]
    result = relax(values, rates_ref)
    if flags_ref is not None:
        solid = flags_ref[pl.ds(pl.multiple_of(u * 8, 8), 8), :] == 1
        result = [jnp.where(solid, values[26 - i], result[i]) for i in range(27)]
    for i in range(27):
        store(i, u, result[i])


def store8(ref):
    def store(i, u, value):
        ref[pl.ds(pl.multiple_of(i * TILES + u * 8, 8), 8), :] = value

    return store


def pack_z(out_ref, zp_ref, zm_ref, shifted):
    lanes = lane_index(8)
    for ref, c, edge in ((zp_ref, 2, LANES - 1), (zm_ref, 0, 0)):
        for half in range(2):
            packed = jnp.zeros((8, LANES), jnp.float32)
            for p in range(SLABS):
                for j in range(9):
                    source = p - (j // 3 - 1) if shifted else p
                    if 0 <= source < SLABS:
                        start = (3 * j + c) * TILES + source * ROWS + half * 8
                        column = turn(out_ref[start : start + 8, :], 16 * p + j - edge)
                        packed = jnp.where(lanes == 16 * p + j, column, packed)
            ref[half * 8 : half * 8 + 8, :] = packed


def pack_y(out_ref, zp_ref, zm_ref, yp_ref, ym_ref, shifted):
    lanes = lane_index(8)
    ends = [jnp.zeros((8, LANES), jnp.float32), None, jnp.zeros((8, LANES), jnp.float32)]
    for ref, b, q in ((yp_ref, 2, ROWS - 1), (ym_ref, 0, 0)):
        for a in range(3):
            for c in range(3):
                i = 9 * a + 3 * b + c
                rows = out_ref[pl.ds(i * TILES + q, 8, stride=ROWS), :]
                ref[pl.ds((3 * a + c) * 8, 8), :] = rows
                j = 3 * a + b
                if c != 1:
                    edge = LANES - 1 if c == 2 else 0
                    if shifted and a != 1:
                        rows = pltpu.roll(rows, 1 if a == 2 else 7, 0)
                    ends[c] = jnp.where(lanes == j, turn(rows, j - edge), ends[c])
    zp_ref[16:24, :] = ends[2]
    zm_ref[16:24, :] = ends[0]


def collide(load, flags_ref, rates_ref, out_ref, zp_ref, zm_ref, yp_ref, ym_ref, xp_ref, xm_ref):
    def step(u, carry):
        collide_at(load, flags_ref, rates_ref, store8(out_ref), u)
        return carry

    lax.fori_loop(0, 2 * SLABS, step, 0, unroll=2)
    pack_z(out_ref, zp_ref, zm_ref, False)
    pack_y(out_ref, zp_ref, zm_ref, yp_ref, ym_ref, False)
    for j in range(9):
        xp_ref[pl.ds(j * ROWS, ROWS), :] = out_ref[pl.ds((18 + j) * TILES + 7 * ROWS, ROWS), :]
        xm_ref[pl.ds(j * ROWS, ROWS), :] = out_ref[pl.ds(j * TILES, ROWS), :]


def collide_ends(load, flags_ref, rates_ref, ends_ref, xp_ref, xm_ref):
    def step(k, carry):
        def store(i, u, value):
            ends_ref[pl.ds(pl.multiple_of(i * 2 * ROWS + k * 8, 8), 8), :] = value

        collide_at(load, flags_ref, rates_ref, store, k + (2 * SLABS - 4) * (k // 2))
        return carry

    lax.fori_loop(0, 4, step, 0, unroll=2)
    for j in range(9):
        xp_ref[pl.ds(j * ROWS, ROWS), :] = ends_ref[pl.ds((18 + j) * 2 * ROWS + ROWS, ROWS), :]
        xm_ref[pl.ds(j * ROWS, ROWS), :] = ends_ref[pl.ds(j * 2 * ROWS, ROWS), :]


def collide_rest(load, flags_ref, rates_ref, ends_ref, out_ref, zp_ref, zm_ref, yp_ref, ym_ref):
    def step(u, carry):
        collide_at(load, flags_ref, rates_ref, store8(out_ref), u)
        return carry

    lax.fori_loop(2, 2 * SLABS - 2, step, 0, unroll=2)
    for i in range(27):
        out_ref[pl.ds(i * TILES, ROWS), :] = ends_ref[pl.ds(i * 2 * ROWS, ROWS), :]
        out_ref[pl.ds((i + 1) * TILES - ROWS, ROWS), :] = ends_ref[pl.ds(i * 2 * ROWS + ROWS, ROWS), :]
    pack_z(out_ref, zp_ref, zm_ref, True)
    pack_y(out_ref, zp_ref, zm_ref, yp_ref, ym_ref, True)


def face_z_kernel(zp_ref, zm_ref, xp_ref, xm_ref, op_ref, om_ref):
    lanes = lane_index(8)
    subs = lax.broadcasted_iota(jnp.int32, (8, LANES), 0)
    for ref, out, c, edge in ((zp_ref, op_ref, 2, LANES - 1), (zm_ref, om_ref, 0, 0)):
        parts = [ref[0:8, :], ref[8:16, :], ref[16:24, :]]
        for ghost, a, p in ((xp_ref, 2, 0), (xm_ref, 0, SLABS - 1)):
            for b in range(3):
                j = 3 * a + b
                first = (3 * b + c) * ROWS
                for half in range(2):
                    column = turn(ghost[first + half * 8 : first + half * 8 + 8, :], 16 * p + j - edge)
                    parts[half] = jnp.where(lanes == 16 * p + j, column, parts[half])
                if b != 1:
                    q = ROWS - 1 if b == 2 else 0
                    row = jnp.broadcast_to(ghost[first + q : first + q + 1, :], (8, LANES))
                    here = jnp.logical_and(lanes == j, subs == p)
                    parts[2] = jnp.where(here, turn(row, j - edge), parts[2])
        for k in range(3):
            out[k * 8 : k * 8 + 8, :] = parts[k]


def move_x_kernel(state_ref, zp_ref, zm_ref, xp_ref, xm_ref, op_ref, om_ref, out_ref):
    face_z_kernel(zp_ref, zm_ref, xp_ref, xm_ref, op_ref, om_ref)
    long = TILES - ROWS
    for k in range(9):
        for a, ghost, at, to, start in ((2, xp_ref, 0, ROWS, 0), (0, xm_ref, long, 0, ROWS)):
            first = (9 * a + k) * TILES
            out_ref[pl.ds(first + to, long), :] = state_ref[pl.ds(first + start, long), :]
            out_ref[pl.ds(first + at, ROWS), :] = ghost[pl.ds(k * ROWS, ROWS), :]
    middle = pl.ds(9 * TILES, 9 * TILES)
    out_ref[middle, :] = state_ref[middle, :]


def face_y_moved_kernel(state_ref, zp_ref, zm_ref, op_ref, om_ref):
    lanes = lane_index(8)
    zp, zm = zp_ref[16:24, :], zm_ref[16:24, :]
    for out, b, q in ((op_ref, 2, ROWS - 1), (om_ref, 0, 0)):
        for a in range(3):
            j = 3 * a + b
            for c in range(3):
                value = state_ref[pl.ds((9 * a + 3 * b + c) * TILES + q, 8, stride=ROWS), :]
                low = turn(zp, -j) if c == 2 else None
                high = turn(zm, LANES - 1 - j) if c == 0 else None
                out[pl.ds((3 * a + c) * 8, 8), :] = move_z(value, c, low, high, lanes)


def face_y_last_kernel(yp_ref, ym_ref, xp_ref, xm_ref, zp_ref, zm_ref, op_ref, om_ref):
    lanes = lane_index(8)
    subs = lax.broadcasted_iota(jnp.int32, (8, LANES), 0)
    zp, zm = zp_ref[16:24, :], zm_ref[16:24, :]
    for ref, out, b, q in ((yp_ref, op_ref, 2, ROWS - 1), (ym_ref, om_ref, 0, 0)):
        for a in range(3):
            j = 3 * a + b
            for c in range(3):
                place = pl.ds((3 * a + c) * 8, 8)
                value = ref[place, :]
                if a != 1:
                    ghost = xp_ref if a == 2 else xm_ref
                    spot = (3 * b + c) * ROWS + q
                    row = jnp.broadcast_to(ghost[spot : spot + 1, :], (8, LANES))
                    value = pltpu.roll(value, 1 if a == 2 else 7, 0)
                    value = jnp.where(subs == (0 if a == 2 else SLABS - 1), row, value)
                low = turn(zp, -j) if c == 2 else None
                high = turn(zm, LANES - 1 - j) if c == 0 else None
                out[place, :] = move_z(value, c, low, high, lanes)


def stream_moved_kernel(source, zp_ref, zm_ref, out_ref):
    stream_first_kernel(source, None, None, zp_ref, zm_ref, out_ref)


def stream_first_kernel(source, xp_ref, xm_ref, zp_ref, zm_ref, out_ref):
    lanes = lane_index(ROWS)

    def step(p, carry):
        back = lax.rem(LANES - 16 * p, LANES)
        zp = turn(zp_ref[0:16, :], back)
        zm = turn(zm_ref[0:16, :], back)
        for a in range(3):
            origin = jnp.maximum(p - 1, 0) if a == 2 else jnp.minimum(p + 1, SLABS - 1)
            if a == 1 or xp_ref is None:
                origin = p
            for b in range(3):
                j = 3 * a + b
                for c in range(3):
                    i = 9 * a + 3 * b + c
                    value = source[pl.ds(pl.multiple_of(i * TILES + origin * ROWS, ROWS), ROWS), :]
                    place = pl.ds((3 * b + c) * ROWS, ROWS)
                    if a == 2 and xp_ref is not None:
                        value = jnp.where(p == 0, xp_ref[place, :], value)
                    if a == 0 and xm_ref is not None:
                        value = jnp.where(p == SLABS - 1, xm_ref[place, :], value)
                    low = turn(zp, -j) if c == 2 else None
                    high = turn(zm, LANES - 1 - j) if c == 0 else None
                    value = move_z(value, c, low, high, lanes)
                    if b != 1:
                        value = pltpu.roll(value, 1 if b == 2 else ROWS - 1, 0)
                    out_ref[pl.ds(pl.multiple_of(i * TILES + p * ROWS, ROWS), ROWS), :] = value
        return carry

    lax.fori_loop(0, SLABS, step, 0)


def fill(tiles, state_ref, first, ghost_ref=None, slab=None):
    for k in range(9):
        tiles[pl.ds(k * WIDE, TILES), :] = state_ref[pl.ds((first + k) * TILES, TILES), :]
        if ghost_ref is not None:
            tiles[pl.ds(k * WIDE + slab * ROWS, ROWS), :] = ghost_ref[pl.ds(k * ROWS, ROWS), :]


def pack(tiles, table_ref, sent, first=0, last=None):
    def step(r, carry):
        for j in range(2):
            tile = jnp.maximum(table_ref[j, r], 0)
            most = tiles[pl.ds(tile, 8, stride=WIDE), :]
            last = tiles[pl.ds(8 * WIDE + tile, 1), :]
            sent[pl.ds(r * CHUNK + j, 8, stride=2), :] = most
            sent[pl.ds(r * CHUNK + 16 + j, 1), :] = last
        return carry

    lax.fori_loop(first, PEERS if last is None else last, step, 0, unroll=4)


def pack_halves(tiles, table_ref, sent, sent_hbm, *semaphores):
    middle = PEERS // 2
    copies = []
    for (first, last), semaphore in zip(((0, middle), (middle, PEERS)), semaphores):
        pack(tiles, table_ref, sent, first, last)
        rows = pl.ds(first * CHUNK, (last - first) * CHUNK)
        copies.append(fetch(sent.at[rows], sent_hbm.at[rows], semaphore))
    return copies


def install(tiles, table_ref, received_ref):
    def step(r, carry):
        moved = []
        for j in range(2):
            tile = table_ref[j, r]
            tile = jnp.where(tile < 0, TILES, tile)
            most = received_ref[pl.ds(r * CHUNK + j, 8, stride=2), :]
            last = received_ref[pl.ds(r * CHUNK + 16 + j, 1), :]
            moved.append((tile, most, last))
        for tile, most, last in moved:
            tiles[pl.ds(tile, 8, stride=WIDE), :] = most
            tiles[pl.ds(8 * WIDE + tile, 1), :] = last
        return carry

    lax.fori_loop(0, PEERS, step, 0, unroll=4)


def move_z(value, c, low_ghost, high_ghost, lanes):
    if c == 2:
        return jnp.where(lanes == 0, low_ghost, turn(value, 1))
    if c == 0:
        return jnp.where(lanes == LANES - 1, high_ghost, turn(value, LANES - 1))
    return value


def move_y(value, b, ghost, rows):
    if b == 2:
        return jnp.where(rows == 0, ghost, pltpu.roll(value, 1, 0))
    if b == 0:
        return jnp.where(rows == ROWS - 1, ghost, pltpu.roll(value, ROWS - 1, 0))
    return value


def face_y_kernel(yp_ref, ym_ref, zp_ref, zm_ref, op_ref, om_ref):
    lanes = lane_index(8)
    zp, zm = zp_ref[16:24, :], zm_ref[16:24, :]
    for ref, out, b in ((yp_ref, op_ref, 2), (ym_ref, om_ref, 0)):
        for a in range(3):
            j = 3 * a + b
            for c in range(3):
                place = pl.ds((3 * a + c) * 8, 8)
                low = turn(zp, -j) if c == 2 else None
                high = turn(zm, LANES - 1 - j) if c == 0 else None
                out[place, :] = move_z(ref[place, :], c, low, high, lanes)


def face_x_kernel(xp_ref, xm_ref, zp_ref, zm_ref, yp_ref, ym_ref, op_ref, om_ref):
    lanes = lane_index(ROWS)
    rows = lax.broadcasted_iota(jnp.int32, (ROWS, LANES), 0)
    zp, zm = zp_ref[0:16, :], zm_ref[0:16, :]
    for ref, out, a, p in ((xp_ref, op_ref, 2, SLABS - 1), (xm_ref, om_ref, 0, 0)):
        for b in range(3):
            j = 3 * a + b
            for c in range(3):
                place = pl.ds((3 * b + c) * ROWS, ROWS)
                low = turn(zp, -(16 * p + j)) if c == 2 else None
                high = turn(zm, LANES - 1 - 16 * p - j) if c == 0 else None
                value = move_z(ref[place, :], c, low, high, lanes)
                spot = pl.ds((3 * a + c) * 8 + p, 1)
                ghost = yp_ref[spot, :] if b == 2 else ym_ref[spot, :]
                out[place, :] = move_y(value, b, ghost, rows)


def stream_kernel(source, zp_ref, zm_ref, yp_ref, ym_ref, out_ref):
    lanes = lane_index(ROWS)
    rows = lax.broadcasted_iota(jnp.int32, (ROWS, LANES), 0)

    def step(p, carry):
        for a in range(3):
            origin = p if a == 1 else (jnp.maximum(p - 1, 0) if a == 2 else jnp.minimum(p + 1, SLABS - 1))
            back = lax.rem(LANES - 16 * origin, LANES)
            zp = turn(zp_ref[0:16, :], back)
            zm = turn(zm_ref[0:16, :], back)
            for b in range(3):
                j = 3 * a + b
                for c in range(3):
                    i = 9 * a + 3 * b + c
                    value = source[pl.ds(pl.multiple_of(i * TILES + origin * ROWS, ROWS), ROWS), :]
                    low = turn(zp, -j) if c == 2 else None
                    high = turn(zm, LANES - 1 - j) if c == 0 else None
                    value = move_z(value, c, low, high, lanes)
                    spot = pl.ds((3 * a + c) * 8 + origin, 1)
                    ghost = yp_ref[spot, :] if b == 2 else ym_ref[spot, :]
                    value = move_y(value, b, ghost, rows)
                    out_ref[pl.ds(pl.multiple_of(i * TILES + p * ROWS, ROWS), ROWS), :] = value
        return carry

    lax.fori_loop(0, SLABS, step, 0)


def coarse_ends_kernel(state_hbm, rates_hbm, *refs):
    outs = refs[:3]
    state, rates, semaphores = refs[3:]
    pieces = [
        fetch(state_hbm.at[:, pl.ds(0, ROWS), :], state.at[:, pl.ds(0, ROWS), :], semaphores.at[0]),
        fetch(
            state_hbm.at[:, pl.ds(TILES - ROWS, ROWS), :], state.at[:, pl.ds(ROWS, ROWS), :], semaphores.at[1]
        ),
        fetch(rates_hbm, rates, semaphores.at[2]),
    ]
    wait(pieces)

    def load(i, u):
        return state[i, pl.ds(pl.multiple_of(lax.rem(u, 4) * 8, 8), 8), :]

    collide_ends(load, None, rates, *outs)


def coarse_rest_kernel(state_hbm, rates_hbm, ends_ref, *refs):
    outs = refs[:5]
    state, rates, semaphores = refs[5:]
    middle = pl.ds(ROWS, TILES - 2 * ROWS)
    pieces = [
        fetch(state_hbm.at[:, middle, :], state, semaphores.at[0]),
        fetch(rates_hbm, rates, semaphores.at[1]),
    ]
    wait(pieces)

    def load(i, u):
        return state[i, pl.ds(pl.multiple_of((u - 2) * 8, 8), 8), :]

    collide_rest(load, None, rates, ends_ref, *outs)


def old_kernel(state_hbm, table_hbm, sent_hbm, table, tiles, sent, chunks, semaphores):
    pieces = [fetch(table_hbm, table, semaphores.at[0])]
    for k in range(9):
        rows = pl.ds((18 + k) * TILES, TILES)
        pieces.append(fetch(state_hbm.at[rows], tiles.at[pl.ds(k * WIDE, TILES)], chunks.at[k]))
    wait(pieces)
    wait(pack_halves(tiles, table, sent, sent_hbm, semaphores.at[1], semaphores.at[2]))


def tile8(tiles, k, u):
    return tiles[pl.ds(pl.multiple_of(k * WIDE + u * 8, 8), 8), :]


def fine_first_kernel(state_hbm, flags_hbm, rates_hbm, table_hbm, received_ref, *refs):
    outs = refs[:7]
    state, flags, rates, table, tiles, chunks, semaphores = refs[7:]
    pieces = [
        fetch(
            state_hbm.at[pl.ds((18 + k) * TILES, TILES)], tiles.at[pl.ds(k * WIDE, TILES)], chunks.at[k]
        )
        for k in range(9)
    ]
    second = fetch(table_hbm, table, semaphores.at[0])
    others = [
        fetch(state_hbm.at[pl.ds(0, 18 * TILES)], state, semaphores.at[1]),
        fetch(flags_hbm, flags, semaphores.at[2]),
        fetch(rates_hbm, rates, semaphores.at[3]),
    ]
    for piece in pieces:
        piece.wait()
    second.wait()
    install(tiles, table, received_ref)
    for other in others:
        other.wait()

    def load(i, u):
        return tile8(tiles, i - 18, u) if i >= 18 else load8(state, i, u)

    collide(load, flags, rates, *outs)


def fine_ends_kernel(state_ref, xp_ref, xm_ref, received_ref, flags_hbm, rates_hbm, table_hbm, *refs):
    tiles, outs = refs[0], refs[1:4]
    flags, rates, table, semaphores = refs[4:]
    first = fetch(table_hbm, table, semaphores.at[0])
    others = [fetch(flags_hbm, flags, semaphores.at[1]), fetch(rates_hbm, rates, semaphores.at[2])]
    fill(tiles, state_ref, 18, xp_ref, 0)
    first.wait()
    install(tiles, table, received_ref)
    wait(others)

    def load(i, u):
        if i >= 18:
            return tile8(tiles, i - 18, u)
        value = load8(state_ref, i, u)
        if i < 9:
            ghost = xm_ref[pl.ds(pl.multiple_of(i * ROWS + lax.rem(u, 2) * 8, 8), 8), :]
            value = jnp.where(u >= 2 * SLABS - 2, ghost, value)
        return value

    collide_ends(load, flags, rates, *outs)


def fine_rest_kernel(state_ref, tiles_ref, flags_hbm, rates_hbm, ends_ref, *refs):
    outs = refs[:5]
    flags, rates, semaphores = refs[5:]
    wait([fetch(flags_hbm, flags, semaphores.at[0]), fetch(rates_hbm, rates, semaphores.at[1])])

    def load(i, u):
        return tile8(tiles_ref, i - 18, u) if i >= 18 else load8(state_ref, i, u)

    collide_rest(load, flags, rates, ends_ref, *outs)


def finish(state_ref, yp_ref, ym_ref, whole, out_hbm, semaphore):
    whole[...] = state_ref[...]
    for i in range(27):
        a, b, c = i // 9, (i // 3) % 3, i % 3
        if b != 1:
            ghost, q = (yp_ref, 0) if b == 2 else (ym_ref, ROWS - 1)
            whole[pl.ds(i * TILES + q, 8, stride=ROWS), :] = ghost[pl.ds((3 * a + c) * 8, 8), :]
    return fetch(whole, out_hbm, semaphore)


def mean_kernel(state_ref, yp_ref, ym_ref, old_hbm, table_hbm, sent_hbm, kept_ref, out_hbm, *scratch):
    whole, old, table, tiles, sent, semaphores = scratch
    second = fetch(old_hbm.at[pl.ds(18 * TILES, 9 * TILES)], old, semaphores.at[0])
    first = fetch(table_hbm, table, semaphores.at[1])
    copy = finish(state_ref, yp_ref, ym_ref, whole, out_hbm, semaphores.at[2])
    kept_ref[...] = whole[pl.ds(0, 9 * TILES), :]
    second.wait()
    for k in range(9):
        new = whole[pl.ds((18 + k) * TILES, TILES), :]
        tiles[pl.ds(k * WIDE, TILES), :] = 0.5 * (old[pl.ds(k * TILES, TILES), :] + new)
    first.wait()
    wait(pack_halves(tiles, table, sent, sent_hbm, semaphores.at[3], semaphores.at[4]))
    copy.wait()


def up_kernel(state_ref, yp_ref, ym_ref, table_hbm, sent_ref, out_hbm, *scratch):
    whole, table, tiles, semaphores = scratch
    first = fetch(table_hbm, table, semaphores.at[0])
    copy = finish(state_ref, yp_ref, ym_ref, whole, out_hbm, semaphores.at[1])
    fill(tiles, whole, 0)
    first.wait()
    pack(tiles, table, sent_ref)
    copy.wait()


def coarse_install_kernel(whole_hbm, kept_ref, received_ref, table_hbm, out_hbm, *scratch):
    table, tiles, semaphores, stores = scratch
    first = fetch(table_hbm, table, semaphores.at[0])
    for k in range(9):
        tiles[pl.ds(k * WIDE, TILES), :] = kept_ref[pl.ds(k * TILES, TILES), :]
    first.wait()
    install(tiles, table, received_ref)
    wait(
        [
            fetch(tiles.at[pl.ds(k * WIDE, TILES)], out_hbm.at[pl.ds(k * TILES, TILES)], stores.at[k])
            for k in range(9)
        ]
    )


STATE = (27 * TILES, LANES)
MESSAGE = (PEERS * CHUNK, LANES)
Z_FACE = (24, LANES)
Y_FACE = (9 * 8, LANES)
X_FACE = (9 * ROWS, LANES)
WIDE_TILES = (9 * WIDE, LANES)
NINE = (9 * TILES, LANES)
ENDS = (27 * 2 * ROWS, LANES)
REST = (STATE, Z_FACE, Z_FACE, Y_FACE, Y_FACE)
COLLIDED = (STATE, Z_FACE, Z_FACE, Y_FACE, Y_FACE, X_FACE, X_FACE)


def floats(*shape):
    return pltpu.VMEM(shape, jnp.float32)


def copies(count):
    return pltpu.SemaphoreType.DMA((count,))


FLAGS = pltpu.VMEM((TILES, LANES), jnp.int32)
RATES = pltpu.SMEM((27,), jnp.float32)
TABLE = pltpu.SMEM((2, PEERS), jnp.int32)


def run(kernel, name, spaces, shapes, *operands, scratch=(), alias=False, microseconds=1.0):
    spots = {"v": pltpu.VMEM, "h": pltpu.HBM}
    given, made = spaces.split(":")
    operands = [
        pltpu.with_memory_space_constraint(operand, pltpu.HBM) if space == "h" else operand
        for operand, space in zip(operands, given)
    ]
    return pl.pallas_call(
        kernel,
        name=name,
        out_shape=tuple(jax.ShapeDtypeStruct(shape, jnp.float32) for shape in shapes),
        in_specs=[pl.BlockSpec(memory_space=spots[space]) for space in given],
        out_specs=tuple(pl.BlockSpec(memory_space=spots[space]) for space in made),
        scratch_shapes=list(scratch),
        input_output_aliases={0: 0} if alias else {},
        compiler_params=pltpu.CompilerParams(vmem_limit_bytes=VMEM_BYTES),
        cost_estimate=pl.CostEstimate(
            flops=0, bytes_accessed=int(microseconds * 3.0e6), transcendentals=0
        ),
    )(*operands)


def swap(axis, plus, minus):
    count = lax.axis_size(axis)
    up = [(i, (i + 1) % count) for i in range(count)]
    down = [(i, (i - 1) % count) for i in range(count)]
    return lax.ppermute(plus, axis, up), lax.ppermute(minus, axis, down)


def halo(collided, zp, zm, yp, ym, xp, xm):
    zp, zm = swap("gz", zp, zm)
    yp, ym = run(face_y_kernel, "face_y", "vvvv:vv", (Y_FACE, Y_FACE), yp, ym, zp, zm)
    yp, ym = swap("gy", yp, ym)
    xp, xm = run(face_x_kernel, "face_x", "vvvvvv:vv", (X_FACE, X_FACE), xp, xm, zp, zm, yp, ym)
    xp, xm = swap("gx", xp, xm)
    (moved,) = run(
        stream_kernel, "stream", "vvvvv:v", (STATE,), collided, zp, zm, yp, ym, microseconds=2.0
    )
    return moved, xp, xm


def halo_x_first(xp, xm, rest):
    xp, xm = swap("gx", xp, xm)
    collided, zp, zm, yp, ym = rest()
    zp, zm = run(face_z_kernel, "face_z", "vvvv:vv", (Z_FACE, Z_FACE), zp, zm, xp, xm)
    zp, zm = swap("gz", zp, zm)
    yp, ym = run(face_y_last_kernel, "face_y", "vvvvvv:vv", (Y_FACE, Y_FACE), yp, ym, xp, xm, zp, zm)
    return yp, ym, (collided, xp, xm, zp, zm)


def halo_moved(xp, xm, rest, between):
    xp, xm = swap("gx", xp, xm)
    collided, zp, zm, _, _ = rest()
    zp, zm, moved = run(
        move_x_kernel, "move_x", "vvvvv:vvv", (Z_FACE, Z_FACE, STATE), collided, zp, zm, xp, xm
    )
    zp, zm = between(zp, zm)
    zp, zm = swap("gz", zp, zm)
    yp, ym = run(face_y_moved_kernel, "face_y", "vvv:vv", (Y_FACE, Y_FACE), moved, zp, zm)
    yp, ym = swap("gy", yp, ym)
    (state,) = run(stream_moved_kernel, "stream", "vvv:v", (STATE,), moved, zp, zm, microseconds=2.0)
    return state, yp, ym


def stream_first(operands):
    return run(stream_first_kernel, "stream", "vvvvv:v", (STATE,), *operands, microseconds=2.0)[0]


def routed(message):
    chunks = message.reshape(PEERS, 9, 2, LANES)
    received = lax.all_to_all(chunks, ("gx", "gz"), split_axis=0, concat_axis=0, tiled=True)
    return received.reshape(MESSAGE)


def body(fine, coarse, fine_rates, coarse_rates, flags, down_source, down_target, up_source, up_target):
    fine = fine.reshape(STATE)
    coarse = coarse.reshape(STATE)
    flags = flags.reshape(TILES, LANES)
    down_source, down_target, up_source, up_target = (
        table.reshape(-1, 2).T for table in (down_source, down_target, up_source, up_target)
    )
    cube = coarse.reshape(27, TILES, LANES)
    ends, xp, xm = run(
        coarse_ends_kernel, "coarse_ends", "hh:vvv", (ENDS, X_FACE, X_FACE), cube, coarse_rates,
        scratch=(floats(27, 2 * ROWS, LANES), RATES, copies(3)),
        microseconds=2.0,
    )

    def coarse_rest():
        return run(
            coarse_rest_kernel, "coarse_rest", "hhv:vvvvv", REST, cube, coarse_rates, ends,
            scratch=(floats(27, TILES - 2 * ROWS, LANES), RATES, copies(2)),
            microseconds=3.0,
        )

    (sent_old,) = run(
        old_kernel, "pack_old", "hh:h", (MESSAGE,), coarse, down_source,
        scratch=(TABLE, floats(*WIDE_TILES), floats(*MESSAGE), copies(9), copies(3)),
        microseconds=1.0,
    )
    arrived = []

    def send_old(zp, zm):
        sent, zp, zm = lax.optimization_barrier((sent_old, zp, zm))
        arrived.append(routed(sent))
        return zp, zm

    moved, yp, ym = halo_moved(xp, xm, coarse_rest, send_old)
    (received,) = arrived
    sent_mean, kept, coarse_new = run(
        mean_kernel, "pack_mean", "vvvhh:hvh", (MESSAGE, NINE, STATE), moved, yp, ym, coarse, down_source,
        scratch=(floats(*STATE), floats(*NINE), TABLE, floats(*WIDE_TILES), floats(*MESSAGE), copies(5)),
        microseconds=2.0,
    )
    mean = routed(sent_mean)
    parts = run(
        fine_first_kernel, "fine_first", "hhhhv:vvvvvvv", COLLIDED,
        fine, flags, fine_rates, down_target, received,
        scratch=(
            floats(18 * TILES, LANES), FLAGS, RATES, TABLE, floats(*WIDE_TILES), copies(9), copies(4)
        ),
        microseconds=4.0,
    )
    moved, xp, xm = halo(*parts)
    tiles, ends, face_xp, face_xm = run(
        fine_ends_kernel, "fine_ends", "vvvvhhh:vvvv", (WIDE_TILES, ENDS, X_FACE, X_FACE),
        moved, xp, xm, mean, flags, fine_rates, down_target,
        scratch=(FLAGS, RATES, TABLE, copies(3)),
        microseconds=3.0,
    )

    def fine_rest():
        return run(
            fine_rest_kernel, "fine_rest", "vvhhv:vvvvv", REST, moved, tiles, flags, fine_rates, ends,
            scratch=(FLAGS, RATES, copies(2)),
            microseconds=3.0,
        )

    yp, ym, whole = halo_x_first(face_xp, face_xm, fine_rest)
    yp, ym = swap("gy", yp, ym)
    sent_up, fine_next = run(
        up_kernel, "pack_up", "vvvh:vh", (MESSAGE, STATE), stream_first(whole), yp, ym, up_source,
        scratch=(floats(*STATE), TABLE, floats(*WIDE_TILES), copies(2)),
        microseconds=2.0,
    )
    up = routed(sent_up)
    (coarse_next,) = run(
        coarse_install_kernel, "coarse_install", "hvvh:h", (STATE,), coarse_new, kept, up, up_target,
        scratch=(TABLE, floats(*WIDE_TILES), copies(1), copies(9)),
        alias=True,
        microseconds=2.0,
    )
    block = (27, SLABS, ROWS, LANES)
    return fine_next.reshape(block), coarse_next.reshape(block)


def solution(mesh):
    placed = (
        P(None, "gx", "gy", "gz"),
        P(None, "gx", "gy", "gz"),
        P(),
        P(),
        P("gx", "gy", "gz"),
        P("gx", "gy", "gz", None, None),
        P("gx", "gy", "gz", None, None),
        P("gx", "gy", "gz", None, None),
        P("gx", "gy", "gz", None, None),
    )
    return jax.shard_map(
        body,
        mesh=mesh,
        in_specs=placed,
        out_specs=(P(None, "gx", "gy", "gz"), P(None, "gx", "gy", "gz")),
        check_vma=False,
    )
```

```python
import jax
import jax.numpy as jnp
from jax import lax
from jax.experimental import pallas as pl
from jax.experimental.pallas import tpu as pltpu
from jax.sharding import PartitionSpec as P

SLABS = 8
ROWS = 16
LANES = 128
TILES = SLABS * ROWS
CHUNK = 18
PEERS = 64
VMEM_BYTES = 10 * 1024 * 1024
WIDE = 136


def load8(ref, i, u):
    return ref[pl.ds(pl.multiple_of(i * TILES + u * 8, 8), 8), :]


def fetch(source, target, semaphore):
    copy = pltpu.make_async_copy(source, target, semaphore)
    copy.start()
    return copy


def wait(copies):
    for copy in copies:
        copy.wait()


def forward(values):
    for step in (9, 3, 1):
        out = list(values)
        for i in range(27):
            if (i // step) % 3 == 0:
                low, mid, high = values[i], values[i + step], values[i + 2 * step]
                even = high + low
                out[i] = even + 4.0 * mid
                out[i + step] = high - low
                out[i + 2 * step] = even
        values = out
    return values


def backward(values):
    for step in (9, 3, 1):
        out = list(values)
        for i in range(27):
            if (i // step) % 3 == 0:
                zero, one, two = values[i], values[i + step], values[i + 2 * step]
                out[i] = two - one
                out[i + step] = zero - two
                out[i + 2 * step] = two + one
        values = out
    return values


def equilibrium(moments):
    density = moments[0]
    momentum = (moments[9], moments[3], moments[1])
    squares = [part * part * (1.0 / 72.0) for part in momentum]
    scale = (1.0, 1.0 / 3.0, 1.0 / 9.0, 1.0 / 27.0)
    result = []
    for k in range(27):
        powers = (k // 9, (k // 3) % 3, k % 3)
        ones = [axis for axis in range(3) if powers[axis] == 1]
        twos = [axis for axis in range(3) if powers[axis] == 2]
        if len(ones) == 0:
            value = density
            for axis in twos:
                value = value + squares[axis]
        elif len(ones) == 1:
            value = momentum[ones[0]]
        elif len(ones) == 2:
            value = momentum[ones[0]] * momentum[ones[1]] * (1.0 / 216.0)
        else:
            value = jnp.zeros_like(density)
        if twos:
            value = value * scale[len(twos)]
        result.append(value)
    return result


def relax(values, rates_ref):
    moments = forward(values)
    target = equilibrium(moments)
    change = backward([(rates_ref[k] * 0.125) * (target[k] - moments[k]) for k in range(27)])
    result = []
    for i in range(27):
        rests = sum(1 for part in (i // 9, (i // 3) % 3, i % 3) if part == 1)
        moved = change[i] if rests == 0 else change[i] * (0.5**rests)
        result.append(values[i] + moved)
    return result


def lane_index(rows):
    return lax.broadcasted_iota(jnp.int32, (rows, LANES), 1)


def turn(value, amount):
    amount = amount % LANES if isinstance(amount, int) else amount
    if isinstance(amount, int) and amount == 0:
        return value
    return pltpu.roll(value, amount, 1)


def collide_at(load, flags_ref, rates_ref, store, u):
    values = [load(i, u) for i in range(27)]
    result = relax(values, rates_ref)
    if flags_ref is not None:
        solid = flags_ref[pl.ds(pl.multiple_of(u * 8, 8), 8), :] == 1
        result = [jnp.where(solid, values[26 - i], result[i]) for i in range(27)]
    for i in range(27):
        store(i, u, result[i])


def store8(ref):
    def store(i, u, value):
        ref[pl.ds(pl.multiple_of(i * TILES + u * 8, 8), 8), :] = value

    return store


def pack_z(out_ref, zp_ref, zm_ref, shifted):
    lanes = lane_index(8)
    for ref, c, edge in ((zp_ref, 2, LANES - 1), (zm_ref, 0, 0)):
        for half in range(2):
            packed = jnp.zeros((8, LANES), jnp.float32)
            for p in range(SLABS):
                for j in range(9):
                    source = p - (j // 3 - 1) if shifted else p
                    if 0 <= source < SLABS:
                        start = (3 * j + c) * TILES + source * ROWS + half * 8
                        column = turn(out_ref[start : start + 8, :], 16 * p + j - edge)
                        packed = jnp.where(lanes == 16 * p + j, column, packed)
            ref[half * 8 : half * 8 + 8, :] = packed


def pack_y(out_ref, zp_ref, zm_ref, yp_ref, ym_ref, shifted):
    lanes = lane_index(8)
    ends = [jnp.zeros((8, LANES), jnp.float32), None, jnp.zeros((8, LANES), jnp.float32)]
    for ref, b, q in ((yp_ref, 2, ROWS - 1), (ym_ref, 0, 0)):
        for a in range(3):
            for c in range(3):
                i = 9 * a + 3 * b + c
                rows = out_ref[pl.ds(i * TILES + q, 8, stride=ROWS), :]
                ref[pl.ds((3 * a + c) * 8, 8), :] = rows
                j = 3 * a + b
                if c != 1:
                    edge = LANES - 1 if c == 2 else 0
                    if shifted and a != 1:
                        rows = pltpu.roll(rows, 1 if a == 2 else 7, 0)
                    ends[c] = jnp.where(lanes == j, turn(rows, j - edge), ends[c])
    zp_ref[16:24, :] = ends[2]
    zm_ref[16:24, :] = ends[0]


def collide_ends(load, flags_ref, rates_ref, ends_ref, xp_ref, xm_ref):
    def step(k, carry):
        def store(i, u, value):
            ends_ref[pl.ds(pl.multiple_of(i * 2 * ROWS + k * 8, 8), 8), :] = value

        collide_at(load, flags_ref, rates_ref, store, k + (2 * SLABS - 4) * (k // 2))
        return carry

    lax.fori_loop(0, 4, step, 0, unroll=2)
    for j in range(9):
        xp_ref[pl.ds(j * ROWS, ROWS), :] = ends_ref[pl.ds((18 + j) * 2 * ROWS + ROWS, ROWS), :]
        xm_ref[pl.ds(j * ROWS, ROWS), :] = ends_ref[pl.ds(j * 2 * ROWS, ROWS), :]


def collide_rest(load, flags_ref, rates_ref, ends_ref, out_ref, zp_ref, zm_ref, yp_ref, ym_ref):
    def step(u, carry):
        collide_at(load, flags_ref, rates_ref, store8(out_ref), u)
        return carry

    lax.fori_loop(2, 2 * SLABS - 2, step, 0, unroll=2)
    for i in range(27):
        out_ref[pl.ds(i * TILES, ROWS), :] = ends_ref[pl.ds(i * 2 * ROWS, ROWS), :]
        out_ref[pl.ds((i + 1) * TILES - ROWS, ROWS), :] = ends_ref[pl.ds(i * 2 * ROWS + ROWS, ROWS), :]
    pack_z(out_ref, zp_ref, zm_ref, True)
    pack_y(out_ref, zp_ref, zm_ref, yp_ref, ym_ref, True)


def face_z_kernel(zp_ref, zm_ref, xp_ref, xm_ref, op_ref, om_ref):
    lanes = lane_index(8)
    subs = lax.broadcasted_iota(jnp.int32, (8, LANES), 0)
    for ref, out, c, edge in ((zp_ref, op_ref, 2, LANES - 1), (zm_ref, om_ref, 0, 0)):
        parts = [ref[0:8, :], ref[8:16, :], ref[16:24, :]]
        for ghost, a, p in ((xp_ref, 2, 0), (xm_ref, 0, SLABS - 1)):
            for b in range(3):
                j = 3 * a + b
                first = (3 * b + c) * ROWS
                for half in range(2):
                    column = turn(ghost[first + half * 8 : first + half * 8 + 8, :], 16 * p + j - edge)
                    parts[half] = jnp.where(lanes == 16 * p + j, column, parts[half])
                if b != 1:
                    q = ROWS - 1 if b == 2 else 0
                    row = jnp.broadcast_to(ghost[first + q : first + q + 1, :], (8, LANES))
                    here = jnp.logical_and(lanes == j, subs == p)
                    parts[2] = jnp.where(here, turn(row, j - edge), parts[2])
        for k in range(3):
            out[k * 8 : k * 8 + 8, :] = parts[k]


def move_x_kernel(state_ref, zp_ref, zm_ref, xp_ref, xm_ref, op_ref, om_ref, out_ref):
    face_z_kernel(zp_ref, zm_ref, xp_ref, xm_ref, op_ref, om_ref)
    long = TILES - ROWS
    for k in range(9):
        for a, ghost, at, to, start in ((2, xp_ref, 0, ROWS, 0), (0, xm_ref, long, 0, ROWS)):
            first = (9 * a + k) * TILES
            out_ref[pl.ds(first + to, long), :] = state_ref[pl.ds(first + start, long), :]
            out_ref[pl.ds(first + at, ROWS), :] = ghost[pl.ds(k * ROWS, ROWS), :]
    middle = pl.ds(9 * TILES, 9 * TILES)
    out_ref[middle, :] = state_ref[middle, :]


def face_y_moved_kernel(state_ref, zp_ref, zm_ref, op_ref, om_ref):
    lanes = lane_index(8)
    zp, zm = zp_ref[16:24, :], zm_ref[16:24, :]
    for out, b, q in ((op_ref, 2, ROWS - 1), (om_ref, 0, 0)):
        for a in range(3):
            j = 3 * a + b
            for c in range(3):
                value = state_ref[pl.ds((9 * a + 3 * b + c) * TILES + q, 8, stride=ROWS), :]
                low = turn(zp, -j) if c == 2 else None
                high = turn(zm, LANES - 1 - j) if c == 0 else None
                out[pl.ds((3 * a + c) * 8, 8), :] = move_z(value, c, low, high, lanes)


def face_y_last_kernel(yp_ref, ym_ref, xp_ref, xm_ref, zp_ref, zm_ref, op_ref, om_ref):
    lanes = lane_index(8)
    subs = lax.broadcasted_iota(jnp.int32, (8, LANES), 0)
    zp, zm = zp_ref[16:24, :], zm_ref[16:24, :]
    for ref, out, b, q in ((yp_ref, op_ref, 2, ROWS - 1), (ym_ref, om_ref, 0, 0)):
        for a in range(3):
            j = 3 * a + b
            for c in range(3):
                place = pl.ds((3 * a + c) * 8, 8)
                value = ref[place, :]
                if a != 1:
                    ghost = xp_ref if a == 2 else xm_ref
                    spot = (3 * b + c) * ROWS + q
                    row = jnp.broadcast_to(ghost[spot : spot + 1, :], (8, LANES))
                    value = pltpu.roll(value, 1 if a == 2 else 7, 0)
                    value = jnp.where(subs == (0 if a == 2 else SLABS - 1), row, value)
                low = turn(zp, -j) if c == 2 else None
                high = turn(zm, LANES - 1 - j) if c == 0 else None
                out[place, :] = move_z(value, c, low, high, lanes)


def stream_moved_kernel(source, zp_ref, zm_ref, out_ref):
    stream_first_kernel(source, None, None, zp_ref, zm_ref, out_ref)


def stream_first_kernel(source, xp_ref, xm_ref, zp_ref, zm_ref, out_ref):
    lanes = lane_index(ROWS)

    def step(p, carry):
        back = lax.rem(LANES - 16 * p, LANES)
        zp = turn(zp_ref[0:16, :], back)
        zm = turn(zm_ref[0:16, :], back)
        for a in range(3):
            origin = jnp.maximum(p - 1, 0) if a == 2 else jnp.minimum(p + 1, SLABS - 1)
            if a == 1 or xp_ref is None:
                origin = p
            for b in range(3):
                j = 3 * a + b
                for c in range(3):
                    i = 9 * a + 3 * b + c
                    value = source[pl.ds(pl.multiple_of(i * TILES + origin * ROWS, ROWS), ROWS), :]
                    place = pl.ds((3 * b + c) * ROWS, ROWS)
                    if a == 2 and xp_ref is not None:
                        value = jnp.where(p == 0, xp_ref[place, :], value)
                    if a == 0 and xm_ref is not None:
                        value = jnp.where(p == SLABS - 1, xm_ref[place, :], value)
                    low = turn(zp, -j) if c == 2 else None
                    high = turn(zm, LANES - 1 - j) if c == 0 else None
                    value = move_z(value, c, low, high, lanes)
                    if b != 1:
                        value = pltpu.roll(value, 1 if b == 2 else ROWS - 1, 0)
                    out_ref[pl.ds(pl.multiple_of(i * TILES + p * ROWS, ROWS), ROWS), :] = value
        return carry

    lax.fori_loop(0, SLABS, step, 0)


def fill(tiles, state_ref, first, ghost_ref=None, slab=None):
    for k in range(9):
        tiles[pl.ds(k * WIDE, TILES), :] = state_ref[pl.ds((first + k) * TILES, TILES), :]
        if ghost_ref is not None:
            tiles[pl.ds(k * WIDE + slab * ROWS, ROWS), :] = ghost_ref[pl.ds(k * ROWS, ROWS), :]


def pack(tiles, table_ref, sent, first=0, last=None):
    def step(r, carry):
        for j in range(2):
            tile = jnp.maximum(table_ref[j, r], 0)
            most = tiles[pl.ds(tile, 8, stride=WIDE), :]
            last = tiles[pl.ds(8 * WIDE + tile, 1), :]
            sent[pl.ds(r * CHUNK + j, 8, stride=2), :] = most
            sent[pl.ds(r * CHUNK + 16 + j, 1), :] = last
        return carry

    lax.fori_loop(first, PEERS if last is None else last, step, 0, unroll=4)


def pack_halves(tiles, table_ref, sent, sent_hbm, *semaphores):
    middle = PEERS // 2
    copies = []
    for (first, last), semaphore in zip(((0, middle), (middle, PEERS)), semaphores):
        pack(tiles, table_ref, sent, first, last)
        rows = pl.ds(first * CHUNK, (last - first) * CHUNK)
        copies.append(fetch(sent.at[rows], sent_hbm.at[rows], semaphore))
    return copies


def install(tiles, table_ref, received_ref):
    def step(r, carry):
        moved = []
        for j in range(2):
            tile = table_ref[j, r]
            tile = jnp.where(tile < 0, TILES, tile)
            most = received_ref[pl.ds(r * CHUNK + j, 8, stride=2), :]
            last = received_ref[pl.ds(r * CHUNK + 16 + j, 1), :]
            moved.append((tile, most, last))
        for tile, most, last in moved:
            tiles[pl.ds(tile, 8, stride=WIDE), :] = most
            tiles[pl.ds(8 * WIDE + tile, 1), :] = last
        return carry

    lax.fori_loop(0, PEERS, step, 0, unroll=4)


def move_z(value, c, low_ghost, high_ghost, lanes):
    if c == 2:
        return jnp.where(lanes == 0, low_ghost, turn(value, 1))
    if c == 0:
        return jnp.where(lanes == LANES - 1, high_ghost, turn(value, LANES - 1))
    return value


def move_y(value, b, ghost, rows):
    if b == 2:
        return jnp.where(rows == 0, ghost, pltpu.roll(value, 1, 0))
    if b == 0:
        return jnp.where(rows == ROWS - 1, ghost, pltpu.roll(value, ROWS - 1, 0))
    return value


def stream_kernel(source, yp_ref, ym_ref, zp_ref, zm_ref, out_ref):
    lanes = lane_index(ROWS)
    rows = lax.broadcasted_iota(jnp.int32, (ROWS, LANES), 0)

    def step(p, carry):
        for a in range(3):
            origin = p if a == 1 else (jnp.maximum(p - 1, 0) if a == 2 else jnp.minimum(p + 1, SLABS - 1))
            back = lax.rem(LANES - 16 * origin, LANES)
            zp = turn(zp_ref[0:16, :], back)
            zm = turn(zm_ref[0:16, :], back)
            for b in range(3):
                j = 3 * a + b
                for c in range(3):
                    i = 9 * a + 3 * b + c
                    value = source[pl.ds(pl.multiple_of(i * TILES + origin * ROWS, ROWS), ROWS), :]
                    spot = pl.ds((3 * a + c) * 8 + origin, 1)
                    ghost = yp_ref[spot, :] if b == 2 else ym_ref[spot, :]
                    value = move_y(value, b, ghost, rows)
                    low = turn(zp, -j) if c == 2 else None
                    high = turn(zm, LANES - 1 - j) if c == 0 else None
                    value = move_z(value, c, low, high, lanes)
                    out_ref[pl.ds(pl.multiple_of(i * TILES + p * ROWS, ROWS), ROWS), :] = value
        return carry

    lax.fori_loop(0, SLABS, step, 0)


def coarse_ends_kernel(state_hbm, rates_hbm, *refs):
    outs, rest_ref, tiles = refs[:3], refs[3], refs[4]
    state, rates, semaphores, chunks = refs[5:]
    pieces = [
        fetch(state_hbm.at[:, pl.ds(0, ROWS), :], state.at[:, pl.ds(0, ROWS), :], semaphores.at[0]),
        fetch(
            state_hbm.at[:, pl.ds(TILES - ROWS, ROWS), :], state.at[:, pl.ds(ROWS, ROWS), :], semaphores.at[1]
        ),
        fetch(rates_hbm, rates, semaphores.at[2]),
    ]
    others = [fetch(state_hbm.at[:, pl.ds(ROWS, TILES - 2 * ROWS), :], rest_ref, semaphores.at[3])]
    for k in range(9):
        others.append(fetch(state_hbm.at[18 + k], tiles.at[pl.ds(k * WIDE, TILES)], chunks.at[k]))
    wait(pieces)

    def load(i, u):
        return state[i, pl.ds(pl.multiple_of(lax.rem(u, 4) * 8, 8), 8), :]

    collide_ends(load, None, rates, *outs)
    wait(others)


def coarse_rest_kernel(state_ref, rates_hbm, ends_ref, *refs):
    outs = refs[:5]
    rates, semaphores = refs[5:]
    fetch(rates_hbm, rates, semaphores.at[0]).wait()

    def load(i, u):
        return state_ref[i, pl.ds(pl.multiple_of((u - 2) * 8, 8), 8), :]

    collide_rest(load, None, rates, ends_ref, *outs)


def old_kernel(tiles, table_hbm, sent_hbm, table, sent, semaphores):
    fetch(table_hbm, table, semaphores.at[0]).wait()
    wait(pack_halves(tiles, table, sent, sent_hbm, semaphores.at[1], semaphores.at[2]))


def tile8(tiles, k, u):
    return tiles[pl.ds(pl.multiple_of(k * WIDE + u * 8, 8), 8), :]


def fine_rows_kernel(state_hbm, flags_hbm, rates_hbm, table_hbm, received_ref, *refs):
    tiles, state, yp_ref, ym_ref, flags, rates, table, chunks, semaphores = refs
    pieces = [
        fetch(
            state_hbm.at[pl.ds((18 + k) * TILES, TILES)], tiles.at[pl.ds(k * WIDE, TILES)], chunks.at[k]
        )
        for k in range(9)
    ]
    pieces.append(fetch(table_hbm, table, semaphores.at[0]))
    others = [
        fetch(state_hbm.at[pl.ds(0, 18 * TILES)], state, semaphores.at[1]),
        fetch(flags_hbm, flags, semaphores.at[2]),
        fetch(rates_hbm, rates, semaphores.at[3]),
    ]
    wait(pieces)
    install(tiles, table, received_ref)
    wait(others)
    for ref, b, q in ((yp_ref, 2, ROWS - 1), (ym_ref, 0, 0)):
        values = []
        for i in range(27):
            first = (i - 18) * WIDE if i >= 18 else i * TILES
            values.append((tiles if i >= 18 else state)[pl.ds(first + q, 8, stride=ROWS), :])
        result = relax(values, rates)
        solid = flags[pl.ds(q, 8, stride=ROWS), :] == 1
        for a in range(3):
            for c in range(3):
                i = 9 * a + 3 * b + c
                ref[pl.ds((3 * a + c) * 8, 8), :] = jnp.where(solid, values[26 - i], result[i])


def fine_all_kernel(tiles, state_ref, flags_hbm, rates_hbm, *refs):
    out_ref, zp_ref, zm_ref, xp_ref, xm_ref, flags, rates, semaphores = refs
    wait([fetch(flags_hbm, flags, semaphores.at[0]), fetch(rates_hbm, rates, semaphores.at[1])])

    def load(i, u):
        return tile8(tiles, i - 18, u) if i >= 18 else load8(state_ref, i, u)

    def step(u, carry):
        collide_at(load, flags, rates, store8(out_ref), u)
        return carry

    lax.fori_loop(0, 2 * SLABS, step, 0, unroll=2)
    pack_z(out_ref, zp_ref, zm_ref, False)
    for j in range(9):
        xp_ref[pl.ds(j * ROWS, ROWS), :] = out_ref[pl.ds((18 + j) * TILES + 7 * ROWS, ROWS), :]
        xm_ref[pl.ds(j * ROWS, ROWS), :] = out_ref[pl.ds(j * TILES, ROWS), :]


def face_z_after_y_kernel(zp_ref, zm_ref, yp_ref, ym_ref, op_ref, om_ref):
    lanes = lane_index(ROWS)
    rows = lax.broadcasted_iota(jnp.int32, (ROWS, LANES), 0)
    j_of = lax.bitwise_and(lanes, 15)
    up = jnp.logical_or(jnp.logical_or(j_of == 2, j_of == 5), j_of == 8)
    down = jnp.logical_or(jnp.logical_or(j_of == 0, j_of == 3), j_of == 6)
    small = lane_index(8)
    slab = lax.broadcasted_iota(jnp.int32, (8, LANES), 0) * 16
    for ref, out, c, edge in ((zp_ref, op_ref, 2, LANES - 1), (zm_ref, om_ref, 0, 0)):
        packed = ref[0:16, :]
        value = jnp.where(up, pltpu.roll(packed, 1, 0), packed)
        value = jnp.where(down, pltpu.roll(packed, ROWS - 1, 0), value)
        for ghost, b, q, lane_set in ((yp_ref, 2, 0, up), (ym_ref, 0, ROWS - 1, down)):
            spread = jnp.zeros((8, LANES), jnp.float32)
            for a in range(3):
                j = 3 * a + b
                column = ghost[pl.ds((3 * a + c) * 8, 8), :]
                column = pltpu.roll(column, (j - edge) % LANES, 1, stride=16, stride_axis=0)
                spread = jnp.where(small == slab + j, column, spread)
            row = jnp.sum(spread, axis=0, keepdims=True)
            here = jnp.logical_and(lane_set, rows == q)
            value = jnp.where(here, jnp.broadcast_to(row, (ROWS, LANES)), value)
        out[0:16, :] = value
        out[16:24, :] = jnp.zeros((8, LANES), jnp.float32)


def face_x_after_z_kernel(xp_ref, xm_ref, yp_ref, ym_ref, zp_ref, zm_ref, op_ref, om_ref):
    lanes = lane_index(ROWS)
    rows = lax.broadcasted_iota(jnp.int32, (ROWS, LANES), 0)
    zp, zm = zp_ref[0:16, :], zm_ref[0:16, :]
    for ref, out, a, p in ((xp_ref, op_ref, 2, SLABS - 1), (xm_ref, om_ref, 0, 0)):
        for b in range(3):
            j = 3 * a + b
            for c in range(3):
                place = pl.ds((3 * b + c) * ROWS, ROWS)
                spot = pl.ds((3 * a + c) * 8 + p, 1)
                ghost = yp_ref[spot, :] if b == 2 else ym_ref[spot, :]
                value = move_y(ref[place, :], b, ghost, rows)
                low = turn(zp, -(16 * p + j)) if c == 2 else None
                high = turn(zm, LANES - 1 - 16 * p - j) if c == 0 else None
                out[place, :] = move_z(value, c, low, high, lanes)


def fine_ends_kernel(state_ref, xp_ref, xm_ref, received_ref, flags_hbm, rates_hbm, table_hbm, *refs):
    tiles, outs = refs[0], refs[1:4]
    flags, rates, table, semaphores = refs[4:]
    first = fetch(table_hbm, table, semaphores.at[0])
    others = [fetch(flags_hbm, flags, semaphores.at[1]), fetch(rates_hbm, rates, semaphores.at[2])]
    fill(tiles, state_ref, 18, xp_ref, 0)
    first.wait()
    install(tiles, table, received_ref)
    wait(others)

    def load(i, u):
        if i >= 18:
            return tile8(tiles, i - 18, u)
        value = load8(state_ref, i, u)
        if i < 9:
            ghost = xm_ref[pl.ds(pl.multiple_of(i * ROWS + lax.rem(u, 2) * 8, 8), 8), :]
            value = jnp.where(u >= 2 * SLABS - 2, ghost, value)
        return value

    collide_ends(load, flags, rates, *outs)


def fine_rest_kernel(state_ref, tiles_ref, flags_hbm, rates_hbm, ends_ref, *refs):
    outs = refs[:5]
    flags, rates, semaphores = refs[5:]
    wait([fetch(flags_hbm, flags, semaphores.at[0]), fetch(rates_hbm, rates, semaphores.at[1])])

    def load(i, u):
        return tile8(tiles_ref, i - 18, u) if i >= 18 else load8(state_ref, i, u)

    collide_rest(load, flags, rates, ends_ref, *outs)


def finish(state_ref, yp_ref, ym_ref, whole, out_hbm, semaphore):
    whole[...] = state_ref[...]
    for i in range(27):
        a, b, c = i // 9, (i // 3) % 3, i % 3
        if b != 1:
            ghost, q = (yp_ref, 0) if b == 2 else (ym_ref, ROWS - 1)
            whole[pl.ds(i * TILES + q, 8, stride=ROWS), :] = ghost[pl.ds((3 * a + c) * 8, 8), :]
    return fetch(whole, out_hbm, semaphore)


def mean_kernel(state_ref, yp_ref, ym_ref, old_hbm, table_hbm, sent_hbm, kept_ref, out_hbm, *scratch):
    whole, old, table, tiles, sent, semaphores = scratch
    second = fetch(old_hbm.at[pl.ds(18 * TILES, 9 * TILES)], old, semaphores.at[0])
    first = fetch(table_hbm, table, semaphores.at[1])
    copy = finish(state_ref, yp_ref, ym_ref, whole, out_hbm, semaphores.at[2])
    kept_ref[...] = whole[pl.ds(0, 9 * TILES), :]
    second.wait()
    for k in range(9):
        new = whole[pl.ds((18 + k) * TILES, TILES), :]
        tiles[pl.ds(k * WIDE, TILES), :] = 0.5 * (old[pl.ds(k * TILES, TILES), :] + new)
    first.wait()
    wait(pack_halves(tiles, table, sent, sent_hbm, semaphores.at[3], semaphores.at[4]))
    copy.wait()


def up_kernel(state_ref, yp_ref, ym_ref, table_hbm, sent_ref, out_hbm, *scratch):
    whole, table, tiles, semaphores = scratch
    first = fetch(table_hbm, table, semaphores.at[0])
    copy = finish(state_ref, yp_ref, ym_ref, whole, out_hbm, semaphores.at[1])
    fill(tiles, whole, 0)
    first.wait()
    pack(tiles, table, sent_ref)
    copy.wait()


def coarse_install_kernel(whole_hbm, kept_ref, received_ref, table_hbm, out_hbm, *scratch):
    table, tiles, semaphores, stores = scratch
    first = fetch(table_hbm, table, semaphores.at[0])
    for k in range(9):
        tiles[pl.ds(k * WIDE, TILES), :] = kept_ref[pl.ds(k * TILES, TILES), :]
    first.wait()
    install(tiles, table, received_ref)
    wait(
        [
            fetch(tiles.at[pl.ds(k * WIDE, TILES)], out_hbm.at[pl.ds(k * TILES, TILES)], stores.at[k])
            for k in range(9)
        ]
    )


STATE = (27 * TILES, LANES)
MESSAGE = (PEERS * CHUNK, LANES)
Z_FACE = (24, LANES)
Y_FACE = (9 * 8, LANES)
X_FACE = (9 * ROWS, LANES)
WIDE_TILES = (9 * WIDE, LANES)
NINE = (9 * TILES, LANES)
ENDS = (27 * 2 * ROWS, LANES)
REST = (STATE, Z_FACE, Z_FACE, Y_FACE, Y_FACE)


def floats(*shape):
    return pltpu.VMEM(shape, jnp.float32)


def copies(count):
    return pltpu.SemaphoreType.DMA((count,))


FLAGS = pltpu.VMEM((TILES, LANES), jnp.int32)
RATES = pltpu.SMEM((27,), jnp.float32)
TABLE = pltpu.SMEM((2, PEERS), jnp.int32)


def run(kernel, name, spaces, shapes, *operands, scratch=(), alias=False, microseconds=1.0):
    spots = {"v": pltpu.VMEM, "h": pltpu.HBM}
    given, made = spaces.split(":")
    operands = [
        pltpu.with_memory_space_constraint(operand, pltpu.HBM) if space == "h" else operand
        for operand, space in zip(operands, given)
    ]
    return pl.pallas_call(
        kernel,
        name=name,
        out_shape=tuple(jax.ShapeDtypeStruct(shape, jnp.float32) for shape in shapes),
        in_specs=[pl.BlockSpec(memory_space=spots[space]) for space in given],
        out_specs=tuple(pl.BlockSpec(memory_space=spots[space]) for space in made),
        scratch_shapes=list(scratch),
        input_output_aliases={0: 0} if alias else {},
        compiler_params=pltpu.CompilerParams(vmem_limit_bytes=VMEM_BYTES),
        cost_estimate=pl.CostEstimate(
            flops=0, bytes_accessed=int(microseconds * 3.0e6), transcendentals=0
        ),
    )(*operands)


def swap(axis, plus, minus):
    count = lax.axis_size(axis)
    up = [(i, (i + 1) % count) for i in range(count)]
    down = [(i, (i - 1) % count) for i in range(count)]
    return lax.ppermute(plus, axis, up), lax.ppermute(minus, axis, down)


def halo_y_first(yp, ym, rest):
    yp, ym = swap("gy", yp, ym)
    collided, zp, zm, xp, xm = rest()
    zp, zm = run(face_z_after_y_kernel, "face_z", "vvvv:vv", (Z_FACE, Z_FACE), zp, zm, yp, ym)
    zp, zm = swap("gz", zp, zm)
    xp, xm = run(face_x_after_z_kernel, "face_x", "vvvvvv:vv", (X_FACE, X_FACE), xp, xm, yp, ym, zp, zm)
    xp, xm = swap("gx", xp, xm)
    (moved,) = run(
        stream_kernel, "stream", "vvvvv:v", (STATE,), collided, yp, ym, zp, zm, microseconds=2.0
    )
    return moved, xp, xm


def halo_x_first(xp, xm, rest):
    xp, xm = swap("gx", xp, xm)
    collided, zp, zm, yp, ym = rest()
    zp, zm = run(face_z_kernel, "face_z", "vvvv:vv", (Z_FACE, Z_FACE), zp, zm, xp, xm)
    zp, zm = swap("gz", zp, zm)
    yp, ym = run(face_y_last_kernel, "face_y", "vvvvvv:vv", (Y_FACE, Y_FACE), yp, ym, xp, xm, zp, zm)
    return yp, ym, (collided, xp, xm, zp, zm)


def halo_moved(xp, xm, rest, between):
    xp, xm = swap("gx", xp, xm)
    collided, zp, zm, _, _ = rest()
    zp, zm, moved = run(
        move_x_kernel, "move_x", "vvvvv:vvv", (Z_FACE, Z_FACE, STATE), collided, zp, zm, xp, xm
    )
    zp, zm = between(zp, zm)
    zp, zm = swap("gz", zp, zm)
    yp, ym = run(face_y_moved_kernel, "face_y", "vvv:vv", (Y_FACE, Y_FACE), moved, zp, zm)
    yp, ym = swap("gy", yp, ym)
    (state,) = run(stream_moved_kernel, "stream", "vvv:v", (STATE,), moved, zp, zm, microseconds=2.0)
    return state, yp, ym


def stream_first(operands):
    return run(stream_first_kernel, "stream", "vvvvv:v", (STATE,), *operands, microseconds=2.0)[0]


def routed(message):
    chunks = message.reshape(PEERS, 9, 2, LANES)
    received = lax.all_to_all(chunks, ("gx", "gz"), split_axis=0, concat_axis=0, tiled=True)
    return received.reshape(MESSAGE)


def body(fine, coarse, fine_rates, coarse_rates, flags, down_source, down_target, up_source, up_target):
    fine = fine.reshape(STATE)
    coarse = coarse.reshape(STATE)
    flags = flags.reshape(TILES, LANES)
    down_source, down_target, up_source, up_target = (
        table.reshape(-1, 2).T for table in (down_source, down_target, up_source, up_target)
    )
    cube = coarse.reshape(27, TILES, LANES)
    ends, xp, xm, others, tiles = run(
        coarse_ends_kernel, "coarse_ends", "hh:vvvvv",
        (ENDS, X_FACE, X_FACE, (27, TILES - 2 * ROWS, LANES), WIDE_TILES), cube, coarse_rates,
        scratch=(floats(27, 2 * ROWS, LANES), RATES, copies(4), copies(9)),
        microseconds=2.0,
    )

    def coarse_rest():
        return run(
            coarse_rest_kernel, "coarse_rest", "vhv:vvvvv", REST, others, coarse_rates, ends,
            scratch=(RATES, copies(1)),
            microseconds=3.0,
        )

    (sent_old,) = run(
        old_kernel, "pack_old", "vh:h", (MESSAGE,), tiles, down_source,
        scratch=(TABLE, floats(*MESSAGE), copies(3)),
        microseconds=1.0,
    )
    arrived = []

    def send_old(zp, zm):
        sent, zp, zm = lax.optimization_barrier((sent_old, zp, zm))
        arrived.append(routed(sent))
        return zp, zm

    moved, yp, ym = halo_moved(xp, xm, coarse_rest, send_old)
    (received,) = arrived
    sent_mean, kept, coarse_new = run(
        mean_kernel, "pack_mean", "vvvhh:hvh", (MESSAGE, NINE, STATE), moved, yp, ym, coarse, down_source,
        scratch=(floats(*STATE), floats(*NINE), TABLE, floats(*WIDE_TILES), floats(*MESSAGE), copies(5)),
        microseconds=2.0,
    )
    mean = routed(sent_mean)
    tiles, others, yp, ym = run(
        fine_rows_kernel, "fine_rows", "hhhhv:vvvv", (WIDE_TILES, (18 * TILES, LANES), Y_FACE, Y_FACE),
        fine, flags, fine_rates, down_target, received,
        scratch=(FLAGS, RATES, TABLE, copies(9), copies(4)),
        microseconds=2.0,
    )

    def fine_all():
        return run(
            fine_all_kernel, "fine_all", "vvhh:vvvvv", (STATE, Z_FACE, Z_FACE, X_FACE, X_FACE),
            tiles, others, flags, fine_rates,
            scratch=(FLAGS, RATES, copies(2)),
            microseconds=3.0,
        )

    moved, xp, xm = halo_y_first(yp, ym, fine_all)
    tiles, ends, face_xp, face_xm = run(
        fine_ends_kernel, "fine_ends", "vvvvhhh:vvvv", (WIDE_TILES, ENDS, X_FACE, X_FACE),
        moved, xp, xm, mean, flags, fine_rates, down_target,
        scratch=(FLAGS, RATES, TABLE, copies(3)),
        microseconds=3.0,
    )

    def fine_rest():
        return run(
            fine_rest_kernel, "fine_rest", "vvhhv:vvvvv", REST, moved, tiles, flags, fine_rates, ends,
            scratch=(FLAGS, RATES, copies(2)),
            microseconds=3.0,
        )

    yp, ym, whole = halo_x_first(face_xp, face_xm, fine_rest)
    yp, ym = swap("gy", yp, ym)
    sent_up, fine_next = run(
        up_kernel, "pack_up", "vvvh:vh", (MESSAGE, STATE), stream_first(whole), yp, ym, up_source,
        scratch=(floats(*STATE), TABLE, floats(*WIDE_TILES), copies(2)),
        microseconds=2.0,
    )
    up = routed(sent_up)
    (coarse_next,) = run(
        coarse_install_kernel, "coarse_install", "hvvh:h", (STATE,), coarse_new, kept, up, up_target,
        scratch=(TABLE, floats(*WIDE_TILES), copies(1), copies(9)),
        alias=True,
        microseconds=2.0,
    )
    block = (27, SLABS, ROWS, LANES)
    return fine_next.reshape(block), coarse_next.reshape(block)


def solution(mesh):
    placed = (
        P(None, "gx", "gy", "gz"),
        P(None, "gx", "gy", "gz"),
        P(),
        P(),
        P("gx", "gy", "gz"),
        P("gx", "gy", "gz", None, None),
        P("gx", "gy", "gz", None, None),
        P("gx", "gy", "gz", None, None),
        P("gx", "gy", "gz", None, None),
    )
    return jax.shard_map(
        body,
        mesh=mesh,
        in_specs=placed,
        out_specs=(P(None, "gx", "gy", "gz"), P(None, "gx", "gy", "gz")),
        check_vma=False,
    )
```

```python
import jax
import jax.numpy as jnp
from jax import lax
from jax.experimental import pallas as pl
from jax.experimental.pallas import tpu as pltpu
from jax.sharding import PartitionSpec as P

SLABS = 8
ROWS = 16
LANES = 128
TILES = SLABS * ROWS
CHUNK = 18
PEERS = 64
VMEM_BYTES = 10 * 1024 * 1024
WIDE = 136


def load8(ref, i, u):
    return ref[pl.ds(pl.multiple_of(i * TILES + u * 8, 8), 8), :]


def fetch(source, target, semaphore):
    copy = pltpu.make_async_copy(source, target, semaphore)
    copy.start()
    return copy


def wait(copies):
    for copy in copies:
        copy.wait()


def forward(values):
    for step in (9, 3, 1):
        out = list(values)
        for i in range(27):
            if (i // step) % 3 == 0:
                low, mid, high = values[i], values[i + step], values[i + 2 * step]
                even = high + low
                out[i] = even + 4.0 * mid
                out[i + step] = high - low
                out[i + 2 * step] = even
        values = out
    return values


def backward(values):
    for step in (9, 3, 1):
        out = list(values)
        for i in range(27):
            if (i // step) % 3 == 0:
                zero, one, two = values[i], values[i + step], values[i + 2 * step]
                out[i] = two - one
                out[i + step] = zero - two
                out[i + 2 * step] = two + one
        values = out
    return values


def equilibrium(moments):
    density = moments[0]
    momentum = (moments[9], moments[3], moments[1])
    squares = [part * part * (1.0 / 72.0) for part in momentum]
    scale = (1.0, 1.0 / 3.0, 1.0 / 9.0, 1.0 / 27.0)
    result = []
    for k in range(27):
        powers = (k // 9, (k // 3) % 3, k % 3)
        ones = [axis for axis in range(3) if powers[axis] == 1]
        twos = [axis for axis in range(3) if powers[axis] == 2]
        if len(ones) == 0:
            value = density
            for axis in twos:
                value = value + squares[axis]
        elif len(ones) == 1:
            value = momentum[ones[0]]
        elif len(ones) == 2:
            value = momentum[ones[0]] * momentum[ones[1]] * (1.0 / 216.0)
        else:
            value = jnp.zeros_like(density)
        if twos:
            value = value * scale[len(twos)]
        result.append(value)
    return result


def relax(values, rates_ref):
    moments = forward(values)
    target = equilibrium(moments)
    change = backward([(rates_ref[k] * 0.125) * (target[k] - moments[k]) for k in range(27)])
    result = []
    for i in range(27):
        rests = sum(1 for part in (i // 9, (i // 3) % 3, i % 3) if part == 1)
        moved = change[i] if rests == 0 else change[i] * (0.5**rests)
        result.append(values[i] + moved)
    return result


def lane_index(rows):
    return lax.broadcasted_iota(jnp.int32, (rows, LANES), 1)


def turn(value, amount):
    amount = amount % LANES if isinstance(amount, int) else amount
    if isinstance(amount, int) and amount == 0:
        return value
    return pltpu.roll(value, amount, 1)


def collide_at(load, flags_ref, rates_ref, store, u):
    values = [load(i, u) for i in range(27)]
    result = relax(values, rates_ref)
    if flags_ref is not None:
        solid = flags_ref[pl.ds(pl.multiple_of(u * 8, 8), 8), :] == 1
        result = [jnp.where(solid, values[26 - i], result[i]) for i in range(27)]
    for i in range(27):
        store(i, u, result[i])


def store8(ref):
    def store(i, u, value):
        ref[pl.ds(pl.multiple_of(i * TILES + u * 8, 8), 8), :] = value

    return store


def pack_z(out_ref, zp_ref, zm_ref, shifted):
    lanes = lane_index(8)
    for ref, c, edge in ((zp_ref, 2, LANES - 1), (zm_ref, 0, 0)):
        for half in range(2):
            packed = jnp.zeros((8, LANES), jnp.float32)
            for p in range(SLABS):
                for j in range(9):
                    source = p - (j // 3 - 1) if shifted else p
                    if 0 <= source < SLABS:
                        start = (3 * j + c) * TILES + source * ROWS + half * 8
                        column = turn(out_ref[start : start + 8, :], 16 * p + j - edge)
                        packed = jnp.where(lanes == 16 * p + j, column, packed)
            ref[half * 8 : half * 8 + 8, :] = packed


def pack_y(out_ref, zp_ref, zm_ref, yp_ref, ym_ref, shifted):
    lanes = lane_index(8)
    ends = [jnp.zeros((8, LANES), jnp.float32), None, jnp.zeros((8, LANES), jnp.float32)]
    for ref, b, q in ((yp_ref, 2, ROWS - 1), (ym_ref, 0, 0)):
        for a in range(3):
            for c in range(3):
                i = 9 * a + 3 * b + c
                rows = out_ref[pl.ds(i * TILES + q, 8, stride=ROWS), :]
                ref[pl.ds((3 * a + c) * 8, 8), :] = rows
                j = 3 * a + b
                if c != 1:
                    edge = LANES - 1 if c == 2 else 0
                    if shifted and a != 1:
                        rows = pltpu.roll(rows, 1 if a == 2 else 7, 0)
                    ends[c] = jnp.where(lanes == j, turn(rows, j - edge), ends[c])
    zp_ref[16:24, :] = ends[2]
    zm_ref[16:24, :] = ends[0]


def collide_ends(load, flags_ref, rates_ref, ends_ref, xp_ref, xm_ref):
    def step(k, carry):
        def store(i, u, value):
            ends_ref[pl.ds(pl.multiple_of(i * 2 * ROWS + k * 8, 8), 8), :] = value

        collide_at(load, flags_ref, rates_ref, store, k + (2 * SLABS - 4) * (k // 2))
        return carry

    lax.fori_loop(0, 4, step, 0, unroll=2)
    for j in range(9):
        xp_ref[pl.ds(j * ROWS, ROWS), :] = ends_ref[pl.ds((18 + j) * 2 * ROWS + ROWS, ROWS), :]
        xm_ref[pl.ds(j * ROWS, ROWS), :] = ends_ref[pl.ds(j * 2 * ROWS, ROWS), :]


def collide_rest(load, flags_ref, rates_ref, ends_ref, out_ref, zp_ref, zm_ref, yp_ref, ym_ref):
    def step(u, carry):
        collide_at(load, flags_ref, rates_ref, store8(out_ref), u)
        return carry

    lax.fori_loop(2, 2 * SLABS - 2, step, 0, unroll=2)
    for i in range(27):
        out_ref[pl.ds(i * TILES, ROWS), :] = ends_ref[pl.ds(i * 2 * ROWS, ROWS), :]
        out_ref[pl.ds((i + 1) * TILES - ROWS, ROWS), :] = ends_ref[pl.ds(i * 2 * ROWS + ROWS, ROWS), :]
    pack_z(out_ref, zp_ref, zm_ref, True)
    pack_y(out_ref, zp_ref, zm_ref, yp_ref, ym_ref, True)


def face_z_kernel(zp_ref, zm_ref, xp_ref, xm_ref, op_ref, om_ref):
    lanes = lane_index(8)
    subs = lax.broadcasted_iota(jnp.int32, (8, LANES), 0)
    for ref, out, c, edge in ((zp_ref, op_ref, 2, LANES - 1), (zm_ref, om_ref, 0, 0)):
        parts = [ref[0:8, :], ref[8:16, :], ref[16:24, :]]
        for ghost, a, p in ((xp_ref, 2, 0), (xm_ref, 0, SLABS - 1)):
            for b in range(3):
                j = 3 * a + b
                first = (3 * b + c) * ROWS
                for half in range(2):
                    column = turn(ghost[first + half * 8 : first + half * 8 + 8, :], 16 * p + j - edge)
                    parts[half] = jnp.where(lanes == 16 * p + j, column, parts[half])
                if b != 1:
                    q = ROWS - 1 if b == 2 else 0
                    row = jnp.broadcast_to(ghost[first + q : first + q + 1, :], (8, LANES))
                    here = jnp.logical_and(lanes == j, subs == p)
                    parts[2] = jnp.where(here, turn(row, j - edge), parts[2])
        for k in range(3):
            out[k * 8 : k * 8 + 8, :] = parts[k]


def move_x_kernel(state_ref, zp_ref, zm_ref, xp_ref, xm_ref, op_ref, om_ref, out_ref):
    face_z_kernel(zp_ref, zm_ref, xp_ref, xm_ref, op_ref, om_ref)
    long = TILES - ROWS
    for k in range(9):
        for a, ghost, at, to, start in ((2, xp_ref, 0, ROWS, 0), (0, xm_ref, long, 0, ROWS)):
            first = (9 * a + k) * TILES
            out_ref[pl.ds(first + to, long), :] = state_ref[pl.ds(first + start, long), :]
            out_ref[pl.ds(first + at, ROWS), :] = ghost[pl.ds(k * ROWS, ROWS), :]
    middle = pl.ds(9 * TILES, 9 * TILES)
    out_ref[middle, :] = state_ref[middle, :]


def face_y_moved_kernel(state_ref, zp_ref, zm_ref, op_ref, om_ref):
    lanes = lane_index(8)
    zp, zm = zp_ref[16:24, :], zm_ref[16:24, :]
    for out, b, q in ((op_ref, 2, ROWS - 1), (om_ref, 0, 0)):
        for a in range(3):
            j = 3 * a + b
            for c in range(3):
                value = state_ref[pl.ds((9 * a + 3 * b + c) * TILES + q, 8, stride=ROWS), :]
                low = turn(zp, -j) if c == 2 else None
                high = turn(zm, LANES - 1 - j) if c == 0 else None
                out[pl.ds((3 * a + c) * 8, 8), :] = move_z(value, c, low, high, lanes)


def face_y_last_kernel(yp_ref, ym_ref, xp_ref, xm_ref, zp_ref, zm_ref, op_ref, om_ref):
    lanes = lane_index(8)
    subs = lax.broadcasted_iota(jnp.int32, (8, LANES), 0)
    zp, zm = zp_ref[16:24, :], zm_ref[16:24, :]
    for ref, out, b, q in ((yp_ref, op_ref, 2, ROWS - 1), (ym_ref, om_ref, 0, 0)):
        for a in range(3):
            j = 3 * a + b
            for c in range(3):
                place = pl.ds((3 * a + c) * 8, 8)
                value = ref[place, :]
                if a != 1:
                    ghost = xp_ref if a == 2 else xm_ref
                    spot = (3 * b + c) * ROWS + q
                    row = jnp.broadcast_to(ghost[spot : spot + 1, :], (8, LANES))
                    value = pltpu.roll(value, 1 if a == 2 else 7, 0)
                    value = jnp.where(subs == (0 if a == 2 else SLABS - 1), row, value)
                low = turn(zp, -j) if c == 2 else None
                high = turn(zm, LANES - 1 - j) if c == 0 else None
                out[place, :] = move_z(value, c, low, high, lanes)


def stream_moved_kernel(source, zp_ref, zm_ref, out_ref):
    stream_first_kernel(source, None, None, zp_ref, zm_ref, out_ref)


def stream_first_kernel(source, xp_ref, xm_ref, zp_ref, zm_ref, out_ref):
    lanes = lane_index(ROWS)

    def step(p, carry):
        back = lax.rem(LANES - 16 * p, LANES)
        zp = turn(zp_ref[0:16, :], back)
        zm = turn(zm_ref[0:16, :], back)
        for a in range(3):
            origin = jnp.maximum(p - 1, 0) if a == 2 else jnp.minimum(p + 1, SLABS - 1)
            if a == 1 or xp_ref is None:
                origin = p
            for b in range(3):
                j = 3 * a + b
                for c in range(3):
                    i = 9 * a + 3 * b + c
                    value = source[pl.ds(pl.multiple_of(i * TILES + origin * ROWS, ROWS), ROWS), :]
                    place = pl.ds((3 * b + c) * ROWS, ROWS)
                    if a == 2 and xp_ref is not None:
                        value = jnp.where(p == 0, xp_ref[place, :], value)
                    if a == 0 and xm_ref is not None:
                        value = jnp.where(p == SLABS - 1, xm_ref[place, :], value)
                    low = turn(zp, -j) if c == 2 else None
                    high = turn(zm, LANES - 1 - j) if c == 0 else None
                    value = move_z(value, c, low, high, lanes)
                    if b != 1:
                        value = pltpu.roll(value, 1 if b == 2 else ROWS - 1, 0)
                    out_ref[pl.ds(pl.multiple_of(i * TILES + p * ROWS, ROWS), ROWS), :] = value
        return carry

    lax.fori_loop(0, SLABS, step, 0)


def fill(tiles, state_ref, first, ghost_ref=None, slab=None):
    for k in range(9):
        tiles[pl.ds(k * WIDE, TILES), :] = state_ref[pl.ds((first + k) * TILES, TILES), :]
        if ghost_ref is not None:
            tiles[pl.ds(k * WIDE + slab * ROWS, ROWS), :] = ghost_ref[pl.ds(k * ROWS, ROWS), :]


def pack(tiles, table_ref, sent, first=0, last=None):
    def step(r, carry):
        for j in range(2):
            tile = jnp.maximum(table_ref[j, r], 0)
            most = tiles[pl.ds(tile, 8, stride=WIDE), :]
            last = tiles[pl.ds(8 * WIDE + tile, 1), :]
            sent[pl.ds(r * CHUNK + j, 8, stride=2), :] = most
            sent[pl.ds(r * CHUNK + 16 + j, 1), :] = last
        return carry

    lax.fori_loop(first, PEERS if last is None else last, step, 0, unroll=4)


def pack_halves(tiles, table_ref, sent, sent_hbm, *semaphores):
    middle = PEERS // 2
    copies = []
    for (first, last), semaphore in zip(((0, middle), (middle, PEERS)), semaphores):
        pack(tiles, table_ref, sent, first, last)
        rows = pl.ds(first * CHUNK, (last - first) * CHUNK)
        copies.append(fetch(sent.at[rows], sent_hbm.at[rows], semaphore))
    return copies


def install(tiles, table_ref, received_ref):
    def step(r, carry):
        moved = []
        for j in range(2):
            tile = table_ref[j, r]
            tile = jnp.where(tile < 0, TILES, tile)
            most = received_ref[pl.ds(r * CHUNK + j, 8, stride=2), :]
            last = received_ref[pl.ds(r * CHUNK + 16 + j, 1), :]
            moved.append((tile, most, last))
        for tile, most, last in moved:
            tiles[pl.ds(tile, 8, stride=WIDE), :] = most
            tiles[pl.ds(8 * WIDE + tile, 1), :] = last
        return carry

    lax.fori_loop(0, PEERS, step, 0, unroll=4)


def move_z(value, c, low_ghost, high_ghost, lanes):
    if c == 2:
        return jnp.where(lanes == 0, low_ghost, turn(value, 1))
    if c == 0:
        return jnp.where(lanes == LANES - 1, high_ghost, turn(value, LANES - 1))
    return value


def move_y(value, b, ghost, rows):
    if b == 2:
        return jnp.where(rows == 0, ghost, pltpu.roll(value, 1, 0))
    if b == 0:
        return jnp.where(rows == ROWS - 1, ghost, pltpu.roll(value, ROWS - 1, 0))
    return value


def stream_kernel(source, yp_ref, ym_ref, zp_ref, zm_ref, out_ref):
    lanes = lane_index(ROWS)
    rows = lax.broadcasted_iota(jnp.int32, (ROWS, LANES), 0)

    def step(p, carry):
        for a in range(3):
            origin = p if a == 1 else (jnp.maximum(p - 1, 0) if a == 2 else jnp.minimum(p + 1, SLABS - 1))
            back = lax.rem(LANES - 16 * origin, LANES)
            zp = turn(zp_ref[0:16, :], back)
            zm = turn(zm_ref[0:16, :], back)
            for b in range(3):
                j = 3 * a + b
                for c in range(3):
                    i = 9 * a + 3 * b + c
                    value = source[pl.ds(pl.multiple_of(i * TILES + origin * ROWS, ROWS), ROWS), :]
                    spot = pl.ds((3 * a + c) * 8 + origin, 1)
                    ghost = yp_ref[spot, :] if b == 2 else ym_ref[spot, :]
                    value = move_y(value, b, ghost, rows)
                    low = turn(zp, -j) if c == 2 else None
                    high = turn(zm, LANES - 1 - j) if c == 0 else None
                    value = move_z(value, c, low, high, lanes)
                    out_ref[pl.ds(pl.multiple_of(i * TILES + p * ROWS, ROWS), ROWS), :] = value
        return carry

    lax.fori_loop(0, SLABS, step, 0)


def coarse_ends_kernel(state_hbm, rates_hbm, *refs):
    outs, rest_ref, tiles = refs[:3], refs[3], refs[4]
    state, rates, semaphores = refs[5:]
    pieces = [
        fetch(state_hbm.at[:, pl.ds(0, ROWS), :], state.at[:, pl.ds(0, ROWS), :], semaphores.at[0]),
        fetch(
            state_hbm.at[:, pl.ds(TILES - ROWS, ROWS), :], state.at[:, pl.ds(ROWS, ROWS), :], semaphores.at[1]
        ),
        fetch(rates_hbm, rates, semaphores.at[2]),
    ]
    others = [fetch(state_hbm.at[:, pl.ds(ROWS, TILES - 2 * ROWS), :], rest_ref, semaphores.at[3])]
    wait(pieces)

    def load(i, u):
        return state[i, pl.ds(pl.multiple_of(lax.rem(u, 4) * 8, 8), 8), :]

    collide_ends(load, None, rates, *outs)
    wait(others)
    for k in range(9):
        tiles[pl.ds(k * WIDE, ROWS), :] = state[18 + k, 0:ROWS, :]
        tiles[pl.ds(k * WIDE + ROWS, TILES - 2 * ROWS), :] = rest_ref[18 + k]
        tiles[pl.ds(k * WIDE + TILES - ROWS, ROWS), :] = state[18 + k, ROWS : 2 * ROWS, :]


def coarse_rest_kernel(state_ref, rates_hbm, ends_ref, *refs):
    outs = refs[:5]
    rates, semaphores = refs[5:]
    fetch(rates_hbm, rates, semaphores.at[0]).wait()

    def load(i, u):
        return state_ref[i, pl.ds(pl.multiple_of((u - 2) * 8, 8), 8), :]

    collide_rest(load, None, rates, ends_ref, *outs)


def old_kernel(tiles, table_hbm, sent_hbm, table, sent, semaphores):
    fetch(table_hbm, table, semaphores.at[0]).wait()
    wait(pack_halves(tiles, table, sent, sent_hbm, semaphores.at[1], semaphores.at[2]))


def tile8(tiles, k, u):
    return tiles[pl.ds(pl.multiple_of(k * WIDE + u * 8, 8), 8), :]


def fine_rows_kernel(state_hbm, flags_hbm, rates_hbm, table_hbm, received_ref, *refs):
    tiles, state, yp_ref, ym_ref, flags, rates, table, chunks, semaphores = refs
    pieces = [
        fetch(
            state_hbm.at[pl.ds((18 + k) * TILES, TILES)], tiles.at[pl.ds(k * WIDE, TILES)], chunks.at[k]
        )
        for k in range(9)
    ]
    pieces.append(fetch(table_hbm, table, semaphores.at[0]))
    others = [
        fetch(state_hbm.at[pl.ds(0, 18 * TILES)], state, semaphores.at[1]),
        fetch(flags_hbm, flags, semaphores.at[2]),
        fetch(rates_hbm, rates, semaphores.at[3]),
    ]
    wait(pieces)
    install(tiles, table, received_ref)
    wait(others)
    for ref, b, q in ((yp_ref, 2, ROWS - 1), (ym_ref, 0, 0)):
        values = []
        for i in range(27):
            first = (i - 18) * WIDE if i >= 18 else i * TILES
            values.append((tiles if i >= 18 else state)[pl.ds(first + q, 8, stride=ROWS), :])
        result = relax(values, rates)
        solid = flags[pl.ds(q, 8, stride=ROWS), :] == 1
        for a in range(3):
            for c in range(3):
                i = 9 * a + 3 * b + c
                ref[pl.ds((3 * a + c) * 8, 8), :] = jnp.where(solid, values[26 - i], result[i])


def fine_all_kernel(tiles, state_ref, flags_hbm, rates_hbm, *refs):
    out_ref, zp_ref, zm_ref, xp_ref, xm_ref, flags, rates, semaphores = refs
    wait([fetch(flags_hbm, flags, semaphores.at[0]), fetch(rates_hbm, rates, semaphores.at[1])])

    def load(i, u):
        return tile8(tiles, i - 18, u) if i >= 18 else load8(state_ref, i, u)

    def step(u, carry):
        collide_at(load, flags, rates, store8(out_ref), u)
        return carry

    lax.fori_loop(0, 2 * SLABS, step, 0, unroll=2)
    pack_z(out_ref, zp_ref, zm_ref, False)
    for j in range(9):
        xp_ref[pl.ds(j * ROWS, ROWS), :] = out_ref[pl.ds((18 + j) * TILES + 7 * ROWS, ROWS), :]
        xm_ref[pl.ds(j * ROWS, ROWS), :] = out_ref[pl.ds(j * TILES, ROWS), :]


def face_z_after_y_kernel(zp_ref, zm_ref, yp_ref, ym_ref, op_ref, om_ref):
    lanes = lane_index(ROWS)
    rows = lax.broadcasted_iota(jnp.int32, (ROWS, LANES), 0)
    j_of = lax.bitwise_and(lanes, 15)
    up = jnp.logical_or(jnp.logical_or(j_of == 2, j_of == 5), j_of == 8)
    down = jnp.logical_or(jnp.logical_or(j_of == 0, j_of == 3), j_of == 6)
    small = lane_index(8)
    slab = lax.broadcasted_iota(jnp.int32, (8, LANES), 0) * 16
    for ref, out, c, edge in ((zp_ref, op_ref, 2, LANES - 1), (zm_ref, om_ref, 0, 0)):
        packed = ref[0:16, :]
        value = jnp.where(up, pltpu.roll(packed, 1, 0), packed)
        value = jnp.where(down, pltpu.roll(packed, ROWS - 1, 0), value)
        for ghost, b, q, lane_set in ((yp_ref, 2, 0, up), (ym_ref, 0, ROWS - 1, down)):
            spread = jnp.zeros((8, LANES), jnp.float32)
            for a in range(3):
                j = 3 * a + b
                column = ghost[pl.ds((3 * a + c) * 8, 8), :]
                column = pltpu.roll(column, (j - edge) % LANES, 1, stride=16, stride_axis=0)
                spread = jnp.where(small == slab + j, column, spread)
            row = jnp.sum(spread, axis=0, keepdims=True)
            here = jnp.logical_and(lane_set, rows == q)
            value = jnp.where(here, jnp.broadcast_to(row, (ROWS, LANES)), value)
        out[0:16, :] = value
        out[16:24, :] = jnp.zeros((8, LANES), jnp.float32)


def face_x_after_z_kernel(xp_ref, xm_ref, yp_ref, ym_ref, zp_ref, zm_ref, op_ref, om_ref):
    lanes = lane_index(ROWS)
    rows = lax.broadcasted_iota(jnp.int32, (ROWS, LANES), 0)
    zp, zm = zp_ref[0:16, :], zm_ref[0:16, :]
    for ref, out, a, p in ((xp_ref, op_ref, 2, SLABS - 1), (xm_ref, om_ref, 0, 0)):
        for b in range(3):
            j = 3 * a + b
            for c in range(3):
                place = pl.ds((3 * b + c) * ROWS, ROWS)
                spot = pl.ds((3 * a + c) * 8 + p, 1)
                ghost = yp_ref[spot, :] if b == 2 else ym_ref[spot, :]
                value = move_y(ref[place, :], b, ghost, rows)
                low = turn(zp, -(16 * p + j)) if c == 2 else None
                high = turn(zm, LANES - 1 - 16 * p - j) if c == 0 else None
                out[place, :] = move_z(value, c, low, high, lanes)


def fine_ends_kernel(state_ref, xp_ref, xm_ref, received_ref, flags_hbm, rates_hbm, table_hbm, *refs):
    tiles, outs = refs[0], refs[1:4]
    flags, rates, table, semaphores = refs[4:]
    first = fetch(table_hbm, table, semaphores.at[0])
    others = [fetch(flags_hbm, flags, semaphores.at[1]), fetch(rates_hbm, rates, semaphores.at[2])]
    fill(tiles, state_ref, 18, xp_ref, 0)
    first.wait()
    install(tiles, table, received_ref)
    wait(others)

    def load(i, u):
        if i >= 18:
            return tile8(tiles, i - 18, u)
        value = load8(state_ref, i, u)
        if i < 9:
            ghost = xm_ref[pl.ds(pl.multiple_of(i * ROWS + lax.rem(u, 2) * 8, 8), 8), :]
            value = jnp.where(u >= 2 * SLABS - 2, ghost, value)
        return value

    collide_ends(load, flags, rates, *outs)


def fine_rest_kernel(state_ref, tiles_ref, flags_hbm, rates_hbm, ends_ref, *refs):
    outs = refs[:5]
    flags, rates, semaphores = refs[5:]
    wait([fetch(flags_hbm, flags, semaphores.at[0]), fetch(rates_hbm, rates, semaphores.at[1])])

    def load(i, u):
        return tile8(tiles_ref, i - 18, u) if i >= 18 else load8(state_ref, i, u)

    collide_rest(load, flags, rates, ends_ref, *outs)


def finish(state_ref, yp_ref, ym_ref, whole):
    whole[...] = state_ref[...]
    for i in range(27):
        a, b, c = i // 9, (i // 3) % 3, i % 3
        if b != 1:
            ghost, q = (yp_ref, 0) if b == 2 else (ym_ref, ROWS - 1)
            whole[pl.ds(i * TILES + q, 8, stride=ROWS), :] = ghost[pl.ds((3 * a + c) * 8, 8), :]


def mean_kernel(state_ref, yp_ref, ym_ref, old_hbm, table_hbm, sent_hbm, whole, *scratch):
    old, table, tiles, sent, semaphores = scratch
    second = fetch(old_hbm.at[pl.ds(18 * TILES, 9 * TILES)], old, semaphores.at[0])
    first = fetch(table_hbm, table, semaphores.at[1])
    finish(state_ref, yp_ref, ym_ref, whole)
    second.wait()
    for k in range(9):
        new = whole[pl.ds((18 + k) * TILES, TILES), :]
        tiles[pl.ds(k * WIDE, TILES), :] = 0.5 * (old[pl.ds(k * TILES, TILES), :] + new)
    first.wait()
    wait(pack_halves(tiles, table, sent, sent_hbm, semaphores.at[2], semaphores.at[3]))


def write_kernel(state_ref, kept_ref, out_hbm, semaphores):
    copy = fetch(state_ref, out_hbm, semaphores.at[0])
    kept_ref[...] = state_ref[pl.ds(0, 9 * TILES), :]
    copy.wait()


def up_kernel(state_ref, yp_ref, ym_ref, table_hbm, sent_ref, out_hbm, *scratch):
    whole, table, tiles, semaphores = scratch
    first = fetch(table_hbm, table, semaphores.at[0])
    finish(state_ref, yp_ref, ym_ref, whole)
    copy = fetch(whole, out_hbm, semaphores.at[1])
    fill(tiles, whole, 0)
    first.wait()
    pack(tiles, table, sent_ref)
    copy.wait()


def coarse_install_kernel(whole_hbm, kept_ref, received_ref, table_hbm, out_hbm, *scratch):
    table, tiles, semaphores, stores = scratch
    first = fetch(table_hbm, table, semaphores.at[0])
    for k in range(9):
        tiles[pl.ds(k * WIDE, TILES), :] = kept_ref[pl.ds(k * TILES, TILES), :]
    first.wait()
    install(tiles, table, received_ref)
    wait(
        [
            fetch(tiles.at[pl.ds(k * WIDE, TILES)], out_hbm.at[pl.ds(k * TILES, TILES)], stores.at[k])
            for k in range(9)
        ]
    )


STATE = (27 * TILES, LANES)
MESSAGE = (PEERS * CHUNK, LANES)
Z_FACE = (24, LANES)
Y_FACE = (9 * 8, LANES)
X_FACE = (9 * ROWS, LANES)
WIDE_TILES = (9 * WIDE, LANES)
NINE = (9 * TILES, LANES)
ENDS = (27 * 2 * ROWS, LANES)
REST = (STATE, Z_FACE, Z_FACE, Y_FACE, Y_FACE)


def floats(*shape):
    return pltpu.VMEM(shape, jnp.float32)


def copies(count):
    return pltpu.SemaphoreType.DMA((count,))


FLAGS = pltpu.VMEM((TILES, LANES), jnp.int32)
RATES = pltpu.SMEM((27,), jnp.float32)
TABLE = pltpu.SMEM((2, PEERS), jnp.int32)


def run(kernel, name, spaces, shapes, *operands, scratch=(), alias=False, microseconds=1.0):
    spots = {"v": pltpu.VMEM, "h": pltpu.HBM}
    given, made = spaces.split(":")
    operands = [
        pltpu.with_memory_space_constraint(operand, pltpu.HBM) if space == "h" else operand
        for operand, space in zip(operands, given)
    ]
    return pl.pallas_call(
        kernel,
        name=name,
        out_shape=tuple(jax.ShapeDtypeStruct(shape, jnp.float32) for shape in shapes),
        in_specs=[pl.BlockSpec(memory_space=spots[space]) for space in given],
        out_specs=tuple(pl.BlockSpec(memory_space=spots[space]) for space in made),
        scratch_shapes=list(scratch),
        input_output_aliases={0: 0} if alias else {},
        compiler_params=pltpu.CompilerParams(vmem_limit_bytes=VMEM_BYTES),
        cost_estimate=pl.CostEstimate(
            flops=0, bytes_accessed=int(microseconds * 3.0e6), transcendentals=0
        ),
    )(*operands)


def swap(axis, plus, minus):
    count = lax.axis_size(axis)
    up = [(i, (i + 1) % count) for i in range(count)]
    down = [(i, (i - 1) % count) for i in range(count)]
    return lax.ppermute(plus, axis, up), lax.ppermute(minus, axis, down)


def halo_y_first(yp, ym, rest, beside):
    yp, ym = swap("gy", yp, ym)
    collided, zp, zm, xp, xm = rest()
    zp, zm = run(face_z_after_y_kernel, "face_z", "vvvv:vv", (Z_FACE, Z_FACE), zp, zm, yp, ym)
    zp, zm, xp = beside(zp, zm, xp)
    zp, zm = swap("gz", zp, zm)
    xp, xm = run(face_x_after_z_kernel, "face_x", "vvvvvv:vv", (X_FACE, X_FACE), xp, xm, yp, ym, zp, zm)
    xp, xm = swap("gx", xp, xm)
    (moved,) = run(
        stream_kernel, "stream", "vvvvv:v", (STATE,), collided, yp, ym, zp, zm, microseconds=2.0
    )
    return moved, xp, xm


def halo_x_first(xp, xm, rest):
    xp, xm = swap("gx", xp, xm)
    collided, zp, zm, yp, ym = rest()
    zp, zm = run(face_z_kernel, "face_z", "vvvv:vv", (Z_FACE, Z_FACE), zp, zm, xp, xm)
    zp, zm = swap("gz", zp, zm)
    yp, ym = run(face_y_last_kernel, "face_y", "vvvvvv:vv", (Y_FACE, Y_FACE), yp, ym, xp, xm, zp, zm)
    return yp, ym, (collided, xp, xm, zp, zm)


def halo_moved(xp, xm, rest, between):
    xp, xm = swap("gx", xp, xm)
    collided, zp, zm, _, _ = rest()
    zp, zm, moved = run(
        move_x_kernel, "move_x", "vvvvv:vvv", (Z_FACE, Z_FACE, STATE), collided, zp, zm, xp, xm
    )
    zp, zm = between(zp, zm)
    zp, zm = swap("gz", zp, zm)
    yp, ym = run(face_y_moved_kernel, "face_y", "vvv:vv", (Y_FACE, Y_FACE), moved, zp, zm)
    yp, ym = swap("gy", yp, ym)
    (state,) = run(stream_moved_kernel, "stream", "vvv:v", (STATE,), moved, zp, zm, microseconds=2.0)
    return state, yp, ym


def stream_first(operands):
    return run(stream_first_kernel, "stream", "vvvvv:v", (STATE,), *operands, microseconds=2.0)[0]


def routed(message):
    chunks = message.reshape(PEERS, 9, 2, LANES)
    received = lax.all_to_all(chunks, ("gx", "gz"), split_axis=0, concat_axis=0, tiled=True)
    return received.reshape(MESSAGE)


def body(fine, coarse, fine_rates, coarse_rates, flags, down_source, down_target, up_source, up_target):
    fine = fine.reshape(STATE)
    coarse = coarse.reshape(STATE)
    flags = flags.reshape(TILES, LANES)
    down_source, down_target, up_source, up_target = (
        table.reshape(-1, 2).T for table in (down_source, down_target, up_source, up_target)
    )
    cube = coarse.reshape(27, TILES, LANES)
    ends, xp, xm, others, tiles = run(
        coarse_ends_kernel, "coarse_ends", "hh:vvvvv",
        (ENDS, X_FACE, X_FACE, (27, TILES - 2 * ROWS, LANES), WIDE_TILES), cube, coarse_rates,
        scratch=(floats(27, 2 * ROWS, LANES), RATES, copies(4)),
        microseconds=2.0,
    )

    def coarse_rest():
        return run(
            coarse_rest_kernel, "coarse_rest", "vhv:vvvvv", REST, others, coarse_rates, ends,
            scratch=(RATES, copies(1)),
            microseconds=3.0,
        )

    (sent_old,) = run(
        old_kernel, "pack_old", "vh:h", (MESSAGE,), tiles, down_source,
        scratch=(TABLE, floats(*MESSAGE), copies(3)),
        microseconds=1.0,
    )
    arrived = []

    def send_old(zp, zm):
        sent, zp, zm = lax.optimization_barrier((sent_old, zp, zm))
        arrived.append(routed(sent))
        return zp, zm

    moved, yp, ym = halo_moved(xp, xm, coarse_rest, send_old)
    (received,) = arrived
    sent_mean, coarse_moved = run(
        mean_kernel, "pack_mean", "vvvhh:hv", (MESSAGE, STATE), moved, yp, ym, coarse, down_source,
        scratch=(floats(*NINE), TABLE, floats(*WIDE_TILES), floats(*MESSAGE), copies(4)),
        microseconds=2.0,
    )
    mean = routed(sent_mean)
    tiles, others, yp, ym = run(
        fine_rows_kernel, "fine_rows", "hhhhv:vvvv", (WIDE_TILES, (18 * TILES, LANES), Y_FACE, Y_FACE),
        fine, flags, fine_rates, down_target, received,
        scratch=(FLAGS, RATES, TABLE, copies(9), copies(4)),
        microseconds=2.0,
    )

    def fine_all():
        return run(
            fine_all_kernel, "fine_all", "vvhh:vvvvv", (STATE, Z_FACE, Z_FACE, X_FACE, X_FACE),
            tiles, others, flags, fine_rates,
            scratch=(FLAGS, RATES, copies(2)),
            microseconds=3.0,
        )

    written = []

    def write_coarse(zp, zm, xp):
        state, zp, zm = lax.optimization_barrier((coarse_moved, zp, zm))
        kept, coarse_new = run(
            write_kernel, "coarse_write", "v:vh", (NINE, STATE), state, scratch=(copies(1),), microseconds=1.0
        )
        kept, coarse_new, xp = lax.optimization_barrier((kept, coarse_new, xp))
        written.extend((kept, coarse_new))
        return zp, zm, xp

    moved, xp, xm = halo_y_first(yp, ym, fine_all, write_coarse)
    kept, coarse_new = written
    tiles, ends, face_xp, face_xm = run(
        fine_ends_kernel, "fine_ends", "vvvvhhh:vvvv", (WIDE_TILES, ENDS, X_FACE, X_FACE),
        moved, xp, xm, mean, flags, fine_rates, down_target,
        scratch=(FLAGS, RATES, TABLE, copies(3)),
        microseconds=3.0,
    )

    def fine_rest():
        return run(
            fine_rest_kernel, "fine_rest", "vvhhv:vvvvv", REST, moved, tiles, flags, fine_rates, ends,
            scratch=(FLAGS, RATES, copies(2)),
            microseconds=3.0,
        )

    yp, ym, whole = halo_x_first(face_xp, face_xm, fine_rest)
    yp, ym = swap("gy", yp, ym)
    sent_up, fine_next = run(
        up_kernel, "pack_up", "vvvh:vh", (MESSAGE, STATE), stream_first(whole), yp, ym, up_source,
        scratch=(floats(*STATE), TABLE, floats(*WIDE_TILES), copies(2)),
        microseconds=2.0,
    )
    up = routed(sent_up)
    (coarse_next,) = run(
        coarse_install_kernel, "coarse_install", "hvvh:h", (STATE,), coarse_new, kept, up, up_target,
        scratch=(TABLE, floats(*WIDE_TILES), copies(1), copies(9)),
        alias=True,
        microseconds=2.0,
    )
    block = (27, SLABS, ROWS, LANES)
    return fine_next.reshape(block), coarse_next.reshape(block)


def solution(mesh):
    placed = (
        P(None, "gx", "gy", "gz"),
        P(None, "gx", "gy", "gz"),
        P(),
        P(),
        P("gx", "gy", "gz"),
        P("gx", "gy", "gz", None, None),
        P("gx", "gy", "gz", None, None),
        P("gx", "gy", "gz", None, None),
        P("gx", "gy", "gz", None, None),
    )
    return jax.shard_map(
        body,
        mesh=mesh,
        in_specs=placed,
        out_specs=(P(None, "gx", "gy", "gz"), P(None, "gx", "gy", "gz")),
        check_vma=False,
    )
```

```python
import jax
import jax.numpy as jnp
from jax import lax
from jax.experimental import pallas as pl
from jax.experimental.pallas import tpu as pltpu
from jax.sharding import PartitionSpec as P

SLABS = 8
ROWS = 16
LANES = 128
TILES = SLABS * ROWS
CHUNK = 18
PEERS = 64
VMEM_BYTES = 10 * 1024 * 1024
WIDE = 136


def load8(ref, i, u):
    return ref[pl.ds(pl.multiple_of(i * TILES + u * 8, 8), 8), :]


def fetch(source, target, semaphore):
    copy = pltpu.make_async_copy(source, target, semaphore)
    copy.start()
    return copy


def wait(copies):
    for copy in copies:
        copy.wait()


def forward(values):
    for step in (9, 3, 1):
        out = list(values)
        for i in range(27):
            if (i // step) % 3 == 0:
                low, mid, high = values[i], values[i + step], values[i + 2 * step]
                even = high + low
                out[i] = even + 4.0 * mid
                out[i + step] = high - low
                out[i + 2 * step] = even
        values = out
    return values


def backward(values):
    for step in (9, 3, 1):
        out = list(values)
        for i in range(27):
            if (i // step) % 3 == 0:
                zero, one, two = values[i], values[i + step], values[i + 2 * step]
                out[i] = two - one
                out[i + step] = zero - two
                out[i + 2 * step] = two + one
        values = out
    return values


def equilibrium(moments):
    density = moments[0]
    momentum = (moments[9], moments[3], moments[1])
    squares = [part * part * (1.0 / 72.0) for part in momentum]
    scale = (1.0, 1.0 / 3.0, 1.0 / 9.0, 1.0 / 27.0)
    result = []
    for k in range(27):
        powers = (k // 9, (k // 3) % 3, k % 3)
        ones = [axis for axis in range(3) if powers[axis] == 1]
        twos = [axis for axis in range(3) if powers[axis] == 2]
        if len(ones) == 0:
            value = density
            for axis in twos:
                value = value + squares[axis]
        elif len(ones) == 1:
            value = momentum[ones[0]]
        elif len(ones) == 2:
            value = momentum[ones[0]] * momentum[ones[1]] * (1.0 / 216.0)
        else:
            value = jnp.zeros_like(density)
        if twos:
            value = value * scale[len(twos)]
        result.append(value)
    return result


def relax(values, rates_ref):
    moments = forward(values)
    target = equilibrium(moments)
    change = backward([(rates_ref[k] * 0.125) * (target[k] - moments[k]) for k in range(27)])
    result = []
    for i in range(27):
        rests = sum(1 for part in (i // 9, (i // 3) % 3, i % 3) if part == 1)
        moved = change[i] if rests == 0 else change[i] * (0.5**rests)
        result.append(values[i] + moved)
    return result


def lane_index(rows):
    return lax.broadcasted_iota(jnp.int32, (rows, LANES), 1)


def turn(value, amount):
    amount = amount % LANES if isinstance(amount, int) else amount
    if isinstance(amount, int) and amount == 0:
        return value
    return pltpu.roll(value, amount, 1)


def collide_at(load, flags_ref, rates_ref, store, u):
    values = [load(i, u) for i in range(27)]
    result = relax(values, rates_ref)
    if flags_ref is not None:
        solid = flags_ref[pl.ds(pl.multiple_of(u * 8, 8), 8), :] == 1
        result = [jnp.where(solid, values[26 - i], result[i]) for i in range(27)]
    for i in range(27):
        store(i, u, result[i])


def store8(ref):
    def store(i, u, value):
        ref[pl.ds(pl.multiple_of(i * TILES + u * 8, 8), 8), :] = value

    return store


def pack_z(out_ref, zp_ref, zm_ref, shifted):
    lanes = lane_index(8)
    for ref, c, edge in ((zp_ref, 2, LANES - 1), (zm_ref, 0, 0)):
        for half in range(2):
            packed = jnp.zeros((8, LANES), jnp.float32)
            for p in range(SLABS):
                for j in range(9):
                    source = p - (j // 3 - 1) if shifted else p
                    if 0 <= source < SLABS:
                        start = (3 * j + c) * TILES + source * ROWS + half * 8
                        column = turn(out_ref[start : start + 8, :], 16 * p + j - edge)
                        packed = jnp.where(lanes == 16 * p + j, column, packed)
            ref[half * 8 : half * 8 + 8, :] = packed


def pack_y(out_ref, zp_ref, zm_ref, yp_ref, ym_ref, shifted):
    lanes = lane_index(8)
    ends = [jnp.zeros((8, LANES), jnp.float32), None, jnp.zeros((8, LANES), jnp.float32)]
    for ref, b, q in ((yp_ref, 2, ROWS - 1), (ym_ref, 0, 0)):
        for a in range(3):
            for c in range(3):
                i = 9 * a + 3 * b + c
                rows = out_ref[pl.ds(i * TILES + q, 8, stride=ROWS), :]
                ref[pl.ds((3 * a + c) * 8, 8), :] = rows
                j = 3 * a + b
                if c != 1:
                    edge = LANES - 1 if c == 2 else 0
                    if shifted and a != 1:
                        rows = pltpu.roll(rows, 1 if a == 2 else 7, 0)
                    ends[c] = jnp.where(lanes == j, turn(rows, j - edge), ends[c])
    zp_ref[16:24, :] = ends[2]
    zm_ref[16:24, :] = ends[0]


def collide_ends(load, flags_ref, rates_ref, ends_ref, xp_ref, xm_ref):
    def step(k, carry):
        def store(i, u, value):
            ends_ref[pl.ds(pl.multiple_of(i * 2 * ROWS + k * 8, 8), 8), :] = value

        collide_at(load, flags_ref, rates_ref, store, k + (2 * SLABS - 4) * (k // 2))
        return carry

    lax.fori_loop(0, 4, step, 0, unroll=2)
    for j in range(9):
        xp_ref[pl.ds(j * ROWS, ROWS), :] = ends_ref[pl.ds((18 + j) * 2 * ROWS + ROWS, ROWS), :]
        xm_ref[pl.ds(j * ROWS, ROWS), :] = ends_ref[pl.ds(j * 2 * ROWS, ROWS), :]


def collide_rest(load, flags_ref, rates_ref, ends_ref, out_ref, zp_ref, zm_ref, yp_ref, ym_ref):
    def step(u, carry):
        collide_at(load, flags_ref, rates_ref, store8(out_ref), u)
        return carry

    lax.fori_loop(2, 2 * SLABS - 2, step, 0, unroll=2)
    for i in range(27):
        out_ref[pl.ds(i * TILES, ROWS), :] = ends_ref[pl.ds(i * 2 * ROWS, ROWS), :]
        out_ref[pl.ds((i + 1) * TILES - ROWS, ROWS), :] = ends_ref[pl.ds(i * 2 * ROWS + ROWS, ROWS), :]
    pack_z(out_ref, zp_ref, zm_ref, True)
    pack_y(out_ref, zp_ref, zm_ref, yp_ref, ym_ref, True)


def face_z_kernel(zp_ref, zm_ref, xp_ref, xm_ref, op_ref, om_ref):
    lanes = lane_index(8)
    subs = lax.broadcasted_iota(jnp.int32, (8, LANES), 0)
    for ref, out, c, edge in ((zp_ref, op_ref, 2, LANES - 1), (zm_ref, om_ref, 0, 0)):
        parts = [ref[0:8, :], ref[8:16, :], ref[16:24, :]]
        for ghost, a, p in ((xp_ref, 2, 0), (xm_ref, 0, SLABS - 1)):
            for b in range(3):
                j = 3 * a + b
                first = (3 * b + c) * ROWS
                for half in range(2):
                    column = turn(ghost[first + half * 8 : first + half * 8 + 8, :], 16 * p + j - edge)
                    parts[half] = jnp.where(lanes == 16 * p + j, column, parts[half])
                if b != 1:
                    q = ROWS - 1 if b == 2 else 0
                    row = jnp.broadcast_to(ghost[first + q : first + q + 1, :], (8, LANES))
                    here = jnp.logical_and(lanes == j, subs == p)
                    parts[2] = jnp.where(here, turn(row, j - edge), parts[2])
        for k in range(3):
            out[k * 8 : k * 8 + 8, :] = parts[k]


def move_x_kernel(state_ref, zp_ref, zm_ref, xp_ref, xm_ref, op_ref, om_ref, out_ref):
    face_z_kernel(zp_ref, zm_ref, xp_ref, xm_ref, op_ref, om_ref)
    long = TILES - ROWS
    for k in range(9):
        for a, ghost, at, to, start in ((2, xp_ref, 0, ROWS, 0), (0, xm_ref, long, 0, ROWS)):
            first = (9 * a + k) * TILES
            out_ref[pl.ds(first + to, long), :] = state_ref[pl.ds(first + start, long), :]
            out_ref[pl.ds(first + at, ROWS), :] = ghost[pl.ds(k * ROWS, ROWS), :]
    middle = pl.ds(9 * TILES, 9 * TILES)
    out_ref[middle, :] = state_ref[middle, :]


def face_y_moved_kernel(state_ref, zp_ref, zm_ref, op_ref, om_ref):
    lanes = lane_index(8)
    zp, zm = zp_ref[16:24, :], zm_ref[16:24, :]
    for out, b, q in ((op_ref, 2, ROWS - 1), (om_ref, 0, 0)):
        for a in range(3):
            j = 3 * a + b
            for c in range(3):
                value = state_ref[pl.ds((9 * a + 3 * b + c) * TILES + q, 8, stride=ROWS), :]
                low = turn(zp, -j) if c == 2 else None
                high = turn(zm, LANES - 1 - j) if c == 0 else None
                out[pl.ds((3 * a + c) * 8, 8), :] = move_z(value, c, low, high, lanes)


def face_y_last_kernel(yp_ref, ym_ref, xp_ref, xm_ref, zp_ref, zm_ref, op_ref, om_ref):
    lanes = lane_index(8)
    subs = lax.broadcasted_iota(jnp.int32, (8, LANES), 0)
    zp, zm = zp_ref[16:24, :], zm_ref[16:24, :]
    for ref, out, b, q in ((yp_ref, op_ref, 2, ROWS - 1), (ym_ref, om_ref, 0, 0)):
        for a in range(3):
            j = 3 * a + b
            for c in range(3):
                place = pl.ds((3 * a + c) * 8, 8)
                value = ref[place, :]
                if a != 1:
                    ghost = xp_ref if a == 2 else xm_ref
                    spot = (3 * b + c) * ROWS + q
                    row = jnp.broadcast_to(ghost[spot : spot + 1, :], (8, LANES))
                    value = pltpu.roll(value, 1 if a == 2 else 7, 0)
                    value = jnp.where(subs == (0 if a == 2 else SLABS - 1), row, value)
                low = turn(zp, -j) if c == 2 else None
                high = turn(zm, LANES - 1 - j) if c == 0 else None
                out[place, :] = move_z(value, c, low, high, lanes)


def stream_moved_kernel(source, zp_ref, zm_ref, old_hbm, out_ref, old_ref, semaphores):
    copy = fetch(old_hbm.at[pl.ds(18 * TILES, 9 * TILES)], old_ref, semaphores.at[0])
    stream_first_kernel(source, None, None, zp_ref, zm_ref, out_ref)
    copy.wait()


def stream_first_kernel(source, xp_ref, xm_ref, zp_ref, zm_ref, out_ref):
    lanes = lane_index(ROWS)

    def step(p, carry):
        back = lax.rem(LANES - 16 * p, LANES)
        zp = turn(zp_ref[0:16, :], back)
        zm = turn(zm_ref[0:16, :], back)
        for a in range(3):
            origin = jnp.maximum(p - 1, 0) if a == 2 else jnp.minimum(p + 1, SLABS - 1)
            if a == 1 or xp_ref is None:
                origin = p
            for b in range(3):
                j = 3 * a + b
                for c in range(3):
                    i = 9 * a + 3 * b + c
                    value = source[pl.ds(pl.multiple_of(i * TILES + origin * ROWS, ROWS), ROWS), :]
                    place = pl.ds((3 * b + c) * ROWS, ROWS)
                    if a == 2 and xp_ref is not None:
                        value = jnp.where(p == 0, xp_ref[place, :], value)
                    if a == 0 and xm_ref is not None:
                        value = jnp.where(p == SLABS - 1, xm_ref[place, :], value)
                    low = turn(zp, -j) if c == 2 else None
                    high = turn(zm, LANES - 1 - j) if c == 0 else None
                    value = move_z(value, c, low, high, lanes)
                    if b != 1:
                        value = pltpu.roll(value, 1 if b == 2 else ROWS - 1, 0)
                    out_ref[pl.ds(pl.multiple_of(i * TILES + p * ROWS, ROWS), ROWS), :] = value
        return carry

    lax.fori_loop(0, SLABS, step, 0)


def fill(tiles, state_ref, first, ghost_ref=None, slab=None):
    for k in range(9):
        tiles[pl.ds(k * WIDE, TILES), :] = state_ref[pl.ds((first + k) * TILES, TILES), :]
        if ghost_ref is not None:
            tiles[pl.ds(k * WIDE + slab * ROWS, ROWS), :] = ghost_ref[pl.ds(k * ROWS, ROWS), :]


def pack(tiles, table_ref, sent, first=0, last=None):
    def step(r, carry):
        for j in range(2):
            tile = jnp.maximum(table_ref[j, r], 0)
            most = tiles[pl.ds(tile, 8, stride=WIDE), :]
            last = tiles[pl.ds(8 * WIDE + tile, 1), :]
            sent[pl.ds(r * CHUNK + j, 8, stride=2), :] = most
            sent[pl.ds(r * CHUNK + 16 + j, 1), :] = last
        return carry

    lax.fori_loop(first, PEERS if last is None else last, step, 0, unroll=4)


def pack_halves(tiles, table_ref, sent, sent_hbm, *semaphores):
    middle = PEERS // 2
    copies = []
    for (first, last), semaphore in zip(((0, middle), (middle, PEERS)), semaphores):
        pack(tiles, table_ref, sent, first, last)
        rows = pl.ds(first * CHUNK, (last - first) * CHUNK)
        copies.append(fetch(sent.at[rows], sent_hbm.at[rows], semaphore))
    return copies


def install(tiles, table_ref, received_ref):
    def step(r, carry):
        moved = []
        for j in range(2):
            tile = table_ref[j, r]
            tile = jnp.where(tile < 0, TILES, tile)
            most = received_ref[pl.ds(r * CHUNK + j, 8, stride=2), :]
            last = received_ref[pl.ds(r * CHUNK + 16 + j, 1), :]
            moved.append((tile, most, last))
        for tile, most, last in moved:
            tiles[pl.ds(tile, 8, stride=WIDE), :] = most
            tiles[pl.ds(8 * WIDE + tile, 1), :] = last
        return carry

    lax.fori_loop(0, PEERS, step, 0, unroll=4)


def move_z(value, c, low_ghost, high_ghost, lanes):
    if c == 2:
        return jnp.where(lanes == 0, low_ghost, turn(value, 1))
    if c == 0:
        return jnp.where(lanes == LANES - 1, high_ghost, turn(value, LANES - 1))
    return value


def move_y(value, b, ghost, rows):
    if b == 2:
        return jnp.where(rows == 0, ghost, pltpu.roll(value, 1, 0))
    if b == 0:
        return jnp.where(rows == ROWS - 1, ghost, pltpu.roll(value, ROWS - 1, 0))
    return value


def stream_kernel(source, yp_ref, ym_ref, zp_ref, zm_ref, out_ref):
    lanes = lane_index(ROWS)
    rows = lax.broadcasted_iota(jnp.int32, (ROWS, LANES), 0)

    def step(p, carry):
        for a in range(3):
            origin = p if a == 1 else (jnp.maximum(p - 1, 0) if a == 2 else jnp.minimum(p + 1, SLABS - 1))
            back = lax.rem(LANES - 16 * origin, LANES)
            zp = turn(zp_ref[0:16, :], back)
            zm = turn(zm_ref[0:16, :], back)
            for b in range(3):
                j = 3 * a + b
                for c in range(3):
                    i = 9 * a + 3 * b + c
                    value = source[pl.ds(pl.multiple_of(i * TILES + origin * ROWS, ROWS), ROWS), :]
                    spot = pl.ds((3 * a + c) * 8 + origin, 1)
                    ghost = yp_ref[spot, :] if b == 2 else ym_ref[spot, :]
                    value = move_y(value, b, ghost, rows)
                    low = turn(zp, -j) if c == 2 else None
                    high = turn(zm, LANES - 1 - j) if c == 0 else None
                    value = move_z(value, c, low, high, lanes)
                    out_ref[pl.ds(pl.multiple_of(i * TILES + p * ROWS, ROWS), ROWS), :] = value
        return carry

    lax.fori_loop(0, SLABS, step, 0)


def coarse_ends_kernel(state_hbm, rates_hbm, *refs):
    outs, rest_ref, tiles = refs[:3], refs[3], refs[4]
    state, rates, semaphores = refs[5:]
    pieces = [
        fetch(state_hbm.at[:, pl.ds(0, ROWS), :], state.at[:, pl.ds(0, ROWS), :], semaphores.at[0]),
        fetch(
            state_hbm.at[:, pl.ds(TILES - ROWS, ROWS), :], state.at[:, pl.ds(ROWS, ROWS), :], semaphores.at[1]
        ),
        fetch(rates_hbm, rates, semaphores.at[2]),
    ]
    others = [fetch(state_hbm.at[:, pl.ds(ROWS, TILES - 2 * ROWS), :], rest_ref, semaphores.at[3])]
    wait(pieces)

    def load(i, u):
        return state[i, pl.ds(pl.multiple_of(lax.rem(u, 4) * 8, 8), 8), :]

    collide_ends(load, None, rates, *outs)
    wait(others)
    for k in range(9):
        tiles[pl.ds(k * WIDE, ROWS), :] = state[18 + k, 0:ROWS, :]
        tiles[pl.ds(k * WIDE + ROWS, TILES - 2 * ROWS), :] = rest_ref[18 + k]
        tiles[pl.ds(k * WIDE + TILES - ROWS, ROWS), :] = state[18 + k, ROWS : 2 * ROWS, :]


def coarse_rest_kernel(state_ref, tiles, rates_hbm, table_hbm, ends_ref, *refs):
    outs, sent_hbm = refs[:5], refs[5]
    rates, table, sent, semaphores = refs[6:]
    wait([fetch(rates_hbm, rates, semaphores.at[0]), fetch(table_hbm, table, semaphores.at[1])])
    sends = pack_halves(tiles, table, sent, sent_hbm, semaphores.at[2], semaphores.at[3])

    def load(i, u):
        return state_ref[i, pl.ds(pl.multiple_of((u - 2) * 8, 8), 8), :]

    collide_rest(load, None, rates, ends_ref, *outs)
    wait(sends)


def tile8(tiles, k, u):
    return tiles[pl.ds(pl.multiple_of(k * WIDE + u * 8, 8), 8), :]


def fine_rows_kernel(state_hbm, flags_hbm, rates_hbm, table_hbm, received_ref, *refs):
    tiles, state, yp_ref, ym_ref, flags, rates, table, chunks, semaphores = refs
    pieces = [
        fetch(
            state_hbm.at[pl.ds((18 + k) * TILES, TILES)], tiles.at[pl.ds(k * WIDE, TILES)], chunks.at[k]
        )
        for k in range(9)
    ]
    pieces.append(fetch(table_hbm, table, semaphores.at[0]))
    others = [
        fetch(state_hbm.at[pl.ds(0, 18 * TILES)], state, semaphores.at[1]),
        fetch(flags_hbm, flags, semaphores.at[2]),
        fetch(rates_hbm, rates, semaphores.at[3]),
    ]
    wait(pieces)
    install(tiles, table, received_ref)
    wait(others)
    for ref, b, q in ((yp_ref, 2, ROWS - 1), (ym_ref, 0, 0)):
        values = []
        for i in range(27):
            first = (i - 18) * WIDE if i >= 18 else i * TILES
            values.append((tiles if i >= 18 else state)[pl.ds(first + q, 8, stride=ROWS), :])
        result = relax(values, rates)
        solid = flags[pl.ds(q, 8, stride=ROWS), :] == 1
        for a in range(3):
            for c in range(3):
                i = 9 * a + 3 * b + c
                ref[pl.ds((3 * a + c) * 8, 8), :] = jnp.where(solid, values[26 - i], result[i])


def fine_all_kernel(tiles, state_ref, flags_hbm, rates_hbm, *refs):
    out_ref, zp_ref, zm_ref, xp_ref, xm_ref, flags, rates, semaphores = refs
    wait([fetch(flags_hbm, flags, semaphores.at[0]), fetch(rates_hbm, rates, semaphores.at[1])])

    def load(i, u):
        return tile8(tiles, i - 18, u) if i >= 18 else load8(state_ref, i, u)

    def step(u, carry):
        collide_at(load, flags, rates, store8(out_ref), u)
        return carry

    lax.fori_loop(0, 2 * SLABS, step, 0, unroll=2)
    pack_z(out_ref, zp_ref, zm_ref, False)
    for j in range(9):
        xp_ref[pl.ds(j * ROWS, ROWS), :] = out_ref[pl.ds((18 + j) * TILES + 7 * ROWS, ROWS), :]
        xm_ref[pl.ds(j * ROWS, ROWS), :] = out_ref[pl.ds(j * TILES, ROWS), :]


def face_z_after_y_kernel(zp_ref, zm_ref, yp_ref, ym_ref, op_ref, om_ref):
    lanes = lane_index(ROWS)
    rows = lax.broadcasted_iota(jnp.int32, (ROWS, LANES), 0)
    j_of = lax.bitwise_and(lanes, 15)
    up = jnp.logical_or(jnp.logical_or(j_of == 2, j_of == 5), j_of == 8)
    down = jnp.logical_or(jnp.logical_or(j_of == 0, j_of == 3), j_of == 6)
    small = lane_index(8)
    slab = lax.broadcasted_iota(jnp.int32, (8, LANES), 0) * 16
    for ref, out, c, edge in ((zp_ref, op_ref, 2, LANES - 1), (zm_ref, om_ref, 0, 0)):
        packed = ref[0:16, :]
        value = jnp.where(up, pltpu.roll(packed, 1, 0), packed)
        value = jnp.where(down, pltpu.roll(packed, ROWS - 1, 0), value)
        for ghost, b, q, lane_set in ((yp_ref, 2, 0, up), (ym_ref, 0, ROWS - 1, down)):
            spread = jnp.zeros((8, LANES), jnp.float32)
            for a in range(3):
                j = 3 * a + b
                column = ghost[pl.ds((3 * a + c) * 8, 8), :]
                column = pltpu.roll(column, (j - edge) % LANES, 1, stride=16, stride_axis=0)
                spread = jnp.where(small == slab + j, column, spread)
            row = jnp.sum(spread, axis=0, keepdims=True)
            here = jnp.logical_and(lane_set, rows == q)
            value = jnp.where(here, jnp.broadcast_to(row, (ROWS, LANES)), value)
        out[0:16, :] = value
        out[16:24, :] = jnp.zeros((8, LANES), jnp.float32)


def face_x_after_z_kernel(xp_ref, xm_ref, yp_ref, ym_ref, zp_ref, zm_ref, op_ref, om_ref):
    lanes = lane_index(ROWS)
    rows = lax.broadcasted_iota(jnp.int32, (ROWS, LANES), 0)
    zp, zm = zp_ref[0:16, :], zm_ref[0:16, :]
    for ref, out, a, p in ((xp_ref, op_ref, 2, SLABS - 1), (xm_ref, om_ref, 0, 0)):
        for b in range(3):
            j = 3 * a + b
            for c in range(3):
                place = pl.ds((3 * b + c) * ROWS, ROWS)
                spot = pl.ds((3 * a + c) * 8 + p, 1)
                ghost = yp_ref[spot, :] if b == 2 else ym_ref[spot, :]
                value = move_y(ref[place, :], b, ghost, rows)
                low = turn(zp, -(16 * p + j)) if c == 2 else None
                high = turn(zm, LANES - 1 - 16 * p - j) if c == 0 else None
                out[place, :] = move_z(value, c, low, high, lanes)


def fine_ends_kernel(state_ref, xp_ref, xm_ref, received_ref, flags_hbm, rates_hbm, table_hbm, *refs):
    tiles, outs = refs[0], refs[1:4]
    flags, rates, table, semaphores = refs[4:]
    first = fetch(table_hbm, table, semaphores.at[0])
    others = [fetch(flags_hbm, flags, semaphores.at[1]), fetch(rates_hbm, rates, semaphores.at[2])]
    fill(tiles, state_ref, 18, xp_ref, 0)
    first.wait()
    install(tiles, table, received_ref)
    wait(others)

    def load(i, u):
        if i >= 18:
            return tile8(tiles, i - 18, u)
        value = load8(state_ref, i, u)
        if i < 9:
            ghost = xm_ref[pl.ds(pl.multiple_of(i * ROWS + lax.rem(u, 2) * 8, 8), 8), :]
            value = jnp.where(u >= 2 * SLABS - 2, ghost, value)
        return value

    collide_ends(load, flags, rates, *outs)


def fine_rest_kernel(state_ref, tiles_ref, flags_hbm, rates_hbm, ends_ref, *refs):
    outs = refs[:5]
    flags, rates, semaphores = refs[5:]
    wait([fetch(flags_hbm, flags, semaphores.at[0]), fetch(rates_hbm, rates, semaphores.at[1])])

    def load(i, u):
        return tile8(tiles_ref, i - 18, u) if i >= 18 else load8(state_ref, i, u)

    collide_rest(load, flags, rates, ends_ref, *outs)


def finish(state_ref, yp_ref, ym_ref, whole):
    whole[...] = state_ref[...]
    for i in range(27):
        a, b, c = i // 9, (i // 3) % 3, i % 3
        if b != 1:
            ghost, q = (yp_ref, 0) if b == 2 else (ym_ref, ROWS - 1)
            whole[pl.ds(i * TILES + q, 8, stride=ROWS), :] = ghost[pl.ds((3 * a + c) * 8, 8), :]


def mean_kernel(state_ref, yp_ref, ym_ref, old_ref, table_hbm, sent_hbm, whole, *scratch):
    table, tiles, sent, semaphores = scratch
    first = fetch(table_hbm, table, semaphores.at[0])
    finish(state_ref, yp_ref, ym_ref, whole)
    for k in range(9):
        new = whole[pl.ds((18 + k) * TILES, TILES), :]
        tiles[pl.ds(k * WIDE, TILES), :] = 0.5 * (old_ref[pl.ds(k * TILES, TILES), :] + new)
    first.wait()
    wait(pack_halves(tiles, table, sent, sent_hbm, semaphores.at[1], semaphores.at[2]))


def write_kernel(state_ref, kept_ref, out_hbm, semaphores):
    copy = fetch(state_ref, out_hbm, semaphores.at[0])
    kept_ref[...] = state_ref[pl.ds(0, 9 * TILES), :]
    copy.wait()


def up_kernel(state_ref, yp_ref, ym_ref, table_hbm, sent_ref, out_hbm, *scratch):
    whole, table, tiles, semaphores = scratch
    first = fetch(table_hbm, table, semaphores.at[0])
    finish(state_ref, yp_ref, ym_ref, whole)
    copy = fetch(whole, out_hbm, semaphores.at[1])
    fill(tiles, whole, 0)
    first.wait()
    pack(tiles, table, sent_ref)
    copy.wait()


def coarse_install_kernel(whole_hbm, kept_ref, received_ref, table_hbm, out_hbm, *scratch):
    table, tiles, semaphores, stores = scratch
    first = fetch(table_hbm, table, semaphores.at[0])
    for k in range(9):
        tiles[pl.ds(k * WIDE, TILES), :] = kept_ref[pl.ds(k * TILES, TILES), :]
    first.wait()
    install(tiles, table, received_ref)
    wait(
        [
            fetch(tiles.at[pl.ds(k * WIDE, TILES)], out_hbm.at[pl.ds(k * TILES, TILES)], stores.at[k])
            for k in range(9)
        ]
    )


STATE = (27 * TILES, LANES)
MESSAGE = (PEERS * CHUNK, LANES)
Z_FACE = (24, LANES)
Y_FACE = (9 * 8, LANES)
X_FACE = (9 * ROWS, LANES)
WIDE_TILES = (9 * WIDE, LANES)
NINE = (9 * TILES, LANES)
ENDS = (27 * 2 * ROWS, LANES)
REST = (STATE, Z_FACE, Z_FACE, Y_FACE, Y_FACE)


def floats(*shape):
    return pltpu.VMEM(shape, jnp.float32)


def copies(count):
    return pltpu.SemaphoreType.DMA((count,))


FLAGS = pltpu.VMEM((TILES, LANES), jnp.int32)
RATES = pltpu.SMEM((27,), jnp.float32)
TABLE = pltpu.SMEM((2, PEERS), jnp.int32)


def run(kernel, name, spaces, shapes, *operands, scratch=(), alias=False, microseconds=1.0):
    spots = {"v": pltpu.VMEM, "h": pltpu.HBM}
    given, made = spaces.split(":")
    operands = [
        pltpu.with_memory_space_constraint(operand, pltpu.HBM) if space == "h" else operand
        for operand, space in zip(operands, given)
    ]
    return pl.pallas_call(
        kernel,
        name=name,
        out_shape=tuple(jax.ShapeDtypeStruct(shape, jnp.float32) for shape in shapes),
        in_specs=[pl.BlockSpec(memory_space=spots[space]) for space in given],
        out_specs=tuple(pl.BlockSpec(memory_space=spots[space]) for space in made),
        scratch_shapes=list(scratch),
        input_output_aliases={0: 0} if alias else {},
        compiler_params=pltpu.CompilerParams(vmem_limit_bytes=VMEM_BYTES),
        cost_estimate=pl.CostEstimate(
            flops=0, bytes_accessed=int(microseconds * 3.0e6), transcendentals=0
        ),
    )(*operands)


def swap(axis, plus, minus):
    count = lax.axis_size(axis)
    up = [(i, (i + 1) % count) for i in range(count)]
    down = [(i, (i - 1) % count) for i in range(count)]
    return lax.ppermute(plus, axis, up), lax.ppermute(minus, axis, down)


def halo_y_first(yp, ym, rest, beside):
    yp, ym = swap("gy", yp, ym)
    collided, zp, zm, xp, xm = rest()
    zp, zm = run(face_z_after_y_kernel, "face_z", "vvvv:vv", (Z_FACE, Z_FACE), zp, zm, yp, ym)
    zp, zm, xp = beside(zp, zm, xp)
    zp, zm = swap("gz", zp, zm)
    xp, xm = run(face_x_after_z_kernel, "face_x", "vvvvvv:vv", (X_FACE, X_FACE), xp, xm, yp, ym, zp, zm)
    xp, xm = swap("gx", xp, xm)
    (moved,) = run(
        stream_kernel, "stream", "vvvvv:v", (STATE,), collided, yp, ym, zp, zm, microseconds=2.0
    )
    return moved, xp, xm


def halo_x_first(xp, xm, rest):
    xp, xm = swap("gx", xp, xm)
    collided, zp, zm, yp, ym = rest()
    zp, zm = run(face_z_kernel, "face_z", "vvvv:vv", (Z_FACE, Z_FACE), zp, zm, xp, xm)
    zp, zm = swap("gz", zp, zm)
    yp, ym = run(face_y_last_kernel, "face_y", "vvvvvv:vv", (Y_FACE, Y_FACE), yp, ym, xp, xm, zp, zm)
    return yp, ym, (collided, xp, xm, zp, zm)


def halo_moved(old, xp, xm, rest, between):
    xp, xm = swap("gx", xp, xm)
    collided, zp, zm, _, _ = rest()
    zp, zm, moved = run(
        move_x_kernel, "move_x", "vvvvv:vvv", (Z_FACE, Z_FACE, STATE), collided, zp, zm, xp, xm
    )
    zp, zm = between(zp, zm)
    zp, zm = swap("gz", zp, zm)
    yp, ym = run(face_y_moved_kernel, "face_y", "vvv:vv", (Y_FACE, Y_FACE), moved, zp, zm)
    yp, ym = swap("gy", yp, ym)
    state, old = run(
        stream_moved_kernel, "stream", "vvvh:vv", (STATE, NINE), moved, zp, zm, old,
        scratch=(copies(1),),
        microseconds=2.0,
    )
    return state, old, yp, ym


def stream_first(operands):
    return run(stream_first_kernel, "stream", "vvvvv:v", (STATE,), *operands, microseconds=2.0)[0]


def routed(message):
    chunks = message.reshape(PEERS, 9, 2, LANES)
    received = lax.all_to_all(chunks, ("gx", "gz"), split_axis=0, concat_axis=0, tiled=True)
    return received.reshape(MESSAGE)


def body(fine, coarse, fine_rates, coarse_rates, flags, down_source, down_target, up_source, up_target):
    fine = fine.reshape(STATE)
    coarse = coarse.reshape(STATE)
    flags = flags.reshape(TILES, LANES)
    down_source, down_target, up_source, up_target = (
        table.reshape(-1, 2).T for table in (down_source, down_target, up_source, up_target)
    )
    cube = coarse.reshape(27, TILES, LANES)
    ends, xp, xm, others, tiles = run(
        coarse_ends_kernel, "coarse_ends", "hh:vvvvv",
        (ENDS, X_FACE, X_FACE, (27, TILES - 2 * ROWS, LANES), WIDE_TILES), cube, coarse_rates,
        scratch=(floats(27, 2 * ROWS, LANES), RATES, copies(4)),
        microseconds=2.0,
    )

    packed = []

    def coarse_rest():
        *parts, sent_old = run(
            coarse_rest_kernel, "coarse_rest", "vvhhv:vvvvvh", REST + (MESSAGE,),
            others, tiles, coarse_rates, down_source, ends,
            scratch=(RATES, TABLE, floats(*MESSAGE), copies(4)),
            microseconds=4.0,
        )
        packed.append(sent_old)
        return parts

    arrived = []

    def send_old(zp, zm):
        sent, zp, zm = lax.optimization_barrier((packed[0], zp, zm))
        arrived.append(routed(sent))
        return zp, zm

    moved, old, yp, ym = halo_moved(coarse, xp, xm, coarse_rest, send_old)
    (received,) = arrived
    sent_mean, coarse_moved = run(
        mean_kernel, "pack_mean", "vvvvh:hv", (MESSAGE, STATE), moved, yp, ym, old, down_source,
        scratch=(TABLE, floats(*WIDE_TILES), floats(*MESSAGE), copies(3)),
        microseconds=2.0,
    )
    mean = routed(sent_mean)
    tiles, others, yp, ym = run(
        fine_rows_kernel, "fine_rows", "hhhhv:vvvv", (WIDE_TILES, (18 * TILES, LANES), Y_FACE, Y_FACE),
        fine, flags, fine_rates, down_target, received,
        scratch=(FLAGS, RATES, TABLE, copies(9), copies(4)),
        microseconds=2.0,
    )

    def fine_all():
        return run(
            fine_all_kernel, "fine_all", "vvhh:vvvvv", (STATE, Z_FACE, Z_FACE, X_FACE, X_FACE),
            tiles, others, flags, fine_rates,
            scratch=(FLAGS, RATES, copies(2)),
            microseconds=3.0,
        )

    written = []

    def write_coarse(zp, zm, xp):
        state, zp, zm = lax.optimization_barrier((coarse_moved, zp, zm))
        kept, coarse_new = run(
            write_kernel, "coarse_write", "v:vh", (NINE, STATE), state, scratch=(copies(1),), microseconds=1.0
        )
        kept, coarse_new, xp = lax.optimization_barrier((kept, coarse_new, xp))
        written.extend((kept, coarse_new))
        return zp, zm, xp

    moved, xp, xm = halo_y_first(yp, ym, fine_all, write_coarse)
    kept, coarse_new = written
    tiles, ends, face_xp, face_xm = run(
        fine_ends_kernel, "fine_ends", "vvvvhhh:vvvv", (WIDE_TILES, ENDS, X_FACE, X_FACE),
        moved, xp, xm, mean, flags, fine_rates, down_target,
        scratch=(FLAGS, RATES, TABLE, copies(3)),
        microseconds=3.0,
    )

    def fine_rest():
        return run(
            fine_rest_kernel, "fine_rest", "vvhhv:vvvvv", REST, moved, tiles, flags, fine_rates, ends,
            scratch=(FLAGS, RATES, copies(2)),
            microseconds=3.0,
        )

    yp, ym, whole = halo_x_first(face_xp, face_xm, fine_rest)
    yp, ym = swap("gy", yp, ym)
    sent_up, fine_next = run(
        up_kernel, "pack_up", "vvvh:vh", (MESSAGE, STATE), stream_first(whole), yp, ym, up_source,
        scratch=(floats(*STATE), TABLE, floats(*WIDE_TILES), copies(2)),
        microseconds=2.0,
    )
    up = routed(sent_up)
    (coarse_next,) = run(
        coarse_install_kernel, "coarse_install", "hvvh:h", (STATE,), coarse_new, kept, up, up_target,
        scratch=(TABLE, floats(*WIDE_TILES), copies(1), copies(9)),
        alias=True,
        microseconds=2.0,
    )
    block = (27, SLABS, ROWS, LANES)
    return fine_next.reshape(block), coarse_next.reshape(block)


def solution(mesh):
    placed = (
        P(None, "gx", "gy", "gz"),
        P(None, "gx", "gy", "gz"),
        P(),
        P(),
        P("gx", "gy", "gz"),
        P("gx", "gy", "gz", None, None),
        P("gx", "gy", "gz", None, None),
        P("gx", "gy", "gz", None, None),
        P("gx", "gy", "gz", None, None),
    )
    return jax.shard_map(
        body,
        mesh=mesh,
        in_specs=placed,
        out_specs=(P(None, "gx", "gy", "gz"), P(None, "gx", "gy", "gz")),
        check_vma=False,
    )
```

```python
import jax
import jax.numpy as jnp
from jax import lax
from jax.experimental import pallas as pl
from jax.experimental.pallas import tpu as pltpu
from jax.sharding import PartitionSpec as P

SLABS = 8
ROWS = 16
LANES = 128
TILES = SLABS * ROWS
CHUNK = 18
PEERS = 64
VMEM_BYTES = 10 * 1024 * 1024
WIDE = 136


def load8(ref, i, u):
    return ref[pl.ds(pl.multiple_of(i * TILES + u * 8, 8), 8), :]


def fetch(source, target, semaphore):
    copy = pltpu.make_async_copy(source, target, semaphore)
    copy.start()
    return copy


def wait(copies):
    for copy in copies:
        copy.wait()


def forward(values):
    for step in (9, 3, 1):
        out = list(values)
        for i in range(27):
            if (i // step) % 3 == 0:
                low, mid, high = values[i], values[i + step], values[i + 2 * step]
                even = high + low
                out[i] = even + 4.0 * mid
                out[i + step] = high - low
                out[i + 2 * step] = even
        values = out
    return values


def backward(values):
    for step in (9, 3, 1):
        out = list(values)
        for i in range(27):
            if (i // step) % 3 == 0:
                zero, one, two = values[i], values[i + step], values[i + 2 * step]
                out[i] = two - one
                out[i + step] = zero - two
                out[i + 2 * step] = two + one
        values = out
    return values


def equilibrium(moments):
    density = moments[0]
    momentum = (moments[9], moments[3], moments[1])
    squares = [part * part * (1.0 / 72.0) for part in momentum]
    scale = (1.0, 1.0 / 3.0, 1.0 / 9.0, 1.0 / 27.0)
    result = []
    for k in range(27):
        powers = (k // 9, (k // 3) % 3, k % 3)
        ones = [axis for axis in range(3) if powers[axis] == 1]
        twos = [axis for axis in range(3) if powers[axis] == 2]
        if len(ones) == 0:
            value = density
            for axis in twos:
                value = value + squares[axis]
        elif len(ones) == 1:
            value = momentum[ones[0]]
        elif len(ones) == 2:
            value = momentum[ones[0]] * momentum[ones[1]] * (1.0 / 216.0)
        else:
            value = jnp.zeros_like(density)
        if twos:
            value = value * scale[len(twos)]
        result.append(value)
    return result


def relax(values, rates_ref):
    moments = forward(values)
    target = equilibrium(moments)
    change = backward([(rates_ref[k] * 0.125) * (target[k] - moments[k]) for k in range(27)])
    result = []
    for i in range(27):
        rests = sum(1 for part in (i // 9, (i // 3) % 3, i % 3) if part == 1)
        moved = change[i] if rests == 0 else change[i] * (0.5**rests)
        result.append(values[i] + moved)
    return result


def lane_index(rows):
    return lax.broadcasted_iota(jnp.int32, (rows, LANES), 1)


def turn(value, amount):
    amount = amount % LANES if isinstance(amount, int) else amount
    if isinstance(amount, int) and amount == 0:
        return value
    return pltpu.roll(value, amount, 1)


def collide_at(load, flags_ref, rates_ref, store, u):
    values = [load(i, u) for i in range(27)]
    result = relax(values, rates_ref)
    if flags_ref is not None:
        solid = flags_ref[pl.ds(pl.multiple_of(u * 8, 8), 8), :] == 1
        result = [jnp.where(solid, values[26 - i], result[i]) for i in range(27)]
    for i in range(27):
        store(i, u, result[i])


def store8(ref):
    def store(i, u, value):
        ref[pl.ds(pl.multiple_of(i * TILES + u * 8, 8), 8), :] = value

    return store


def pack_z(out_ref, zp_ref, zm_ref, shifted):
    lanes = lane_index(8)
    for ref, c, edge in ((zp_ref, 2, LANES - 1), (zm_ref, 0, 0)):
        for half in range(2):
            packed = jnp.zeros((8, LANES), jnp.float32)
            for p in range(SLABS):
                for j in range(9):
                    source = p - (j // 3 - 1) if shifted else p
                    if 0 <= source < SLABS:
                        start = (3 * j + c) * TILES + source * ROWS + half * 8
                        column = turn(out_ref[start : start + 8, :], 16 * p + j - edge)
                        packed = jnp.where(lanes == 16 * p + j, column, packed)
            ref[half * 8 : half * 8 + 8, :] = packed


def pack_y(out_ref, zp_ref, zm_ref, yp_ref, ym_ref, shifted):
    lanes = lane_index(8)
    ends = [jnp.zeros((8, LANES), jnp.float32), None, jnp.zeros((8, LANES), jnp.float32)]
    for ref, b, q in ((yp_ref, 2, ROWS - 1), (ym_ref, 0, 0)):
        for a in range(3):
            for c in range(3):
                i = 9 * a + 3 * b + c
                rows = out_ref[pl.ds(i * TILES + q, 8, stride=ROWS), :]
                ref[pl.ds((3 * a + c) * 8, 8), :] = rows
                j = 3 * a + b
                if c != 1:
                    edge = LANES - 1 if c == 2 else 0
                    if shifted and a != 1:
                        rows = pltpu.roll(rows, 1 if a == 2 else 7, 0)
                    ends[c] = jnp.where(lanes == j, turn(rows, j - edge), ends[c])
    zp_ref[16:24, :] = ends[2]
    zm_ref[16:24, :] = ends[0]


def collide_ends(load, flags_ref, rates_ref, ends_ref, xp_ref, xm_ref):
    def step(k, carry):
        def store(i, u, value):
            ends_ref[pl.ds(pl.multiple_of(i * 2 * ROWS + k * 8, 8), 8), :] = value

        collide_at(load, flags_ref, rates_ref, store, k + (2 * SLABS - 4) * (k // 2))
        return carry

    lax.fori_loop(0, 4, step, 0, unroll=2)
    for j in range(9):
        xp_ref[pl.ds(j * ROWS, ROWS), :] = ends_ref[pl.ds((18 + j) * 2 * ROWS + ROWS, ROWS), :]
        xm_ref[pl.ds(j * ROWS, ROWS), :] = ends_ref[pl.ds(j * 2 * ROWS, ROWS), :]


def collide_rest(load, flags_ref, rates_ref, ends_ref, out_ref, zp_ref, zm_ref, yp_ref, ym_ref):
    def step(u, carry):
        collide_at(load, flags_ref, rates_ref, store8(out_ref), u)
        return carry

    lax.fori_loop(2, 2 * SLABS - 2, step, 0, unroll=2)
    for i in range(27):
        out_ref[pl.ds(i * TILES, ROWS), :] = ends_ref[pl.ds(i * 2 * ROWS, ROWS), :]
        out_ref[pl.ds((i + 1) * TILES - ROWS, ROWS), :] = ends_ref[pl.ds(i * 2 * ROWS + ROWS, ROWS), :]
    pack_z(out_ref, zp_ref, zm_ref, True)
    pack_y(out_ref, zp_ref, zm_ref, yp_ref, ym_ref, True)


def face_z_kernel(zp_ref, zm_ref, xp_ref, xm_ref, op_ref, om_ref):
    lanes = lane_index(8)
    subs = lax.broadcasted_iota(jnp.int32, (8, LANES), 0)
    for ref, out, c, edge in ((zp_ref, op_ref, 2, LANES - 1), (zm_ref, om_ref, 0, 0)):
        parts = [ref[0:8, :], ref[8:16, :], ref[16:24, :]]
        for ghost, a, p in ((xp_ref, 2, 0), (xm_ref, 0, SLABS - 1)):
            for b in range(3):
                j = 3 * a + b
                first = (3 * b + c) * ROWS
                for half in range(2):
                    column = turn(ghost[first + half * 8 : first + half * 8 + 8, :], 16 * p + j - edge)
                    parts[half] = jnp.where(lanes == 16 * p + j, column, parts[half])
                if b != 1:
                    q = ROWS - 1 if b == 2 else 0
                    row = jnp.broadcast_to(ghost[first + q : first + q + 1, :], (8, LANES))
                    here = jnp.logical_and(lanes == j, subs == p)
                    parts[2] = jnp.where(here, turn(row, j - edge), parts[2])
        for k in range(3):
            out[k * 8 : k * 8 + 8, :] = parts[k]


def move_x_kernel(state_ref, zp_ref, zm_ref, xp_ref, xm_ref, op_ref, om_ref, out_ref):
    face_z_kernel(zp_ref, zm_ref, xp_ref, xm_ref, op_ref, om_ref)
    long = TILES - ROWS
    for k in range(9):
        for a, ghost, at, to, start in ((2, xp_ref, 0, ROWS, 0), (0, xm_ref, long, 0, ROWS)):
            first = (9 * a + k) * TILES
            out_ref[pl.ds(first + to, long), :] = state_ref[pl.ds(first + start, long), :]
            out_ref[pl.ds(first + at, ROWS), :] = ghost[pl.ds(k * ROWS, ROWS), :]
    middle = pl.ds(9 * TILES, 9 * TILES)
    out_ref[middle, :] = state_ref[middle, :]


def face_y_moved_kernel(state_ref, zp_ref, zm_ref, op_ref, om_ref):
    lanes = lane_index(8)
    zp, zm = zp_ref[16:24, :], zm_ref[16:24, :]
    for out, b, q in ((op_ref, 2, ROWS - 1), (om_ref, 0, 0)):
        for a in range(3):
            j = 3 * a + b
            for c in range(3):
                value = state_ref[pl.ds((9 * a + 3 * b + c) * TILES + q, 8, stride=ROWS), :]
                low = turn(zp, -j) if c == 2 else None
                high = turn(zm, LANES - 1 - j) if c == 0 else None
                out[pl.ds((3 * a + c) * 8, 8), :] = move_z(value, c, low, high, lanes)


def face_y_last_kernel(yp_ref, ym_ref, xp_ref, xm_ref, zp_ref, zm_ref, op_ref, om_ref):
    lanes = lane_index(8)
    subs = lax.broadcasted_iota(jnp.int32, (8, LANES), 0)
    zp, zm = zp_ref[16:24, :], zm_ref[16:24, :]
    for ref, out, b, q in ((yp_ref, op_ref, 2, ROWS - 1), (ym_ref, om_ref, 0, 0)):
        for a in range(3):
            j = 3 * a + b
            for c in range(3):
                place = pl.ds((3 * a + c) * 8, 8)
                value = ref[place, :]
                if a != 1:
                    ghost = xp_ref if a == 2 else xm_ref
                    spot = (3 * b + c) * ROWS + q
                    row = jnp.broadcast_to(ghost[spot : spot + 1, :], (8, LANES))
                    value = pltpu.roll(value, 1 if a == 2 else 7, 0)
                    value = jnp.where(subs == (0 if a == 2 else SLABS - 1), row, value)
                low = turn(zp, -j) if c == 2 else None
                high = turn(zm, LANES - 1 - j) if c == 0 else None
                out[place, :] = move_z(value, c, low, high, lanes)


def stream_moved_kernel(source, zp_ref, zm_ref, old_hbm, out_ref, old_ref, semaphores):
    copy = fetch(old_hbm.at[pl.ds(18 * TILES, 9 * TILES)], old_ref, semaphores.at[0])
    stream_first_kernel(source, None, None, zp_ref, zm_ref, out_ref)
    copy.wait()


def stream_first_kernel(source, xp_ref, xm_ref, zp_ref, zm_ref, out_ref):
    lanes = lane_index(ROWS)

    def step(p, carry):
        back = lax.rem(LANES - 16 * p, LANES)
        zp = turn(zp_ref[0:16, :], back)
        zm = turn(zm_ref[0:16, :], back)
        for a in range(3):
            origin = jnp.maximum(p - 1, 0) if a == 2 else jnp.minimum(p + 1, SLABS - 1)
            if a == 1 or xp_ref is None:
                origin = p
            for b in range(3):
                j = 3 * a + b
                for c in range(3):
                    i = 9 * a + 3 * b + c
                    value = source[pl.ds(pl.multiple_of(i * TILES + origin * ROWS, ROWS), ROWS), :]
                    place = pl.ds((3 * b + c) * ROWS, ROWS)
                    if a == 2 and xp_ref is not None:
                        value = jnp.where(p == 0, xp_ref[place, :], value)
                    if a == 0 and xm_ref is not None:
                        value = jnp.where(p == SLABS - 1, xm_ref[place, :], value)
                    low = turn(zp, -j) if c == 2 else None
                    high = turn(zm, LANES - 1 - j) if c == 0 else None
                    value = move_z(value, c, low, high, lanes)
                    if b != 1:
                        value = pltpu.roll(value, 1 if b == 2 else ROWS - 1, 0)
                    out_ref[pl.ds(pl.multiple_of(i * TILES + p * ROWS, ROWS), ROWS), :] = value
        return carry

    lax.fori_loop(0, SLABS, step, 0)


def fill(tiles, state_ref, first, ghost_ref=None, slab=None):
    for k in range(9):
        tiles[pl.ds(k * WIDE, TILES), :] = state_ref[pl.ds((first + k) * TILES, TILES), :]
        if ghost_ref is not None:
            tiles[pl.ds(k * WIDE + slab * ROWS, ROWS), :] = ghost_ref[pl.ds(k * ROWS, ROWS), :]


def pack(tiles, table_ref, sent, first=0, last=None):
    def step(r, carry):
        for j in range(2):
            tile = jnp.maximum(table_ref[j, r], 0)
            most = tiles[pl.ds(tile, 8, stride=WIDE), :]
            last = tiles[pl.ds(8 * WIDE + tile, 1), :]
            sent[pl.ds(r * CHUNK + j, 8, stride=2), :] = most
            sent[pl.ds(r * CHUNK + 16 + j, 1), :] = last
        return carry

    lax.fori_loop(first, PEERS if last is None else last, step, 0, unroll=4)


def pack_halves(tiles, table_ref, sent, sent_hbm, *semaphores):
    middle = PEERS // 2
    copies = []
    for (first, last), semaphore in zip(((0, middle), (middle, PEERS)), semaphores):
        pack(tiles, table_ref, sent, first, last)
        rows = pl.ds(first * CHUNK, (last - first) * CHUNK)
        copies.append(fetch(sent.at[rows], sent_hbm.at[rows], semaphore))
    return copies


def install(tiles, table_ref, received_ref):
    def step(r, carry):
        moved = []
        for j in range(2):
            tile = table_ref[j, r]
            tile = jnp.where(tile < 0, TILES, tile)
            most = received_ref[pl.ds(r * CHUNK + j, 8, stride=2), :]
            last = received_ref[pl.ds(r * CHUNK + 16 + j, 1), :]
            moved.append((tile, most, last))
        for tile, most, last in moved:
            tiles[pl.ds(tile, 8, stride=WIDE), :] = most
            tiles[pl.ds(8 * WIDE + tile, 1), :] = last
        return carry

    lax.fori_loop(0, PEERS, step, 0, unroll=4)


def move_z(value, c, low_ghost, high_ghost, lanes):
    if c == 2:
        return jnp.where(lanes == 0, low_ghost, turn(value, 1))
    if c == 0:
        return jnp.where(lanes == LANES - 1, high_ghost, turn(value, LANES - 1))
    return value


def move_y(value, b, ghost, rows):
    if b == 2:
        return jnp.where(rows == 0, ghost, pltpu.roll(value, 1, 0))
    if b == 0:
        return jnp.where(rows == ROWS - 1, ghost, pltpu.roll(value, ROWS - 1, 0))
    return value


def stream_kernel(source, yp_ref, ym_ref, zp_ref, zm_ref, out_ref):
    lanes = lane_index(ROWS)
    rows = lax.broadcasted_iota(jnp.int32, (ROWS, LANES), 0)

    def step(p, carry):
        for a in range(3):
            origin = p if a == 1 else (jnp.maximum(p - 1, 0) if a == 2 else jnp.minimum(p + 1, SLABS - 1))
            back = lax.rem(LANES - 16 * origin, LANES)
            zp = turn(zp_ref[0:16, :], back)
            zm = turn(zm_ref[0:16, :], back)
            for b in range(3):
                j = 3 * a + b
                for c in range(3):
                    i = 9 * a + 3 * b + c
                    value = source[pl.ds(pl.multiple_of(i * TILES + origin * ROWS, ROWS), ROWS), :]
                    spot = pl.ds((3 * a + c) * 8 + origin, 1)
                    ghost = yp_ref[spot, :] if b == 2 else ym_ref[spot, :]
                    value = move_y(value, b, ghost, rows)
                    low = turn(zp, -j) if c == 2 else None
                    high = turn(zm, LANES - 1 - j) if c == 0 else None
                    value = move_z(value, c, low, high, lanes)
                    out_ref[pl.ds(pl.multiple_of(i * TILES + p * ROWS, ROWS), ROWS), :] = value
        return carry

    lax.fori_loop(0, SLABS, step, 0)


def coarse_ends_kernel(state_hbm, rates_hbm, *refs):
    outs, rest_ref, tiles = refs[:3], refs[3], refs[4]
    state, rates, semaphores = refs[5:]
    pieces = [
        fetch(state_hbm.at[:, pl.ds(0, ROWS), :], state.at[:, pl.ds(0, ROWS), :], semaphores.at[0]),
        fetch(
            state_hbm.at[:, pl.ds(TILES - ROWS, ROWS), :], state.at[:, pl.ds(ROWS, ROWS), :], semaphores.at[1]
        ),
        fetch(rates_hbm, rates, semaphores.at[2]),
    ]
    others = [fetch(state_hbm.at[:, pl.ds(ROWS, TILES - 2 * ROWS), :], rest_ref, semaphores.at[3])]
    wait(pieces)

    def load(i, u):
        return state[i, pl.ds(pl.multiple_of(lax.rem(u, 4) * 8, 8), 8), :]

    collide_ends(load, None, rates, *outs)
    wait(others)
    for k in range(9):
        tiles[pl.ds(k * WIDE, ROWS), :] = state[18 + k, 0:ROWS, :]
        tiles[pl.ds(k * WIDE + ROWS, TILES - 2 * ROWS), :] = rest_ref[18 + k]
        tiles[pl.ds(k * WIDE + TILES - ROWS, ROWS), :] = state[18 + k, ROWS : 2 * ROWS, :]


def coarse_rest_kernel(state_ref, tiles, rates_hbm, table_hbm, ends_ref, *refs):
    outs, sent_hbm = refs[:5], refs[5]
    rates, table, sent, semaphores = refs[6:]
    wait([fetch(rates_hbm, rates, semaphores.at[0]), fetch(table_hbm, table, semaphores.at[1])])
    sends = pack_halves(tiles, table, sent, sent_hbm, semaphores.at[2], semaphores.at[3])

    def load(i, u):
        return state_ref[i, pl.ds(pl.multiple_of((u - 2) * 8, 8), 8), :]

    collide_rest(load, None, rates, ends_ref, *outs)
    wait(sends)


def tile8(tiles, k, u):
    return tiles[pl.ds(pl.multiple_of(k * WIDE + u * 8, 8), 8), :]


def fine_rows_kernel(upper_ref, state_hbm, flags_hbm, rates_hbm, table_hbm, received_ref, *refs):
    tiles, state, yp_ref, ym_ref, flags, rates, table, semaphores = refs
    first = fetch(table_hbm, table, semaphores.at[0])
    others = [
        fetch(flags_hbm, flags, semaphores.at[1]),
        fetch(rates_hbm, rates, semaphores.at[2]),
        fetch(state_hbm.at[pl.ds(0, 18 * TILES)], state, semaphores.at[3]),
    ]
    fill(tiles, upper_ref, 0)
    first.wait()
    install(tiles, table, received_ref)
    wait(others)
    for ref, b, q in ((yp_ref, 2, ROWS - 1), (ym_ref, 0, 0)):
        values = []
        for i in range(27):
            first = (i - 18) * WIDE if i >= 18 else i * TILES
            values.append((tiles if i >= 18 else state)[pl.ds(first + q, 8, stride=ROWS), :])
        result = relax(values, rates)
        solid = flags[pl.ds(q, 8, stride=ROWS), :] == 1
        for a in range(3):
            for c in range(3):
                i = 9 * a + 3 * b + c
                ref[pl.ds((3 * a + c) * 8, 8), :] = jnp.where(solid, values[26 - i], result[i])


def fine_all_kernel(tiles, state_ref, flags_hbm, rates_hbm, *refs):
    out_ref, zp_ref, zm_ref, xp_ref, xm_ref, flags, rates, semaphores = refs
    wait([fetch(flags_hbm, flags, semaphores.at[0]), fetch(rates_hbm, rates, semaphores.at[1])])

    def load(i, u):
        return tile8(tiles, i - 18, u) if i >= 18 else load8(state_ref, i, u)

    def step(u, carry):
        collide_at(load, flags, rates, store8(out_ref), u)
        return carry

    lax.fori_loop(0, 2 * SLABS, step, 0, unroll=2)
    pack_z(out_ref, zp_ref, zm_ref, False)
    for j in range(9):
        xp_ref[pl.ds(j * ROWS, ROWS), :] = out_ref[pl.ds((18 + j) * TILES + 7 * ROWS, ROWS), :]
        xm_ref[pl.ds(j * ROWS, ROWS), :] = out_ref[pl.ds(j * TILES, ROWS), :]


def face_z_after_y_kernel(zp_ref, zm_ref, yp_ref, ym_ref, op_ref, om_ref):
    lanes = lane_index(ROWS)
    rows = lax.broadcasted_iota(jnp.int32, (ROWS, LANES), 0)
    j_of = lax.bitwise_and(lanes, 15)
    up = jnp.logical_or(jnp.logical_or(j_of == 2, j_of == 5), j_of == 8)
    down = jnp.logical_or(jnp.logical_or(j_of == 0, j_of == 3), j_of == 6)
    small = lane_index(8)
    slab = lax.broadcasted_iota(jnp.int32, (8, LANES), 0) * 16
    for ref, out, c, edge in ((zp_ref, op_ref, 2, LANES - 1), (zm_ref, om_ref, 0, 0)):
        packed = ref[0:16, :]
        value = jnp.where(up, pltpu.roll(packed, 1, 0), packed)
        value = jnp.where(down, pltpu.roll(packed, ROWS - 1, 0), value)
        for ghost, b, q, lane_set in ((yp_ref, 2, 0, up), (ym_ref, 0, ROWS - 1, down)):
            spread = jnp.zeros((8, LANES), jnp.float32)
            for a in range(3):
                j = 3 * a + b
                column = ghost[pl.ds((3 * a + c) * 8, 8), :]
                column = pltpu.roll(column, (j - edge) % LANES, 1, stride=16, stride_axis=0)
                spread = jnp.where(small == slab + j, column, spread)
            row = jnp.sum(spread, axis=0, keepdims=True)
            here = jnp.logical_and(lane_set, rows == q)
            value = jnp.where(here, jnp.broadcast_to(row, (ROWS, LANES)), value)
        out[0:16, :] = value
        out[16:24, :] = jnp.zeros((8, LANES), jnp.float32)


def face_x_after_z_kernel(xp_ref, xm_ref, yp_ref, ym_ref, zp_ref, zm_ref, op_ref, om_ref):
    lanes = lane_index(ROWS)
    rows = lax.broadcasted_iota(jnp.int32, (ROWS, LANES), 0)
    zp, zm = zp_ref[0:16, :], zm_ref[0:16, :]
    for ref, out, a, p in ((xp_ref, op_ref, 2, SLABS - 1), (xm_ref, om_ref, 0, 0)):
        for b in range(3):
            j = 3 * a + b
            for c in range(3):
                place = pl.ds((3 * b + c) * ROWS, ROWS)
                spot = pl.ds((3 * a + c) * 8 + p, 1)
                ghost = yp_ref[spot, :] if b == 2 else ym_ref[spot, :]
                value = move_y(ref[place, :], b, ghost, rows)
                low = turn(zp, -(16 * p + j)) if c == 2 else None
                high = turn(zm, LANES - 1 - 16 * p - j) if c == 0 else None
                out[place, :] = move_z(value, c, low, high, lanes)


def fine_ends_kernel(state_ref, xp_ref, xm_ref, received_ref, flags_hbm, rates_hbm, table_hbm, *refs):
    tiles, outs = refs[0], refs[1:4]
    flags, rates, table, semaphores = refs[4:]
    first = fetch(table_hbm, table, semaphores.at[0])
    others = [fetch(flags_hbm, flags, semaphores.at[1]), fetch(rates_hbm, rates, semaphores.at[2])]
    fill(tiles, state_ref, 18, xp_ref, 0)
    first.wait()
    install(tiles, table, received_ref)
    wait(others)

    def load(i, u):
        if i >= 18:
            return tile8(tiles, i - 18, u)
        value = load8(state_ref, i, u)
        if i < 9:
            ghost = xm_ref[pl.ds(pl.multiple_of(i * ROWS + lax.rem(u, 2) * 8, 8), 8), :]
            value = jnp.where(u >= 2 * SLABS - 2, ghost, value)
        return value

    collide_ends(load, flags, rates, *outs)


def fine_rest_kernel(state_ref, tiles_ref, flags_hbm, rates_hbm, ends_ref, *refs):
    outs = refs[:5]
    flags, rates, semaphores = refs[5:]
    wait([fetch(flags_hbm, flags, semaphores.at[0]), fetch(rates_hbm, rates, semaphores.at[1])])

    def load(i, u):
        return tile8(tiles_ref, i - 18, u) if i >= 18 else load8(state_ref, i, u)

    collide_rest(load, flags, rates, ends_ref, *outs)


def finish(state_ref, yp_ref, ym_ref, whole):
    whole[...] = state_ref[...]
    for i in range(27):
        a, b, c = i // 9, (i // 3) % 3, i % 3
        if b != 1:
            ghost, q = (yp_ref, 0) if b == 2 else (ym_ref, ROWS - 1)
            whole[pl.ds(i * TILES + q, 8, stride=ROWS), :] = ghost[pl.ds((3 * a + c) * 8, 8), :]


def mean_kernel(state_ref, yp_ref, ym_ref, old_ref, table_hbm, fine_hbm, sent_hbm, whole, *scratch):
    upper_ref, table, tiles, sent, semaphores = scratch
    first = fetch(table_hbm, table, semaphores.at[0])
    ahead = [fetch(fine_hbm.at[pl.ds(18 * TILES, 9 * TILES)], upper_ref, semaphores.at[3])]
    finish(state_ref, yp_ref, ym_ref, whole)
    for k in range(9):
        new = whole[pl.ds((18 + k) * TILES, TILES), :]
        tiles[pl.ds(k * WIDE, TILES), :] = 0.5 * (old_ref[pl.ds(k * TILES, TILES), :] + new)
    first.wait()
    wait(pack_halves(tiles, table, sent, sent_hbm, semaphores.at[1], semaphores.at[2]) + ahead)


def write_kernel(state_ref, kept_ref, out_hbm, semaphores):
    copy = fetch(state_ref, out_hbm, semaphores.at[0])
    kept_ref[...] = state_ref[pl.ds(0, 9 * TILES), :]
    copy.wait()


def up_kernel(state_ref, yp_ref, ym_ref, table_hbm, sent_ref, out_hbm, *scratch):
    whole, table, tiles, semaphores = scratch
    first = fetch(table_hbm, table, semaphores.at[0])
    finish(state_ref, yp_ref, ym_ref, whole)
    copy = fetch(whole, out_hbm, semaphores.at[1])
    fill(tiles, whole, 0)
    first.wait()
    pack(tiles, table, sent_ref)
    copy.wait()


def coarse_install_kernel(whole_hbm, kept_ref, received_ref, table_hbm, out_hbm, *scratch):
    table, tiles, semaphores, stores = scratch
    first = fetch(table_hbm, table, semaphores.at[0])
    for k in range(9):
        tiles[pl.ds(k * WIDE, TILES), :] = kept_ref[pl.ds(k * TILES, TILES), :]
    first.wait()
    install(tiles, table, received_ref)
    wait(
        [
            fetch(tiles.at[pl.ds(k * WIDE, TILES)], out_hbm.at[pl.ds(k * TILES, TILES)], stores.at[k])
            for k in range(9)
        ]
    )


STATE = (27 * TILES, LANES)
MESSAGE = (PEERS * CHUNK, LANES)
Z_FACE = (24, LANES)
Y_FACE = (9 * 8, LANES)
X_FACE = (9 * ROWS, LANES)
WIDE_TILES = (9 * WIDE, LANES)
NINE = (9 * TILES, LANES)
ENDS = (27 * 2 * ROWS, LANES)
REST = (STATE, Z_FACE, Z_FACE, Y_FACE, Y_FACE)


def floats(*shape):
    return pltpu.VMEM(shape, jnp.float32)


def copies(count):
    return pltpu.SemaphoreType.DMA((count,))


FLAGS = pltpu.VMEM((TILES, LANES), jnp.int32)
RATES = pltpu.SMEM((27,), jnp.float32)
TABLE = pltpu.SMEM((2, PEERS), jnp.int32)


def run(kernel, name, spaces, shapes, *operands, scratch=(), alias=False, microseconds=1.0):
    spots = {"v": pltpu.VMEM, "h": pltpu.HBM}
    given, made = spaces.split(":")
    operands = [
        pltpu.with_memory_space_constraint(operand, pltpu.HBM) if space == "h" else operand
        for operand, space in zip(operands, given)
    ]
    return pl.pallas_call(
        kernel,
        name=name,
        out_shape=tuple(jax.ShapeDtypeStruct(shape, jnp.float32) for shape in shapes),
        in_specs=[pl.BlockSpec(memory_space=spots[space]) for space in given],
        out_specs=tuple(pl.BlockSpec(memory_space=spots[space]) for space in made),
        scratch_shapes=list(scratch),
        input_output_aliases={0: 0} if alias else {},
        compiler_params=pltpu.CompilerParams(vmem_limit_bytes=VMEM_BYTES),
        cost_estimate=pl.CostEstimate(
            flops=0, bytes_accessed=int(microseconds * 3.0e6), transcendentals=0
        ),
    )(*operands)


def swap(axis, plus, minus):
    count = lax.axis_size(axis)
    up = [(i, (i + 1) % count) for i in range(count)]
    down = [(i, (i - 1) % count) for i in range(count)]
    return lax.ppermute(plus, axis, up), lax.ppermute(minus, axis, down)


def halo_y_first(yp, ym, rest, beside):
    yp, ym = swap("gy", yp, ym)
    collided, zp, zm, xp, xm = rest()
    zp, zm = run(face_z_after_y_kernel, "face_z", "vvvv:vv", (Z_FACE, Z_FACE), zp, zm, yp, ym)
    zp, zm, xp = beside(zp, zm, xp)
    zp, zm = swap("gz", zp, zm)
    xp, xm = run(face_x_after_z_kernel, "face_x", "vvvvvv:vv", (X_FACE, X_FACE), xp, xm, yp, ym, zp, zm)
    xp, xm = swap("gx", xp, xm)
    (moved,) = run(
        stream_kernel, "stream", "vvvvv:v", (STATE,), collided, yp, ym, zp, zm, microseconds=2.0
    )
    return moved, xp, xm


def halo_x_first(xp, xm, rest):
    xp, xm = swap("gx", xp, xm)
    collided, zp, zm, yp, ym = rest()
    zp, zm = run(face_z_kernel, "face_z", "vvvv:vv", (Z_FACE, Z_FACE), zp, zm, xp, xm)
    zp, zm = swap("gz", zp, zm)
    yp, ym = run(face_y_last_kernel, "face_y", "vvvvvv:vv", (Y_FACE, Y_FACE), yp, ym, xp, xm, zp, zm)
    return yp, ym, (collided, xp, xm, zp, zm)


def halo_moved(old, xp, xm, rest, between):
    xp, xm = swap("gx", xp, xm)
    collided, zp, zm, _, _ = rest()
    zp, zm, moved = run(
        move_x_kernel, "move_x", "vvvvv:vvv", (Z_FACE, Z_FACE, STATE), collided, zp, zm, xp, xm
    )
    zp, zm = between(zp, zm)
    zp, zm = swap("gz", zp, zm)
    yp, ym = run(face_y_moved_kernel, "face_y", "vvv:vv", (Y_FACE, Y_FACE), moved, zp, zm)
    yp, ym = swap("gy", yp, ym)
    state, old = run(
        stream_moved_kernel, "stream", "vvvh:vv", (STATE, NINE), moved, zp, zm, old,
        scratch=(copies(1),),
        microseconds=2.0,
    )
    return state, old, yp, ym


def stream_first(operands):
    return run(stream_first_kernel, "stream", "vvvvv:v", (STATE,), *operands, microseconds=2.0)[0]


def routed(message):
    chunks = message.reshape(PEERS, 9, 2, LANES)
    received = lax.all_to_all(chunks, ("gx", "gz"), split_axis=0, concat_axis=0, tiled=True)
    return received.reshape(MESSAGE)


def body(fine, coarse, fine_rates, coarse_rates, flags, down_source, down_target, up_source, up_target):
    fine = fine.reshape(STATE)
    coarse = coarse.reshape(STATE)
    flags = flags.reshape(TILES, LANES)
    down_source, down_target, up_source, up_target = (
        table.reshape(-1, 2).T for table in (down_source, down_target, up_source, up_target)
    )
    cube = coarse.reshape(27, TILES, LANES)
    ends, xp, xm, others, tiles = run(
        coarse_ends_kernel, "coarse_ends", "hh:vvvvv",
        (ENDS, X_FACE, X_FACE, (27, TILES - 2 * ROWS, LANES), WIDE_TILES), cube, coarse_rates,
        scratch=(floats(27, 2 * ROWS, LANES), RATES, copies(4)),
        microseconds=2.0,
    )

    packed = []

    def coarse_rest():
        *parts, sent_old = run(
            coarse_rest_kernel, "coarse_rest", "vvhhv:vvvvvh", REST + (MESSAGE,),
            others, tiles, coarse_rates, down_source, ends,
            scratch=(RATES, TABLE, floats(*MESSAGE), copies(4)),
            microseconds=4.0,
        )
        packed.append(sent_old)
        return parts

    arrived = []

    def send_old(zp, zm):
        sent, zp, zm = lax.optimization_barrier((packed[0], zp, zm))
        arrived.append(routed(sent))
        return zp, zm

    moved, old, yp, ym = halo_moved(coarse, xp, xm, coarse_rest, send_old)
    (received,) = arrived
    sent_mean, coarse_moved, upper = run(
        mean_kernel, "pack_mean", "vvvvhh:hvv", (MESSAGE, STATE, NINE),
        moved, yp, ym, old, down_source, fine,
        scratch=(TABLE, floats(*WIDE_TILES), floats(*MESSAGE), copies(5)),
        microseconds=2.0,
    )
    mean = routed(sent_mean)
    tiles, others, yp, ym = run(
        fine_rows_kernel, "fine_rows", "vhhhhv:vvvv", (WIDE_TILES, (18 * TILES, LANES), Y_FACE, Y_FACE),
        upper, fine, flags, fine_rates, down_target, received,
        scratch=(FLAGS, RATES, TABLE, copies(4)),
        microseconds=2.0,
    )

    def fine_all():
        return run(
            fine_all_kernel, "fine_all", "vvhh:vvvvv", (STATE, Z_FACE, Z_FACE, X_FACE, X_FACE),
            tiles, others, flags, fine_rates,
            scratch=(FLAGS, RATES, copies(2)),
            microseconds=3.0,
        )

    written = []

    def write_coarse(zp, zm, xp):
        state, zp, zm = lax.optimization_barrier((coarse_moved, zp, zm))
        kept, coarse_new = run(
            write_kernel, "coarse_write", "v:vh", (NINE, STATE), state, scratch=(copies(1),), microseconds=1.0
        )
        kept, coarse_new, xp = lax.optimization_barrier((kept, coarse_new, xp))
        written.extend((kept, coarse_new))
        return zp, zm, xp

    moved, xp, xm = halo_y_first(yp, ym, fine_all, write_coarse)
    kept, coarse_new = written
    tiles, ends, face_xp, face_xm = run(
        fine_ends_kernel, "fine_ends", "vvvvhhh:vvvv", (WIDE_TILES, ENDS, X_FACE, X_FACE),
        moved, xp, xm, mean, flags, fine_rates, down_target,
        scratch=(FLAGS, RATES, TABLE, copies(3)),
        microseconds=3.0,
    )

    def fine_rest():
        return run(
            fine_rest_kernel, "fine_rest", "vvhhv:vvvvv", REST, moved, tiles, flags, fine_rates, ends,
            scratch=(FLAGS, RATES, copies(2)),
            microseconds=3.0,
        )

    yp, ym, whole = halo_x_first(face_xp, face_xm, fine_rest)
    yp, ym = swap("gy", yp, ym)
    sent_up, fine_next = run(
        up_kernel, "pack_up", "vvvh:vh", (MESSAGE, STATE), stream_first(whole), yp, ym, up_source,
        scratch=(floats(*STATE), TABLE, floats(*WIDE_TILES), copies(2)),
        microseconds=2.0,
    )
    up = routed(sent_up)
    (coarse_next,) = run(
        coarse_install_kernel, "coarse_install", "hvvh:h", (STATE,), coarse_new, kept, up, up_target,
        scratch=(TABLE, floats(*WIDE_TILES), copies(1), copies(9)),
        alias=True,
        microseconds=2.0,
    )
    block = (27, SLABS, ROWS, LANES)
    return fine_next.reshape(block), coarse_next.reshape(block)


def solution(mesh):
    placed = (
        P(None, "gx", "gy", "gz"),
        P(None, "gx", "gy", "gz"),
        P(),
        P(),
        P("gx", "gy", "gz"),
        P("gx", "gy", "gz", None, None),
        P("gx", "gy", "gz", None, None),
        P("gx", "gy", "gz", None, None),
        P("gx", "gy", "gz", None, None),
    )
    return jax.shard_map(
        body,
        mesh=mesh,
        in_specs=placed,
        out_specs=(P(None, "gx", "gy", "gz"), P(None, "gx", "gy", "gz")),
        check_vma=False,
    )
```
